32 devices in a mesh: groups: 2 (over y), ctx: 2 (over x), heads: 8 (over z, core).
Axes of the slice: x: 2, y: 2, z: 4, core: 2. Of those that a mesh axis runs over, the one named last changes fastest.
Arguments:
- hidden_in: bfloat16 [4096, 4096], P(('groups', 'ctx'), 'heads'), parts along dimension 0, may hold values from -6 to 6
- norm_gain: float32 [4096], replicated, may hold values from 0.1 to 1.9
- router_weight: float32 [4096], replicated, may hold values from -0.09375 to 0.09375
- w_query: bfloat16 [4096, 4096], P(None, 'heads')
- w_key: bfloat16 [4096, 1024], P(None, 'heads')
- value_weight: bfloat16 [4096, 1024], P(None, 'heads'), may hold values from -0.09375 to 0.09375
- w_out: bfloat16 [4096, 4096], P(None, 'heads'), may hold values from -1.5 to 1.5
- keep_flags: int32 [4096], P(('groups', 'ctx')), parts along dimension 0, may hold values from 0 to 1, as said below
- keep_counts: int32 [4], P('groups'), parts along dimension 0, may hold values from 1 to 256, as said below
- keep_positions: int32 [4, 256], P('groups'), parts along dimension 0, may hold values from -1 to 2047, as said below
Outputs:
- hidden_out: bfloat16 [4096, 4096], P(('groups', 'ctx'), 'heads'), parts along dimension 0
The draws below stay inside these ranges and needn't reach their ends.
There are 2 independent parts, one for each index of `groups`. The reference program is written for one: setup_inputs(seed, part) draws one part's arguments, and reference() takes and returns one part's arrays. A program takes and returns all parts, laid end to end along the dimension named above; an argument that names none is the same for every part. Nothing has to cross between parts.
Inputs may be any that keep to these rules, and one draw needn't show every extreme that they name: keep_flags is 1 exactly at the positions listed by keep_positions and keep_counts. `keep_counts`: some shard's count is 256. `keep_positions`: row s lists, ascending, keep_counts[s] positions of shard s's tokens, then -1 in the remaining slots.
All inputs are finite; a program needn't handle non-finite values.
Results may differ from the reference program's by a relative error of at most 0.0085.
Values may be sent and summed in bfloat16 or wider, within the bound.
No kernel may reach another device: no remote copies, remote signals or barrier semaphores. Data moves between devices by JAX's collectives and lax.ppermute only.
A program may use at most 128 MiB of HBM per device.

```python
import jax
import jax.numpy as jnp
from jax import lax

MODEL_WIDTH = 4096
QUERY_HEAD_COUNT = 32
KEY_VALUE_HEADS = 8
HEAD_SIZE = 128
TOK_DEV = 1024
CAP = 256
TOKENS = 2048
SLOTS = 512
N_CTX = 2


def keep_lists(key):
    count_key, top_key, rank_key = jax.random.split(key, 3)
    counts = jax.random.randint(count_key, (N_CTX,), 1, CAP + 1).astype(jnp.int32)
    fullest = jax.random.randint(top_key, (), 0, N_CTX)
    counts = counts.at[fullest].set(CAP)
    local_ids = jnp.arange(TOK_DEV, dtype=jnp.int32)
    scores = jax.random.randint(rank_key, (N_CTX, TOK_DEV), 0, 2 ** 16) * TOK_DEV + local_ids[None, :]
    ranking = jnp.argsort(jnp.argsort(scores, axis=1), axis=1)
    kept = ranking < counts[:, None]
    order_ids = jnp.argsort(jnp.where(kept, local_ids[None, :], TOK_DEV + local_ids[None, :]), axis=1)[:, :CAP]
    starts = jnp.arange(N_CTX, dtype=jnp.int32)[:, None] * TOK_DEV
    slot_ids = jnp.arange(CAP, dtype=jnp.int32)[None, :]
    positions = jnp.where(slot_ids < counts[:, None], order_ids + starts, -1)
    return (kept.reshape(-1).astype(jnp.int32), counts, positions.astype(jnp.int32))


def key_base(key):
    return jax.random.normal(key, (MODEL_WIDTH, KEY_VALUE_HEADS * HEAD_SIZE), jnp.float32) * MODEL_WIDTH ** (-0.5)


def draw_keep_flags(key, part):
    return keep_lists(key)[0]


def draw_keep_counts(key, part):
    return keep_lists(key)[1]


def draw_keep_positions(key, part):
    return keep_lists(key)[2]


def draw_w_key(key, part):
    return key_base(key).astype(jnp.bfloat16)


def draw_w_query(key, part):
    key = jax.random.fold_in(key, 7)
    noise = jax.random.normal(key, (MODEL_WIDTH, QUERY_HEAD_COUNT * HEAD_SIZE), jnp.float32) * MODEL_WIDTH ** (-0.5)
    return noise.astype(jnp.bfloat16)


def block_levels(key, shape, shards, least, high):
    level = 1.0
    for axis_at, shards_of in shards:
        draws = jax.random.uniform(jax.random.fold_in(jax.random.fold_in(key, 6), axis_at), (shards_of,), jnp.float32, least / len(shards), high / len(shards))
        level = level * jnp.repeat(jnp.exp(draws), shape[axis_at] // shards_of).reshape((-1,) + (1,) * (len(shape) - 1 - axis_at))
    return level


def scatter_about(key, dims, scale, reach, pieces=(), held_as=jnp.bfloat16):
    entries = scale * jax.random.normal(key, dims, jnp.float32)
    if pieces:
        entries = entries * block_levels(key, dims, pieces, -0.22, 0.18)
    return jnp.clip(entries, -reach, reach).astype(held_as)


def setup_inputs(seed: int = 0, part: int = 0) -> dict:
    arg_keys = jax.random.split(jax.random.key(seed), 11)
    part_keys = jax.random.split(jax.random.fold_in(arg_keys[10], part), 11)
    hidden_in = scatter_about(part_keys[0], (TOKENS, MODEL_WIDTH), 1.0, 6.0, ((0, 2), (1, 8)))
    norm_gain = jnp.clip(1.0 + 0.18 * jax.random.normal(arg_keys[1], (MODEL_WIDTH,), jnp.float32), 0.1, 1.9)
    router_weight = scatter_about(arg_keys[2], (MODEL_WIDTH,), MODEL_WIDTH ** -0.5, 0.09375, (), jnp.float32)
    w_query = draw_w_query(jax.random.fold_in(arg_keys[10], 71), part)
    w_key = draw_w_key(jax.random.fold_in(arg_keys[10], 71), part)
    value_weight = scatter_about(arg_keys[5], (MODEL_WIDTH, KEY_VALUE_HEADS * HEAD_SIZE), MODEL_WIDTH ** -0.5, 0.09375, ((1, 8),))
    w_out = scatter_about(arg_keys[6], (QUERY_HEAD_COUNT * HEAD_SIZE, MODEL_WIDTH), 16 ** -0.5, 1.5, ((1, 8),))
    keep_flags = draw_keep_flags(jax.random.fold_in(jax.random.fold_in(arg_keys[10], part), 71), part)
    keep_counts = draw_keep_counts(jax.random.fold_in(jax.random.fold_in(arg_keys[10], part), 71), part)
    keep_positions = draw_keep_positions(jax.random.fold_in(jax.random.fold_in(arg_keys[10], part), 71), part)
    return {"hidden_in": hidden_in, "norm_gain": norm_gain, "router_weight": router_weight, "w_query": w_query, "w_key": w_key, "value_weight": value_weight, "w_out": w_out, "keep_flags": keep_flags, "keep_counts": keep_counts, "keep_positions": keep_positions}


rope_base = 500000.0
norm_eps = 1e-05

def rotate(tensor, positions_in):
    row_count = tensor.shape[0]
    head_count = tensor.shape[1] // HEAD_SIZE
    tensor = tensor.reshape(row_count, head_count, HEAD_SIZE)
    half_dim = HEAD_SIZE // 2
    frequency = rope_base ** (-(jnp.arange(half_dim, dtype=jnp.float32) * 2.0 / HEAD_SIZE))
    angles = positions_in.astype(jnp.float32)[:, None] * frequency[None, :]
    cosine = jnp.cos(angles)[:, None, :]
    sine_part = jnp.sin(angles)[:, None, :]
    first_half = tensor[..., :half_dim]
    second_half = tensor[..., half_dim:]
    turned = jnp.concatenate([first_half * cosine - second_half * sine_part, second_half * cosine + first_half * sine_part], -1)
    return turned.reshape(row_count, head_count * HEAD_SIZE)

def reference(hidden_in, norm_gain, router_weight, w_query, w_key, value_weight, w_out, keep_flags, keep_counts, keep_positions):
    slot_ids = jnp.arange(CAP, dtype=jnp.int32)
    is_valid = (slot_ids[None, :] < keep_counts[:, None]).reshape(-1)
    flat_pos = keep_positions.reshape(-1).astype(jnp.int32)
    fetch_idx = jnp.where(is_valid, flat_pos, 0).astype(jnp.int32)
    kept_pos = jnp.where(is_valid, flat_pos, TOKENS).astype(jnp.int32)
    key_pos = jnp.where(is_valid, flat_pos, TOKENS + 1).astype(jnp.int32)
    wide_float = hidden_in[fetch_idx].astype(jnp.float32)
    inv_rms = lax.rsqrt(lax.optimization_barrier(jnp.mean(wide_float * wide_float, axis=-1, keepdims=True)) + norm_eps)
    normed = (wide_float * inv_rms * norm_gain[None, :]).astype(jnp.bfloat16)
    gate_value = jax.nn.sigmoid(lax.optimization_barrier(jnp.sum(wide_float * router_weight[None, :], axis=-1)))
    query_rows = rotate(jnp.dot(normed, w_query, preferred_element_type=jnp.float32), kept_pos).astype(jnp.bfloat16)
    key_row_block = rotate(jnp.dot(normed, w_key, preferred_element_type=jnp.float32), kept_pos).astype(jnp.bfloat16)
    value_row_block = jnp.dot(normed, value_weight, preferred_element_type=jnp.float32).astype(jnp.bfloat16)
    group_width = QUERY_HEAD_COUNT // KEY_VALUE_HEADS
    query_single = query_rows.astype(jnp.float32).reshape(SLOTS, KEY_VALUE_HEADS, group_width, HEAD_SIZE).transpose(1, 0, 2, 3)
    key_single = key_row_block.astype(jnp.float32).reshape(SLOTS, KEY_VALUE_HEADS, HEAD_SIZE).transpose(1, 0, 2)
    value_single = value_row_block.astype(jnp.float32).reshape(SLOTS, KEY_VALUE_HEADS, HEAD_SIZE).transpose(1, 0, 2)
    visible = key_pos[None, :] <= kept_pos[:, None]
    score_scale = 1.0 / HEAD_SIZE ** 0.5

    def per_head(head_args):
        query_head, key_head, value_head = head_args
        scores = jnp.einsum('qgd,nd->gqn', query_head, key_head) * score_scale
        masked = jnp.where(visible[None], scores, -1e+30)
        top_score = lax.optimization_barrier(jnp.max(masked, axis=-1, keepdims=True))
        weights_raw = jnp.where(visible[None], jnp.exp(scores - top_score), 0.0)
        denom_sum = lax.optimization_barrier(jnp.sum(weights_raw, axis=-1))
        weights_low = weights_raw.astype(jnp.bfloat16).astype(jnp.float32)
        mixed = jnp.einsum('gqn,nd->qgd', weights_low, value_head)
        return mixed / denom_sum.T[:, :, None]
    attended = lax.map(per_head, (query_single, key_single, value_single))
    attn = attended.transpose(1, 0, 2, 3).reshape(SLOTS, QUERY_HEAD_COUNT * HEAD_SIZE).astype(jnp.bfloat16)
    projected = jnp.dot(attn, w_out, preferred_element_type=jnp.float32)
    update = (gate_value[:, None] * projected).astype(jnp.bfloat16)
    widened = jnp.zeros((TOKENS, MODEL_WIDTH), jnp.float32).at[kept_pos].set(update.astype(jnp.float32), mode='drop')
    flag_float = keep_flags.astype(jnp.float32)[:, None]
    return (hidden_in.astype(jnp.float32) + flag_float * widened).astype(jnp.bfloat16)
```

```python
import functools

import jax
import jax.numpy as jnp
from jax import lax
from jax.experimental import pallas as pl
from jax.experimental.pallas import tpu as pltpu
from jax.sharding import PartitionSpec as P

HEAD_SIZE = 128
ROPE_BASE = 500000.0
NORM_EPS = 1e-05
LOG2E = 1.4426950408889634
VMEM_LIMIT = 24 * 1024 * 1024
F32 = jnp.float32
BF16 = jnp.bfloat16


def whole():
    return pl.BlockSpec(memory_space=pltpu.VMEM)


def fixed(shape):
    return pl.BlockSpec(shape, lambda *_: (0,) * len(shape))


def params():
    return pltpu.CompilerParams(vmem_limit_bytes=VMEM_LIMIT)


def live_row(pos_ref, cnt_ref, shard, dead):
    pos = pos_ref[pl.ds(shard, 1), :]
    slot = lax.broadcasted_iota(jnp.int32, pos.shape, 1)
    return jnp.where(slot < cnt_ref[shard], pos, dead)


def pick_kernel(cnt_ref, pos_ref, hid_ref, x_ref, xa_ref, xb_ref, rowpos_ref):
    own = lax.axis_index("ctx")
    shards = lax.axis_size("ctx")
    tok = hid_ref.shape[0]
    cap = x_ref.shape[0]
    row = live_row(pos_ref, cnt_ref, own, shards * tok)
    column = jnp.transpose(jnp.broadcast_to(row, (128, cap)))
    rowpos_ref[...] = column
    local = column[:, :1] - own * tok
    hot = (lax.broadcasted_iota(jnp.int32, (cap, tok), 1) == local).astype(F32).astype(BF16)
    x = jnp.dot(hot, hid_ref[...], preferred_element_type=F32).astype(BF16)
    x_ref[...] = x
    xa_ref[...] = x[: cap // 2]
    xb_ref[...] = x[cap // 2 :]


def pick(counts, positions, hidden):
    cap, width = positions.shape[1], hidden.shape[1]
    return pl.pallas_call(
        pick_kernel,
        out_shape=[
            jax.ShapeDtypeStruct((cap, width), BF16),
            jax.ShapeDtypeStruct((cap // 2, width), BF16),
            jax.ShapeDtypeStruct((cap // 2, width), BF16),
            jax.ShapeDtypeStruct((cap, 128), jnp.int32),
        ],
        in_specs=[pl.BlockSpec(memory_space=pltpu.SMEM), whole(), whole()],
        out_specs=[whole()] * 4,
        compiler_params=params(),
        name="pick",
    )(counts, positions, hidden)


def heads_perm(size, f):
    return [(2 * z + c, 2 * f(z) + c) for z in range(size // 2) for c in range(2)]


def spread(size, full, first, second):
    cross = functools.partial(lax.ppermute, axis_name="heads", perm=heads_perm(size, lambda z: 3 - z))
    near = functools.partial(lax.ppermute, axis_name="heads", perm=heads_perm(size, lambda z: z ^ 1))
    twin = functools.partial(
        lax.ppermute, axis_name="heads", perm=[(d, d ^ 1) for d in range(size)]
    )
    far_a, far_b = cross(first), cross(second)
    mate = twin(full)
    beside = near(full)
    far_mate_a, far_mate_b = twin(far_a), twin(far_b)
    beside_mate = twin(beside)
    last_a, last_b = near(far_a), near(far_b)
    last_mate_a, last_mate_b = twin(last_a), twin(last_b)
    return (
        ((full,), (mate,)),
        ((far_a, far_b), (far_mate_a, far_mate_b)),
        ((beside,), (beside_mate,)),
        ((last_a, last_b), (last_mate_a, last_mate_b)),
    )


def joined(refs):
    parts = [ref[...] for ref in refs]
    return parts[0] if len(parts) == 1 else jnp.concatenate(parts, axis=0)


def lanes_sum(x):
    total = x[:, :128]
    for at in range(128, x.shape[1], 128):
        total = total + x[:, at : at + 128]
    return total


def kv_terms(mine, twin, gain_ref, router_ref, wk_ref, wv_ref):
    core = lax.rem(lax.axis_index("heads"), 2)
    width = mine.shape[1]
    sums = None
    scaled = []
    for x, at in ((mine, core), (twin, 1 - core)):
        xf = x.astype(F32)
        rows = pl.ds(pl.multiple_of(at * width, width), width)
        gained = (xf * gain_ref[:, rows]).astype(BF16)
        scaled.append(gained)
        part = (
            jnp.dot(gained, wk_ref[rows, :], preferred_element_type=F32),
            jnp.dot(gained, wv_ref[rows, :], preferred_element_type=F32),
            lanes_sum(xf * xf),
            lanes_sum(xf * router_ref[:, rows]),
        )
        sums = part if sums is None else tuple(a + b for a, b in zip(sums, part))
    return scaled, sums


def q_term(scaled, wq_ref):
    core = lax.rem(lax.axis_index("heads"), 2)
    width = scaled[0].shape[1]
    out = None
    for gained, at in zip(scaled, (core, 1 - core)):
        rows = pl.ds(pl.multiple_of(at * width, width), width)
        part = jnp.dot(gained, wq_ref[rows, :], preferred_element_type=F32)
        out = part if out is None else out + part
    return out


def turn(x, cos, sin):
    return x * cos + pltpu.roll(x, HEAD_SIZE // 2, 1) * sin


def qkv_kernel(n_mine, fresh, chip_ref, *refs):
    mine, twin = joined(refs[:n_mine]), joined(refs[n_mine : 2 * n_mine])
    refs = refs[2 * n_mine :]
    gain_ref, router_ref, wq_ref, wk_ref, wv_ref = refs[:5]
    kv_out, q_out = refs[-2:]
    scaled, (k, v, squares, routed) = kv_terms(mine, twin, gain_ref, router_ref, wk_ref, wv_ref)
    q = q_term(scaled, wq_ref)
    if fresh:
        kv_out[:, 0:128], kv_out[:, 128:256] = k, v
        kv_out[:, 256:384], kv_out[:, 384:512] = squares, routed
        q_out[...] = q
    else:
        kv_in, q_in = refs[5:7]
        kv_out[:, 0:128] = kv_in[:, 0:128] + k
        kv_out[:, 128:256] = kv_in[:, 128:256] + v
        kv_out[:, 256:384] = kv_in[:, 256:384] + squares
        kv_out[:, 384:512] = kv_in[:, 384:512] + routed
        q_out[...] = q_in[...] + q


def weight_spec(rows, columns):
    return pl.BlockSpec((rows, columns), lambda i, chip: (chip[0], 0))


def vector_spec(columns):
    return pl.BlockSpec((1, columns), lambda i, chip: (0, chip[0]))


def qkv_part(chip, pair, gain, router, wq, wk, wv, sums):
    mine, twin = pair
    cap = sum(x.shape[0] for x in mine)
    width = mine[0].shape[1]
    operands = [*mine, *twin, gain, router, wq, wk, wv]
    specs = [fixed(x.shape) for x in (*mine, *twin)]
    specs += [vector_spec(2 * width)] * 2
    specs += [weight_spec(2 * width, w.shape[1]) for w in (wq, wk, wv)]
    aliases = {}
    if sums is not None:
        aliases = {1 + len(operands): 0, 2 + len(operands): 1}
        operands += sums
        specs += [fixed(s.shape) for s in sums]
    return pl.pallas_call(
        functools.partial(qkv_kernel, len(mine), sums is None),
        out_shape=[
            jax.ShapeDtypeStruct((cap, 512), F32),
            jax.ShapeDtypeStruct((cap, wq.shape[1]), F32),
        ],
        grid_spec=pltpu.PrefetchScalarGridSpec(
            num_scalar_prefetch=1,
            grid=(1,),
            in_specs=specs,
            out_specs=[fixed((cap, 512)), fixed((cap, wq.shape[1]))],
        ),
        input_output_aliases=aliases,
        compiler_params=params(),
        cost_estimate=pl.CostEstimate(
            flops=2 * cap * 2 * width * 768, bytes_accessed=4 * 1024 * 1024, transcendentals=0
        ),
        name="qkv_part",
    )(chip, *operands)


def kv_last_kernel(n_mine, features, chip_ref, *refs):
    mine, twin = joined(refs[:n_mine]), joined(refs[n_mine : 2 * n_mine])
    gain_ref, router_ref, wk_ref, wv_ref, kv_in, cos_ref, sin_ref, kv_out, stat_out = refs[2 * n_mine :]
    _, (k, v, squares, routed) = kv_terms(mine, twin, gain_ref, router_ref, wk_ref, wv_ref)
    squares = jnp.sum(kv_in[:, 256:384] + squares, axis=1, keepdims=True)
    routed = jnp.sum(kv_in[:, 384:512] + routed, axis=1, keepdims=True)
    inverse = lax.rsqrt(squares * (1.0 / features) + NORM_EPS)
    k = (kv_in[:, 0:128] + k) * inverse
    kv_out[:, 0:128] = turn(k, cos_ref[...], sin_ref[...]).astype(BF16)
    kv_out[:, 128:256] = ((kv_in[:, 128:256] + v) * inverse).astype(BF16)
    stat_out[:, 0:128] = jnp.broadcast_to(inverse, (inverse.shape[0], 128))
    gate = 1.0 / (1.0 + jnp.exp(-routed))
    stat_out[:, 128:256] = jnp.broadcast_to(gate, (gate.shape[0], 128))


def kv_last(chip, pair, gain, router, wk, wv, kv_sum, cos, sin):
    mine, twin = pair
    cap = sum(x.shape[0] for x in mine)
    width = mine[0].shape[1]
    specs = [fixed(x.shape) for x in (*mine, *twin)]
    specs += [vector_spec(2 * width)] * 2
    specs += [weight_spec(2 * width, w.shape[1]) for w in (wk, wv)]
    specs += [fixed(a.shape) for a in (kv_sum, cos, sin)]
    return pl.pallas_call(
        functools.partial(kv_last_kernel, len(mine), gain.shape[1]),
        out_shape=[
            jax.ShapeDtypeStruct((cap, 256), BF16),
            jax.ShapeDtypeStruct((cap, 256), F32),
        ],
        grid_spec=pltpu.PrefetchScalarGridSpec(
            num_scalar_prefetch=1,
            grid=(1,),
            in_specs=specs,
            out_specs=[fixed((cap, 256)), fixed((cap, 256))],
        ),
        compiler_params=params(),
        name="kv_last",
    )(chip, *mine, *twin, gain, router, wk, wv, kv_sum, cos, sin)


def attend(q, kv, visible, carry, heads):
    k, v = kv[:, 0:128], kv[:, 128:256]
    scale = LOG2E / HEAD_SIZE**0.5
    rows = visible.shape[0]
    out = []
    for h in range(heads):
        s = lax.dot_general(q[h], k, (((1,), (1,)), ((), ())), preferred_element_type=F32) * scale
        s = jnp.where(visible, s, -1e30)
        top = jnp.max(s, axis=1, keepdims=True)
        if carry is not None:
            old_top, old_total, old_mix = carry[h]
            top = jnp.maximum(top, old_top)
        e = jnp.where(visible, jnp.exp2(s - top), 0.0)
        total = jnp.sum(e, axis=1, keepdims=True)
        mix = jnp.dot(e.astype(BF16), v, preferred_element_type=F32)
        if carry is not None:
            fade = jnp.exp2(old_top - top)
            total = total + old_total * fade
            mix = mix + old_mix * fade
        out.append((top, total, mix))
    return out


def keep_carry(state, top_ref, total_ref, mix_ref):
    rows = state[0][0].shape[0]
    for h, (top, total, mix) in enumerate(state):
        at = slice(h * 128, (h + 1) * 128)
        top_ref[:, at] = jnp.broadcast_to(top, (rows, 128))
        total_ref[:, at] = jnp.broadcast_to(total, (rows, 128))
        mix_ref[:, at] = mix


def q_last_kernel(n_mine, tok, chip_ref, cnt_ref, *refs):
    mine, twin = joined(refs[:n_mine]), joined(refs[n_mine : 2 * n_mine])
    (gain_ref, wq_ref, q_in, stat_ref, cos_ref, sin_ref, kv_ref, pos_ref, rowpos_ref) = refs[
        2 * n_mine : 2 * n_mine + 9
    ]
    q_out, top_ref, total_ref, mix_ref = refs[2 * n_mine + 9 :]
    core = lax.rem(lax.axis_index("heads"), 2)
    width = mine.shape[1]
    scaled = []
    for x, at in ((mine, core), (twin, 1 - core)):
        rows = pl.ds(pl.multiple_of(at * width, width), width)
        scaled.append((x.astype(F32) * gain_ref[:, rows]).astype(BF16))
    q = (q_in[...] + q_term(scaled, wq_ref)) * stat_ref[:, 0:1]
    heads = q.shape[1] // HEAD_SIZE
    cos, sin = cos_ref[...], sin_ref[...]
    turned = [turn(q[:, h * 128 : (h + 1) * 128], cos, sin).astype(BF16) for h in range(heads)]
    for h in range(heads):
        q_out[:, h * 128 : (h + 1) * 128] = turned[h]
    own = lax.axis_index("ctx")
    shards = lax.axis_size("ctx")
    keys = live_row(pos_ref, cnt_ref, own, shards * tok + 1)
    visible = keys <= rowpos_ref[:, 0:1]
    state = attend(turned, kv_ref[...], visible, None, heads)
    keep_carry(state, top_ref, total_ref, mix_ref)


def q_last(chip, counts, pair, gain, wq, q_sum, stat, cos, sin, kv, positions, rowpos, tok):
    mine, twin = pair
    cap = sum(x.shape[0] for x in mine)
    width = mine[0].shape[1]
    columns = wq.shape[1]
    vector = pl.BlockSpec((1, 2 * width), lambda i, chip, cnt: (0, chip[0]))
    weight = pl.BlockSpec((2 * width, columns), lambda i, chip, cnt: (chip[0], 0))
    specs = [fixed(x.shape) for x in (*mine, *twin)] + [vector, weight]
    rest = (q_sum, stat, cos, sin, kv, positions, rowpos)
    specs += [fixed(a.shape) for a in rest]
    return pl.pallas_call(
        functools.partial(q_last_kernel, len(mine), tok),
        out_shape=[jax.ShapeDtypeStruct((cap, columns), BF16)]
        + [jax.ShapeDtypeStruct((cap, columns), F32)] * 3,
        grid_spec=pltpu.PrefetchScalarGridSpec(
            num_scalar_prefetch=2,
            grid=(1,),
            in_specs=specs,
            out_specs=[fixed((cap, columns))] * 4,
        ),
        compiler_params=params(),
        name="q_last",
    )(chip, counts, *mine, *twin, gain, wq, *rest)


def attend_kernel(step, last, tok, cnt_ref, q_ref, kv_ref, pos_ref, rowpos_ref, top_in, total_in, mix_in, *outs):
    shards = lax.axis_size("ctx")
    source = lax.rem(lax.axis_index("ctx") + shards - step, shards)
    keys = live_row(pos_ref, cnt_ref, source, shards * tok + 1)
    visible = keys <= rowpos_ref[:, 0:1]
    heads = q_ref.shape[1] // HEAD_SIZE
    q, carry = [], []
    for h in range(heads):
        at = slice(h * 128, (h + 1) * 128)
        q.append(q_ref[:, at])
        carry.append((top_in[:, h * 128 : h * 128 + 1], total_in[:, h * 128 : h * 128 + 1], mix_in[:, at]))
    state = attend(q, kv_ref[...], visible, carry, heads)
    if not last:
        keep_carry(state, *outs)
        return
    full, first, second = outs
    half = first.shape[0]
    for h, (_, total, mix) in enumerate(state):
        at = slice(h * 128, (h + 1) * 128)
        attn = (mix / total).astype(BF16)
        full[:, at] = attn
        first[:, at] = attn[:half]
        second[:, at] = attn[half:]


def attend_more(step, last, tok, counts, q, kv, positions, rowpos, carry):
    cap, columns = q.shape
    if last:
        shapes = [
            jax.ShapeDtypeStruct((cap, columns), BF16),
            jax.ShapeDtypeStruct((cap // 2, columns), BF16),
            jax.ShapeDtypeStruct((cap // 2, columns), BF16),
        ]
    else:
        shapes = [jax.ShapeDtypeStruct((cap, columns), F32)] * 3
    return pl.pallas_call(
        functools.partial(attend_kernel, step, last, tok),
        out_shape=shapes,
        in_specs=[pl.BlockSpec(memory_space=pltpu.SMEM)] + [whole()] * 7,
        out_specs=[whole()] * 3,
        compiler_params=params(),
        name="attend_more",
    )(counts, q, kv, positions, rowpos, *carry)


def out_term(mine, twin, w_ref):
    core = lax.rem(lax.axis_index("heads"), 2)
    width = mine.shape[1]
    out = None
    for x, at in ((mine, core), (twin, 1 - core)):
        rows = pl.ds(pl.multiple_of(at * width, width), width)
        part = jnp.dot(x, w_ref[rows, :], preferred_element_type=F32)
        out = part if out is None else out + part
    return out


def out_kernel(n_mine, fresh, chip_ref, *refs):
    mine, twin = joined(refs[:n_mine]), joined(refs[n_mine : 2 * n_mine])
    w_ref = refs[2 * n_mine]
    term = out_term(mine, twin, w_ref)
    refs[-1][...] = term if fresh else refs[2 * n_mine + 1][...] + term


def out_part(chip, pair, w_out, total):
    mine, twin = pair
    cap = sum(x.shape[0] for x in mine)
    width = mine[0].shape[1]
    columns = w_out.shape[1]
    operands = [*mine, *twin, w_out]
    specs = [fixed(x.shape) for x in (*mine, *twin)] + [weight_spec(2 * width, columns)]
    aliases = {}
    if total is not None:
        aliases = {1 + len(operands): 0}
        operands.append(total)
        specs.append(fixed(total.shape))
    return pl.pallas_call(
        functools.partial(out_kernel, len(mine), total is None),
        out_shape=jax.ShapeDtypeStruct((cap, columns), F32),
        grid_spec=pltpu.PrefetchScalarGridSpec(
            num_scalar_prefetch=1, grid=(1,), in_specs=specs, out_specs=fixed((cap, columns))
        ),
        input_output_aliases=aliases,
        compiler_params=params(),
        cost_estimate=pl.CostEstimate(
            flops=2 * cap * 2 * width * columns, bytes_accessed=3 * 1024 * 1024, transcendentals=0
        ),
        name="out_part",
    )(chip, *operands)


def out_last_kernel(n_mine, chip_ref, cnt_ref, *refs):
    x_refs = refs[: 2 * n_mine]
    w_ref, sum_ref, stat_ref, pos_ref, flag_ref, hid_ref, out_ref, update_ref = refs[2 * n_mine :]
    step = pl.program_id(0)
    block = hid_ref.shape[0]

    @pl.when(step == 0)
    def _():
        mine, twin = joined(x_refs[:n_mine]), joined(x_refs[n_mine:])
        projected = sum_ref[...] + out_term(mine, twin, w_ref)
        update_ref[...] = (stat_ref[:, 128:129] * projected).astype(BF16)

    own = lax.axis_index("ctx")
    shards = lax.axis_size("ctx")
    tok = block * pl.num_programs(0)
    row = live_row(pos_ref, cnt_ref, own, shards * tok) - own * tok - step * block
    hot = (lax.broadcasted_iota(jnp.int32, (block, row.shape[1]), 0) == row).astype(F32).astype(BF16)
    placed = jnp.dot(hot, update_ref[...], preferred_element_type=F32)
    flag = jnp.transpose(jnp.broadcast_to(flag_ref[pl.ds(step, 1), :].astype(F32), (128, block)))[:, :1]
    out_ref[...] = (hid_ref[...].astype(F32) + flag * placed).astype(BF16)


def out_last(chip, counts, pair, w_out, total, stat, positions, flags, hidden):
    mine, twin = pair
    cap = sum(x.shape[0] for x in mine)
    width = mine[0].shape[1]
    tok, columns = hidden.shape
    steps = 4
    block = tok // steps
    flags = flags.reshape(steps, block)
    specs = [fixed(x.shape) for x in (*mine, *twin)]
    specs += [pl.BlockSpec((2 * width, columns), lambda i, chip, cnt: (chip[0], 0))]
    specs += [fixed(a.shape) for a in (total, stat, positions, flags)]
    rows = pl.BlockSpec((block, columns), lambda i, chip, cnt: (i, 0))
    return pl.pallas_call(
        functools.partial(out_last_kernel, len(mine)),
        out_shape=jax.ShapeDtypeStruct((tok, columns), BF16),
        grid_spec=pltpu.PrefetchScalarGridSpec(
            num_scalar_prefetch=2,
            grid=(steps,),
            in_specs=specs + [rows],
            out_specs=rows,
            scratch_shapes=[pltpu.VMEM((cap, columns), BF16)],
        ),
        compiler_params=params(),
        name="out_last",
    )(chip, counts, *mine, *twin, w_out, total, stat, positions, flags, hidden)


def angles(row_pos):
    half = HEAD_SIZE // 2
    frequency = ROPE_BASE ** (-(jnp.arange(half, dtype=F32) * 2.0 / HEAD_SIZE))
    turned = row_pos.astype(F32) * jnp.concatenate([frequency, frequency])[None, :]
    sign = jnp.concatenate([-jnp.ones((half,), F32), jnp.ones((half,), F32)])
    return jnp.cos(turned), jnp.sin(turned) * sign[None, :]


def body(
    size,
    hidden_in,
    norm_gain,
    router_weight,
    w_query,
    w_key,
    value_weight,
    w_out,
    keep_flags,
    keep_counts,
    keep_positions,
):
    shards = lax.axis_size("ctx")
    tok = hidden_in.shape[0]
    z = lax.axis_index("heads") // 2
    chips = [jnp.reshape(c, (1,)).astype(jnp.int32) for c in (z, 3 - z, z ^ 1, z ^ 2)]
    gain = norm_gain.reshape(1, -1)
    router = router_weight.reshape(1, -1)

    full, first, second, rowpos = pick(keep_counts, keep_positions, hidden_in)
    cos, sin = angles(rowpos)
    pairs = spread(size, full, first, second)
    sums = None
    for chip, pair in zip(chips[:3], pairs[:3]):
        sums = qkv_part(chip, pair, gain, router, w_query, w_key, value_weight, sums)
    kv, stat = kv_last(chips[3], pairs[3], gain, router, w_key, value_weight, sums[0], cos, sin)
    ring = [(s, (s + 1) % shards) for s in range(shards)]
    moved = lax.ppermute(kv, "ctx", ring) if shards > 1 else kv
    q, *carry = q_last(
        chips[3], keep_counts, pairs[3], gain, w_query, sums[1], stat, cos, sin, kv, keep_positions, rowpos, tok
    )
    for step in range(1, shards):
        last = step == shards - 1
        carry = attend_more(step, last, tok, keep_counts, q, moved, keep_positions, rowpos, carry)
        if not last:
            moved = lax.ppermute(moved, "ctx", ring)
    pairs = spread(size, *carry)
    total = None
    for chip, pair in zip(chips[:3], pairs[:3]):
        total = out_part(chip, pair, w_out, total)
    return out_last(
        chips[3], keep_counts, pairs[3], w_out, total, stat, keep_positions, keep_flags, hidden_in
    )


def solution(mesh):
    in_specs = (
        P(("groups", "ctx"), "heads"),
        P(),
        P(),
        P(None, "heads"),
        P(None, "heads"),
        P(None, "heads"),
        P(None, "heads"),
        P(("groups", "ctx")),
        P("groups"),
        P("groups", None),
    )
    out_specs = P(("groups", "ctx"), "heads")
    return jax.shard_map(
        functools.partial(body, mesh.shape["heads"]),
        mesh=mesh,
        in_specs=in_specs,
        out_specs=out_specs,
        check_vma=False,
    )
```

```python
import functools

import jax
import jax.numpy as jnp
from jax import lax
from jax.experimental import pallas as pl
from jax.experimental.pallas import tpu as pltpu
from jax.sharding import PartitionSpec as P

HEAD_SIZE = 128
ROPE_BASE = 500000.0
NORM_EPS = 1e-05
LOG2E = 1.4426950408889634
VMEM_LIMIT = 24 * 1024 * 1024
F32 = jnp.float32
BF16 = jnp.bfloat16
I32 = jnp.int32
COST = 400_000_000
OWN_OUT = 400_000_000
FAR_OUT = 400_000_000
BESIDE_OUT = 400_000_000

VMEM = pl.BlockSpec(memory_space=pltpu.VMEM)
HBM = pl.BlockSpec(memory_space=pltpu.HBM)


def arr(shape, dtype):
    return jax.ShapeDtypeStruct(shape, dtype)


def call(kernel, name, operands, out_shape, scratch=(), rides=None, hbm=(), out_hbm=False, flops=COST):
    operands = [(o, any(o is h for h in hbm)) for o in operands]
    return pl.pallas_call(
        kernel,
        out_shape=out_shape,
        in_specs=[HBM if far else VMEM for _, far in operands],
        out_specs=[HBM if out_hbm else VMEM] * len(out_shape),
        scratch_shapes=list(scratch),
        input_output_aliases=rides or {},
        compiler_params=pltpu.CompilerParams(vmem_limit_bytes=VMEM_LIMIT),
        cost_estimate=pl.CostEstimate(flops=flops, bytes_accessed=1, transcendentals=0),
        name=name,
    )(*(pltpu.with_memory_space_constraint(o, pltpu.HBM) if far else o for o, far in operands))


def fetch(pairs, sems, base=0):
    copies = [pltpu.make_async_copy(src, dst, sems.at[base + i]) for i, (src, dst) in enumerate(pairs)]
    for copy in copies:
        copy.start()
    return copies


def place():
    d = lax.axis_index("heads")
    return d // 2, lax.rem(d, 2)


def live_row(pos_ref, cnt_ref, shard, dead):
    pos = pos_ref[pl.ds(shard, 1), :]
    slot = lax.broadcasted_iota(I32, pos.shape, 1)
    return jnp.where(slot < cnt_ref[shard], pos, dead)


def column(row):
    return jnp.transpose(jnp.broadcast_to(row, (128, row.shape[1])))


def pick_kernel(cnt_hbm, pos_hbm, hid_hbm, x_ref, xa_ref, xb_ref, rowpos_ref, cnt_ref, pos_ref, hid_ref, sems):
    copies = fetch([(cnt_hbm, cnt_ref), (pos_hbm, pos_ref), (hid_hbm, hid_ref)], sems)
    own, shards = lax.axis_index("ctx"), lax.axis_size("ctx")
    tok, cap = hid_ref.shape[0], x_ref.shape[0]
    copies[0].wait()
    copies[1].wait()
    rowpos = column(live_row(pos_ref, cnt_ref, own, shards * tok))
    rowpos_ref[...] = rowpos
    local = rowpos[:, :1] - own * tok
    hot = (lax.broadcasted_iota(I32, (cap, tok), 1) == local).astype(F32).astype(BF16)
    copies[2].wait()
    x = jnp.dot(hot, hid_ref[...], preferred_element_type=F32).astype(BF16)
    x_ref[...] = x
    xa_ref[...] = x[: cap // 2]
    xb_ref[...] = x[cap // 2 :]


def pick(counts, positions, hidden):
    cap, width = positions.shape[1], hidden.shape[1]
    return call(
        pick_kernel,
        "pick",
        (counts, positions, hidden),
        [arr((cap, width), BF16), arr((cap // 2, width), BF16), arr((cap // 2, width), BF16), arr((cap, 128), I32)],
        scratch=[
            pltpu.SMEM(counts.shape, I32),
            pltpu.VMEM(positions.shape, I32),
            pltpu.VMEM(hidden.shape, BF16),
            pltpu.SemaphoreType.DMA((3,)),
        ],
        hbm=(counts, positions, hidden),
    )


def sender(perm):
    return functools.partial(lax.ppermute, axis_name="heads", perm=perm)


def chip_sender(size, f):
    return sender([(2 * z + c, 2 * f(z) + c) for z in range(size // 2) for c in range(2)])


def spread(size, full, first, second, use_own, use_far, use_beside):
    cross = chip_sender(size, lambda z: 3 - z)
    near = chip_sender(size, lambda z: z ^ 1)
    twin = sender([(d, d ^ 1) for d in range(size)])
    far_a, far_b = cross(first), cross(second)
    mate = twin(full)
    full = use_own(full, mate)
    beside = near(full)
    last_a, last_b = near(far_a), near(far_b)
    last_a = use_far((far_a, far_b), (twin(far_a), twin(far_b)), last_a)
    use_beside((beside,), (twin(beside),))
    return last_a, last_b, twin(last_a), twin(last_b)


def joined(refs):
    parts = [ref[...] for ref in refs]
    return parts[0] if len(parts) == 1 else jnp.concatenate(parts, axis=0)


def lanes_sum(x):
    total = x[:, :128]
    for at in range(128, x.shape[1], 128):
        total = total + x[:, at : at + 128]
    return total


def halves(mine, twin, core):
    width = mine.shape[1]
    return [(x, pl.ds(pl.multiple_of(at * width, width), width)) for x, at in ((mine, core), (twin, 1 - core))]


def add(a, b):
    return b if a is None else a + b


def project(mine, twin, core, gain_ref, router_ref, w_ref, columns, stats=True):
    product = squares = routed = None
    for x, rows in halves(mine, twin, core):
        xf = x.astype(F32)
        gained = (xf * gain_ref[:, rows]).astype(BF16)
        product = add(product, jnp.dot(gained, w_ref[rows, columns], preferred_element_type=F32))
        if stats:
            squares = add(squares, lanes_sum(xf * xf))
            routed = add(routed, lanes_sum(xf * router_ref[:, rows]))
    return product, squares, routed


def block_copies(zz, gain, router, wq, wk, wv, gain_ref, router_ref, w_ref):
    depth = w_ref.shape[0]
    rows = pl.ds(pl.multiple_of(zz * depth, depth), depth)
    nq, nk = wq.shape[1], wk.shape[1]
    return [
        (gain.at[:, rows], gain_ref),
        (router.at[:, rows], router_ref),
        (wq.at[rows, :], w_ref.at[:, 0:nq]),
        (wk.at[rows, :], w_ref.at[:, nq : nq + nk]),
        (wv.at[rows, :], w_ref.at[:, nq + nk : nq + 2 * nk]),
    ]


def fetched(zz, weights, scratch, sems, base=0):
    return fetch(block_copies(zz, *weights, *scratch), sems, base)


def settle(copies):
    for copy in copies:
        copy.wait()


def own_kernel(x_ref, mate_ref, gain, router, wq, wk, wv, cnt_hbm, pos_hbm, flag_hbm, *refs):
    ride, sums_ref, bias_ref, hot_ref = refs[:4]
    gain_ref, router_ref, w_ref, cnt_ref, pos_ref, flag_ref, sems = refs[4:]
    zz, core = place()
    small = fetch([(cnt_hbm, cnt_ref), (pos_hbm, pos_ref), (flag_hbm, flag_ref)], sems, 5)
    copies = fetched(zz, (gain, router, wq, wk, wv), (gain_ref, router_ref, w_ref), sems)
    settle(small)
    own, shards = lax.axis_index("ctx"), lax.axis_size("ctx")
    tok = hot_ref.shape[0]
    seq = shards * tok
    row = live_row(pos_ref, cnt_ref, own, seq)
    for step in range(shards):
        source = lax.rem(own + shards - step, shards)
        keys = column(live_row(pos_ref, cnt_ref, source, seq + 1))[:, :1]
        bias_ref[step] = jnp.where(keys <= row, 0.0, -jnp.inf).astype(F32)
    flags = jnp.transpose(flag_ref[...].astype(F32))
    local = row - own * tok
    for r in range(tok // 128):
        at = lax.broadcasted_iota(I32, (128, row.shape[1]), 0) + r * 128
        hot = jnp.where(at == local, flags[:, r : r + 1], 0.0)
        hot_ref[r * 128 : (r + 1) * 128, :] = hot.astype(BF16)
    settle(copies)
    product, squares, routed = project(x_ref[...], mate_ref[...], core, gain_ref, router_ref, w_ref, slice(None))
    n = product.shape[1]
    sums_ref[:, 0:n] = product
    sums_ref[:, n : n + 128] = squares
    sums_ref[:, n + 128 : n + 256] = routed


def weight_scratch(depth, columns):
    return [pltpu.VMEM((1, depth), F32), pltpu.VMEM((1, depth), F32), pltpu.VMEM((depth, columns), BF16)]


def own_part(full, mate, weights, counts, positions, flags, tok):
    cap, width = full.shape
    columns = sum(w.shape[1] for w in weights[2:])
    shards = positions.shape[0]
    operands = (full, mate, *weights, counts, positions, flags)
    return call(
        own_kernel,
        "own_part",
        operands,
        [
            arr(full.shape, BF16),
            arr((cap, columns + 256), F32),
            arr((shards, cap, cap), F32),
            arr((tok, cap), BF16),
        ],
        scratch=weight_scratch(2 * width, columns)
        + [
            pltpu.SMEM(counts.shape, I32),
            pltpu.VMEM(positions.shape, I32),
            pltpu.VMEM(flags.shape, I32),
            pltpu.SemaphoreType.DMA((8,)),
        ],
        rides={0: 0},
        hbm=operands[2:],
    )


def more_kernel(n_mine, n_ride, flip, keep, *refs):
    mine, twin, refs = refs[:n_mine], refs[n_mine : 2 * n_mine], refs[2 * n_mine :]
    sums_in, refs = refs[0], refs[1 + n_ride :]
    weights, sums_out, refs = refs[:5], refs[5], refs[6 + n_ride :]
    kept, scratch, sems = refs[:-4], refs[-4:-1], refs[-1]
    z, core = place()
    copies = fetched(flip(z), weights, scratch, sems)
    later = fetched(z ^ 2, weights, kept, sems, 5) if keep else []
    settle(copies)
    product, squares, routed = project(joined(mine), joined(twin), core, *scratch, slice(None))
    n = product.shape[1]
    sums_out[:, 0:n] = sums_in[:, 0:n] + product
    sums_out[:, n : n + 128] = sums_in[:, n : n + 128] + squares
    sums_out[:, n + 128 : n + 256] = sums_in[:, n + 128 : n + 256] + routed
    settle(later)


def more_part(mine, twin, sums, rides, weights, flip, keep):
    width = mine[0].shape[1]
    depth, columns = 2 * width, sum(w.shape[1] for w in weights[2:])
    operands = (*mine, *twin, sums, *rides, *weights)
    at = 2 * len(mine)
    kept = [arr((1, depth), F32), arr((1, depth), F32), arr((depth, columns), BF16)] if keep else []
    return call(
        functools.partial(more_kernel, len(mine), len(rides), flip, keep),
        "more_part",
        operands,
        [arr(sums.shape, F32), *(arr(r.shape, BF16) for r in rides), *kept],
        scratch=weight_scratch(depth, columns) + [pltpu.SemaphoreType.DMA((10,))],
        rides={at + i: i for i in range(1 + len(rides))},
        hbm=weights,
    )


def turn(x, cos, sin):
    return x * cos + pltpu.roll(x, HEAD_SIZE // 2, 1) * sin


def kv_last_kernel(nq, features, a, b, c, d, gain_ref, router_ref, w_ref, sums, cos_ref, sin_ref, kv_out, stat_out):
    _, core = place()
    mine, twin = joined((a, b)), joined((c, d))
    n = w_ref.shape[1]
    product, squares, routed = project(mine, twin, core, gain_ref, router_ref, w_ref, slice(nq, n))
    squares = jnp.sum(sums[:, n : n + 128] + squares, axis=1, keepdims=True)
    routed = jnp.sum(sums[:, n + 128 : n + 256] + routed, axis=1, keepdims=True)
    inverse = lax.rsqrt(squares * (1.0 / features) + NORM_EPS)
    kv = (sums[:, nq:n] + product) * inverse
    kv_out[:, 0:128] = turn(kv[:, 0:128], cos_ref[...], sin_ref[...]).astype(BF16)
    kv_out[:, 128:256] = kv[:, 128:256].astype(BF16)
    stat_out[:, 0:128] = jnp.broadcast_to(inverse, (inverse.shape[0], 128))
    gate = 1.0 / (1.0 + jnp.exp(-routed))
    stat_out[:, 128:256] = jnp.broadcast_to(gate, (gate.shape[0], 128))


def kv_last(pair, kept, sums, cos, sin, nq, features):
    cap = sums.shape[0]
    return call(
        functools.partial(kv_last_kernel, nq, features),
        "kv_last",
        (*pair, *kept, sums, cos, sin),
        [arr((cap, 256), BF16), arr((cap, 256), F32)],
    )


def attend(q, kv, bias, carry):
    k, v = kv[:, 0:128], kv[:, 128:256]
    scale = LOG2E / HEAD_SIZE**0.5
    s = lax.dot_general(k, q, (((1,), (1,)), ((), ())), preferred_element_type=F32) * scale + bias
    top = jnp.max(s, axis=0, keepdims=True)
    if carry is not None:
        top = jnp.maximum(top, carry[0])
    e = jnp.exp2(s - top)
    total = jnp.sum(e, axis=0, keepdims=True)
    mix = lax.dot_general(v, e.astype(BF16), (((0,), (0,)), ((), ())), preferred_element_type=F32)
    if carry is not None:
        fade = jnp.exp2(carry[0] - top)
        total = total + carry[1] * fade
        mix = mix + carry[2] * fade
    return top, total, mix


def q_last_kernel(a, b, c, d, gain_ref, w_ref, sums, stat_ref, cos_ref, sin_ref, kv_ref, bias_ref, *outs):
    q_out, top_ref, total_ref, mix_ref = outs
    _, core = place()
    mine, twin = joined((a, b)), joined((c, d))
    nq, cap = q_out.shape[1], q_out.shape[0]
    product, _, _ = project(mine, twin, core, gain_ref, None, w_ref, slice(0, nq), stats=False)
    q = (sums[:, 0:nq] + product) * stat_ref[:, 0:1]
    cos, sin = cos_ref[...], sin_ref[...]
    for h in range(nq // HEAD_SIZE):
        lanes = slice(h * HEAD_SIZE, (h + 1) * HEAD_SIZE)
        turned = turn(q[:, lanes], cos, sin).astype(BF16)
        q_out[:, lanes] = turned
        top, total, mix = attend(turned, kv_ref[...], bias_ref[0], None)
        at = slice(h * cap, (h + 1) * cap)
        top_ref[:, at], total_ref[:, at], mix_ref[:, at] = top, total, mix


def carry_shapes(cap, nq):
    heads = nq // HEAD_SIZE
    return [arr((1, heads * cap), F32), arr((1, heads * cap), F32), arr((HEAD_SIZE, heads * cap), F32)]


def q_last(pair, kept, sums, stat, cos, sin, kv, bias, nq):
    cap = sums.shape[0]
    return call(
        q_last_kernel,
        "q_last",
        (*pair, kept[0], kept[2], sums, stat, cos, sin, kv, bias),
        [arr((cap, nq), BF16), *carry_shapes(cap, nq)],
    )


def attend_kernel(step, last, q_ref, kv_ref, bias_ref, top_in, total_in, mix_in, *outs):
    cap, nq = q_ref.shape
    for h in range(nq // HEAD_SIZE):
        lanes = slice(h * HEAD_SIZE, (h + 1) * HEAD_SIZE)
        at = slice(h * cap, (h + 1) * cap)
        carry = (top_in[:, at], total_in[:, at], mix_in[:, at])
        top, total, mix = attend(q_ref[:, lanes], kv_ref[...], bias_ref[step], carry)
        if not last:
            outs[0][:, at], outs[1][:, at], outs[2][:, at] = top, total, mix
            continue
        full, first, second = outs
        half = cap // 2
        attn = jnp.transpose(mix * (1.0 / total)).astype(BF16)
        full[:, lanes] = attn
        first[:, lanes] = attn[:half]
        second[:, lanes] = attn[half:]


def attend_more(step, last, q, kv, bias, carry):
    cap, nq = q.shape
    shapes = [arr((cap, nq), BF16), arr((cap // 2, nq), BF16), arr((cap // 2, nq), BF16)]
    return call(
        functools.partial(attend_kernel, step, last),
        "attend_more",
        (q, kv, bias, *carry),
        shapes if last else carry_shapes(cap, nq),
    )


def out_term(mine, twin, core, w_ref):
    out = None
    for x, rows in halves(mine, twin, core):
        out = add(out, jnp.dot(x, w_ref[rows, :], preferred_element_type=F32))
    return out


def w_rows(w, zz, depth):
    return w.at[pl.ds(pl.multiple_of(zz * depth, depth), depth), :]


def out_own_kernel(x_ref, mate_ref, w, ride, out_ref, w_ref, sems):
    z, core = place()
    settle(fetch([(w_rows(w, z, w_ref.shape[0]), w_ref)], sems))
    out_ref[...] = out_term(x_ref[...], mate_ref[...], core, w_ref)


def out_own(full, mate, w_out):
    (cap, width), columns = full.shape, w_out.shape[1]
    return call(
        out_own_kernel,
        "out_own",
        (full, mate, w_out),
        [arr(full.shape, BF16), arr((cap, columns), F32)],
        scratch=[pltpu.VMEM((2 * width, columns), BF16), pltpu.SemaphoreType.DMA((1,))],
        rides={0: 0},
        hbm=(w_out,),
        flops=OWN_OUT,
    )


def out_more_kernel(n_mine, n_ride, flip, keep, *refs):
    mine, twin, refs = refs[:n_mine], refs[n_mine : 2 * n_mine], refs[2 * n_mine :]
    total_in, refs = refs[0], refs[1 + n_ride :]
    w, refs = refs[0], refs[1:]
    hidden, refs = (refs[0], refs[1:]) if keep else (None, refs)
    total_out, refs = refs[0], refs[1 + n_ride :]
    w_ref, sems = refs[-2:]
    z, core = place()
    depth = w_ref.shape[0]
    copies = fetch([(w_rows(w, flip(z), depth), w_ref)], sems)
    later = fetch([(w_rows(w, z ^ 2, depth), refs[0]), (hidden, refs[1])], sems, 1) if keep else []
    settle(copies)
    total_out[...] = total_in[...] + out_term(joined(mine), joined(twin), core, w_ref)
    settle(later)


def out_more(mine, twin, total, rides, w_out, flip, hidden=None):
    width, columns = mine[0].shape[1], w_out.shape[1]
    keep = hidden is not None
    operands = (*mine, *twin, total, *rides, w_out) + ((hidden,) if keep else ())
    at = 2 * len(mine)
    kept = [arr((2 * width, columns), BF16), arr(hidden.shape, BF16)] if keep else []
    return call(
        functools.partial(out_more_kernel, len(mine), len(rides), flip, keep),
        "out_more",
        operands,
        [arr(total.shape, F32), *(arr(r.shape, BF16) for r in rides), *kept],
        scratch=[pltpu.VMEM((2 * width, columns), BF16), pltpu.SemaphoreType.DMA((3,))],
        rides={at + i: i for i in range(1 + len(rides))},
        hbm=(w_out, hidden) if keep else (w_out,),
        flops=BESIDE_OUT if keep else FAR_OUT,
    )


def out_last_kernel(a, b, c, d, w_ref, total_ref, stat_ref, hot_ref, hid_ref, out, out_ref, sems):
    _, core = place()
    projected = total_ref[...] + out_term(joined((a, b)), joined((c, d)), core, w_ref)
    update = (stat_ref[:, 128:129] * projected).astype(BF16)
    block = 256
    copies = []
    for i in range(hid_ref.shape[0] // block):
        rows = slice(i * block, (i + 1) * block)
        placed = jnp.dot(hot_ref[rows, :], update, preferred_element_type=F32)
        out_ref[rows, :] = (hid_ref[rows, :].astype(F32) + placed).astype(BF16)
        copies += fetch([(out_ref.at[rows, :], out.at[rows, :])], sems, i)
    settle(copies)


def out_last(pair, w_kept, total, stat, hot, hidden):
    return call(
        out_last_kernel,
        "out_last",
        (*pair, w_kept, total, stat, hot, hidden),
        [arr(hidden.shape, BF16)],
        scratch=[pltpu.VMEM(hidden.shape, BF16), pltpu.SemaphoreType.DMA((hidden.shape[0] // 256,))],
        out_hbm=True,
    )[0]


def angles(row_pos):
    half = HEAD_SIZE // 2
    frequency = ROPE_BASE ** (-(jnp.arange(half, dtype=F32) * 2.0 / HEAD_SIZE))
    turned = row_pos.astype(F32) * jnp.concatenate([frequency, frequency])[None, :]
    sign = jnp.concatenate([-jnp.ones((half,), F32), jnp.ones((half,), F32)])
    return jnp.cos(turned), jnp.sin(turned) * sign[None, :]


def body(
    size,
    hidden_in,
    norm_gain,
    router_weight,
    w_query,
    w_key,
    value_weight,
    w_out,
    keep_flags,
    keep_counts,
    keep_positions,
):
    shards = lax.axis_size("ctx")
    tok = hidden_in.shape[0]
    nq = w_query.shape[1]
    flags = keep_flags.reshape(-1, 128)
    weights = (norm_gain.reshape(1, -1), router_weight.reshape(1, -1), w_query, w_key, value_weight)

    full, first, second, rowpos = pick(keep_counts, keep_positions, hidden_in)
    cos, sin = angles(rowpos)
    held = {}

    def own(x, mate):
        x, held["sums"], held["bias"], held["hot"] = own_part(
            x, mate, weights, keep_counts, keep_positions, flags, tok
        )
        return x

    def far(mine, twin, ride):
        held["sums"], ride = more_part(mine, twin, held["sums"], (ride,), weights, lambda z: 3 - z, False)
        return ride

    def beside(mine, twin):
        held["sums"], *held["kept"] = more_part(mine, twin, held["sums"], (), weights, lambda z: z ^ 1, True)

    pair = spread(size, full, first, second, own, far, beside)
    sums, kept, bias = held["sums"], held["kept"], held["bias"]
    kv, stat = kv_last(pair, kept, sums, cos, sin, nq, norm_gain.shape[0])
    ring = [(s, (s + 1) % shards) for s in range(shards)]
    moved = lax.ppermute(kv, "ctx", ring)
    q, *carry = q_last(pair, kept, sums, stat, cos, sin, kv, bias, nq)
    for step in range(1, shards):
        last = step == shards - 1
        carry = attend_more(step, last, q, moved, bias, carry)
        if not last:
            moved = lax.ppermute(moved, "ctx", ring)

    def own_out(x, mate):
        x, held["total"] = out_own(x, mate, w_out)
        return x

    def far_out(mine, twin, ride):
        held["total"], ride = out_more(mine, twin, held["total"], (ride,), w_out, lambda z: 3 - z)
        return ride

    def beside_out(mine, twin):
        held["total"], held["w"], held["hidden"] = out_more(
            mine, twin, held["total"], (), w_out, lambda z: z ^ 1, hidden_in
        )

    pair = spread(size, *carry, own_out, far_out, beside_out)
    return out_last(pair, held["w"], held["total"], stat, held["hot"], held["hidden"])


def solution(mesh):
    in_specs = (
        P(("groups", "ctx"), "heads"),
        P(),
        P(),
        P(None, "heads"),
        P(None, "heads"),
        P(None, "heads"),
        P(None, "heads"),
        P(("groups", "ctx")),
        P("groups"),
        P("groups", None),
    )
    out_specs = P(("groups", "ctx"), "heads")
    return jax.shard_map(
        functools.partial(body, mesh.shape["heads"]),
        mesh=mesh,
        in_specs=in_specs,
        out_specs=out_specs,
        check_vma=False,
    )
```

```python
import functools

import jax
import jax.numpy as jnp
from jax import lax
from jax.experimental import pallas as pl
from jax.experimental.pallas import tpu as pltpu
from jax.sharding import PartitionSpec as P

HEAD_SIZE = 128
ROPE_BASE = 500000.0
NORM_EPS = 1e-05
LOG2E = 1.4426950408889634
VMEM_LIMIT = 24 * 1024 * 1024
F32 = jnp.float32
BF16 = jnp.bfloat16
I32 = jnp.int32
COST = 400_000_000
PART_COST = 1_500_000_000


VMEM = pl.BlockSpec(memory_space=pltpu.VMEM)
HBM = pl.BlockSpec(memory_space=pltpu.HBM)


def arr(shape, dtype):
    return jax.ShapeDtypeStruct(shape, dtype)


def call(kernel, name, operands, out_shape, scratch=(), rides=None, hbm=(), out_hbm=False, flops=COST):
    operands = [(o, any(o is h for h in hbm)) for o in operands]
    return pl.pallas_call(
        kernel,
        out_shape=out_shape,
        in_specs=[HBM if far else VMEM for _, far in operands],
        out_specs=[HBM if out_hbm else VMEM] * len(out_shape),
        scratch_shapes=list(scratch),
        input_output_aliases=rides or {},
        compiler_params=pltpu.CompilerParams(vmem_limit_bytes=VMEM_LIMIT),
        cost_estimate=pl.CostEstimate(flops=flops, bytes_accessed=1, transcendentals=0),
        name=name,
    )(*(pltpu.with_memory_space_constraint(o, pltpu.HBM) if far else o for o, far in operands))


def fetch(pairs, sems, base=0):
    copies = [pltpu.make_async_copy(src, dst, sems.at[base + i]) for i, (src, dst) in enumerate(pairs)]
    for copy in copies:
        copy.start()
    return copies


def place():
    d = lax.axis_index("heads")
    return d // 2, lax.rem(d, 2)


def live_row(pos_ref, cnt_ref, shard, dead):
    pos = pos_ref[pl.ds(shard, 1), :]
    slot = lax.broadcasted_iota(I32, pos.shape, 1)
    return jnp.where(slot < cnt_ref[shard], pos, dead)


def column(row):
    return jnp.transpose(jnp.broadcast_to(row, (128, row.shape[1])))


def pick_kernel(cnt_hbm, pos_hbm, hid_hbm, x_ref, xa_ref, xb_ref, rowpos_ref, cnt_ref, pos_ref, hid_ref, sems):
    copies = fetch([(cnt_hbm, cnt_ref), (pos_hbm, pos_ref), (hid_hbm, hid_ref)], sems)
    own, shards = lax.axis_index("ctx"), lax.axis_size("ctx")
    tok, cap = hid_ref.shape[0], x_ref.shape[0]
    copies[0].wait()
    copies[1].wait()
    rowpos = column(live_row(pos_ref, cnt_ref, own, shards * tok))
    rowpos_ref[...] = rowpos
    local = rowpos[:, :1] - own * tok
    hot = (lax.broadcasted_iota(I32, (cap, tok), 1) == local).astype(F32).astype(BF16)
    copies[2].wait()
    x = jnp.dot(hot, hid_ref[...], preferred_element_type=F32).astype(BF16)
    x_ref[...] = x
    xa_ref[...] = x[: cap // 2]
    xb_ref[...] = x[cap // 2 :]


def pick(counts, positions, hidden):
    cap, width = positions.shape[1], hidden.shape[1]
    return call(
        pick_kernel,
        "pick",
        (counts, positions, hidden),
        [arr((cap, width), BF16), arr((cap // 2, width), BF16), arr((cap // 2, width), BF16), arr((cap, 128), I32)],
        scratch=[
            pltpu.SMEM(counts.shape, I32),
            pltpu.VMEM(positions.shape, I32),
            pltpu.VMEM(hidden.shape, BF16),
            pltpu.SemaphoreType.DMA((3,)),
        ],
        hbm=(counts, positions, hidden),
    )


def sender(perm):
    return functools.partial(lax.ppermute, axis_name="heads", perm=perm)


def chip_sender(size, f):
    return sender([(2 * z + c, 2 * f(z) + c) for z in range(size // 2) for c in range(2)])


def spread(size, full, first, second, use_own, use_far, use_beside):
    cross = chip_sender(size, lambda z: 3 - z)
    near = chip_sender(size, lambda z: z ^ 1)
    twin = sender([(d, d ^ 1) for d in range(size)])
    far = cross(full)
    mates = twin(first), twin(second)
    beside = near(first), near(second)
    last = near(far)
    beside = use_own((full,), mates, beside)
    beside = use_far((far,), (twin(far),), beside)
    use_beside(beside, (twin(beside[0]), twin(beside[1])))
    return last, twin(last)


def joined(refs):
    parts = [ref[...] for ref in refs]
    return parts[0] if len(parts) == 1 else jnp.concatenate(parts, axis=0)


def lanes_sum(x):
    total = x[:, :128]
    for at in range(128, x.shape[1], 128):
        total = total + x[:, at : at + 128]
    return total


def halves(mine, twin, zz, core):
    width = mine.shape[1]
    rows = [pl.ds(pl.multiple_of((2 * zz + at) * width, width), width) for at in (core, 1 - core)]
    return zip((mine, twin), rows)


def add(a, b):
    return b if a is None else a + b


def project(mine, twin, zz, core, gain_ref, router_ref, w_ref, columns, stats=True):
    product = squares = routed = None
    for x, rows in halves(mine, twin, zz, core):
        xf = x.astype(F32)
        gained = (xf * gain_ref[:, rows]).astype(BF16)
        product = add(product, jnp.dot(gained, w_ref[rows, columns], preferred_element_type=F32))
        if stats:
            squares = add(squares, lanes_sum(xf * xf))
            routed = add(routed, lanes_sum(xf * router_ref[:, rows]))
    return product, squares, routed


def settle(copies):
    for copy in copies:
        copy.wait()


def own_kernel(n_mine, n_twin, *refs):
    mine, twin, refs = refs[:n_mine], refs[n_mine : n_mine + n_twin], refs[n_mine + n_twin :]
    n_ride = (len(refs) - 18) // 2
    gain, router, wq, wk, wv, cnt_hbm, pos_hbm, flag_hbm = refs[n_ride : n_ride + 8]
    sums_ref, bias_ref, hot_ref, gain_ref, router_ref, w_ref = refs[-10:-4]
    cnt_ref, pos_ref, flag_ref, sems = refs[-4:]
    z, core = place()
    small = fetch([(cnt_hbm, cnt_ref), (pos_hbm, pos_ref), (flag_hbm, flag_ref)], sems, 5)
    nq, nk = wq.shape[1], wk.shape[1]
    copies = fetch(
        [
            (gain, gain_ref),
            (router, router_ref),
            (wq, w_ref.at[:, 0:nq]),
            (wk, w_ref.at[:, nq : nq + nk]),
            (wv, w_ref.at[:, nq + nk : nq + 2 * nk]),
        ],
        sems,
    )
    settle(small)
    own, shards = lax.axis_index("ctx"), lax.axis_size("ctx")
    tok = hot_ref.shape[0]
    seq = shards * tok
    row = live_row(pos_ref, cnt_ref, own, seq)
    for step in range(shards):
        source = lax.rem(own + shards - step, shards)
        keys = column(live_row(pos_ref, cnt_ref, source, seq + 1))[:, :1]
        bias_ref[step] = jnp.where(keys <= row, 0.0, -jnp.inf).astype(F32)
    flags = jnp.transpose(flag_ref[...].astype(F32))
    local = row - own * tok
    for r in range(tok // 128):
        at = lax.broadcasted_iota(I32, (128, row.shape[1]), 0) + r * 128
        hot = jnp.where(at == local, flags[:, r : r + 1], 0.0)
        hot_ref[r * 128 : (r + 1) * 128, :] = hot.astype(BF16)
    settle(copies)
    product, squares, routed = project(joined(mine), joined(twin), z, core, gain_ref, router_ref, w_ref, slice(None))
    n = product.shape[1]
    sums_ref[:, 0:n] = product
    sums_ref[:, n : n + 128] = squares
    sums_ref[:, n + 128 : n + 256] = routed


def own_part(mine, twin, rides, weights, counts, positions, flags, tok):
    cap = sum(x.shape[0] for x in mine)
    depth = weights[2].shape[0]
    columns = sum(w.shape[1] for w in weights[2:])
    shards = positions.shape[0]
    far = (*weights, counts, positions, flags)
    at = len(mine) + len(twin)
    return call(
        functools.partial(own_kernel, len(mine), len(twin)),
        "own_part",
        (*mine, *twin, *rides, *far),
        [
            *(arr(r.shape, BF16) for r in rides),
            arr((cap, columns + 256), F32),
            arr((shards, cap, cap), F32),
            arr((tok, cap), BF16),
            arr((1, depth), F32),
            arr((1, depth), F32),
            arr((depth, columns), BF16),
        ],
        scratch=[
            pltpu.SMEM(counts.shape, I32),
            pltpu.VMEM(positions.shape, I32),
            pltpu.VMEM(flags.shape, I32),
            pltpu.SemaphoreType.DMA((8,)),
        ],
        rides={at + i: i for i in range(len(rides))},
        hbm=far,
        flops=PART_COST,
    )


def more_kernel(n_mine, n_twin, flip, *refs):
    mine, twin, refs = refs[:n_mine], refs[n_mine : n_mine + n_twin], refs[n_mine + n_twin :]
    gain_ref, router_ref, w_ref, sums_in = refs[:4]
    sums_out = refs[4 + (len(refs) - 5) // 2]
    z, core = place()
    product, squares, routed = project(
        joined(mine), joined(twin), flip(z), core, gain_ref, router_ref, w_ref, slice(None)
    )
    n = product.shape[1]
    sums_out[:, 0:n] = sums_in[:, 0:n] + product
    sums_out[:, n : n + 128] = sums_in[:, n : n + 128] + squares
    sums_out[:, n + 128 : n + 256] = sums_in[:, n + 128 : n + 256] + routed


def more_part(mine, twin, staged, sums, rides, flip, flops):
    at = len(mine) + len(twin) + 3
    return call(
        functools.partial(more_kernel, len(mine), len(twin), flip),
        "more_part",
        (*mine, *twin, *staged, sums, *rides),
        [arr(sums.shape, F32), *(arr(r.shape, BF16) for r in rides)],
        rides={at + i: i for i in range(1 + len(rides))},
        flops=flops,
    )


def turn(x, cos, sin):
    return x * cos + pltpu.roll(x, HEAD_SIZE // 2, 1) * sin


def kv_last_kernel(nq, mine_ref, twin_ref, gain_ref, router_ref, w_ref, sums, cos_ref, sin_ref, kv_out, stat_out):
    z, core = place()
    n, features = w_ref.shape[1], w_ref.shape[0]
    product, squares, routed = project(
        mine_ref[...], twin_ref[...], z ^ 2, core, gain_ref, router_ref, w_ref, slice(nq, n)
    )
    squares = jnp.sum(sums[:, n : n + 128] + squares, axis=1, keepdims=True)
    routed = jnp.sum(sums[:, n + 128 : n + 256] + routed, axis=1, keepdims=True)
    inverse = lax.rsqrt(squares * (1.0 / features) + NORM_EPS)
    kv = (sums[:, nq:n] + product) * inverse
    kv_out[:, 0:128] = turn(kv[:, 0:128], cos_ref[...], sin_ref[...]).astype(BF16)
    kv_out[:, 128:256] = kv[:, 128:256].astype(BF16)
    stat_out[:, 0:128] = jnp.broadcast_to(inverse, (inverse.shape[0], 128))
    gate = 1.0 / (1.0 + jnp.exp(-routed))
    stat_out[:, 128:256] = jnp.broadcast_to(gate, (gate.shape[0], 128))


def kv_last(pair, staged, sums, cos, sin, nq):
    cap = sums.shape[0]
    return call(
        functools.partial(kv_last_kernel, nq),
        "kv_last",
        (*pair, *staged, sums, cos, sin),
        [arr((cap, 256), BF16), arr((cap, 256), F32)],
    )


def attend(q, kv, bias, carry):
    k, v = kv[:, 0:128], kv[:, 128:256]
    scale = LOG2E / HEAD_SIZE**0.5
    s = lax.dot_general(k, q, (((1,), (1,)), ((), ())), preferred_element_type=F32) * scale + bias
    top = jnp.max(s, axis=0, keepdims=True)
    if carry is not None:
        top = jnp.maximum(top, carry[0])
    e = jnp.exp2(s - top)
    total = jnp.sum(e, axis=0, keepdims=True)
    mix = lax.dot_general(v, e.astype(BF16), (((0,), (0,)), ((), ())), preferred_element_type=F32)
    if carry is not None:
        fade = jnp.exp2(carry[0] - top)
        total = total + carry[1] * fade
        mix = mix + carry[2] * fade
    return top, total, mix


def q_last_kernel(mine_ref, twin_ref, gain_ref, w_ref, sums, stat_ref, cos_ref, sin_ref, kv_ref, bias_ref, *outs):
    q_out, top_ref, total_ref, mix_ref = outs
    z, core = place()
    mine, twin = mine_ref[...], twin_ref[...]
    nq, cap = q_out.shape[1], q_out.shape[0]
    product, _, _ = project(mine, twin, z ^ 2, core, gain_ref, None, w_ref, slice(0, nq), stats=False)
    q = (sums[:, 0:nq] + product) * stat_ref[:, 0:1]
    cos, sin = cos_ref[...], sin_ref[...]
    for h in range(nq // HEAD_SIZE):
        lanes = slice(h * HEAD_SIZE, (h + 1) * HEAD_SIZE)
        turned = turn(q[:, lanes], cos, sin).astype(BF16)
        q_out[:, lanes] = turned
        top, total, mix = attend(turned, kv_ref[...], bias_ref[0], None)
        at = slice(h * cap, (h + 1) * cap)
        top_ref[:, at], total_ref[:, at], mix_ref[:, at] = top, total, mix


def carry_shapes(cap, nq):
    heads = nq // HEAD_SIZE
    return [arr((1, heads * cap), F32), arr((1, heads * cap), F32), arr((HEAD_SIZE, heads * cap), F32)]


def q_last(pair, staged, sums, stat, cos, sin, kv, bias, nq):
    cap = sums.shape[0]
    return call(
        q_last_kernel,
        "q_last",
        (*pair, staged[0], staged[2], sums, stat, cos, sin, kv, bias),
        [arr((cap, nq), BF16), *carry_shapes(cap, nq)],
    )


def attend_kernel(step, last, q_ref, kv_ref, bias_ref, top_in, total_in, mix_in, *outs):
    cap, nq = q_ref.shape
    for h in range(nq // HEAD_SIZE):
        lanes = slice(h * HEAD_SIZE, (h + 1) * HEAD_SIZE)
        at = slice(h * cap, (h + 1) * cap)
        carry = (top_in[:, at], total_in[:, at], mix_in[:, at])
        top, total, mix = attend(q_ref[:, lanes], kv_ref[...], bias_ref[step], carry)
        if not last:
            outs[0][:, at], outs[1][:, at], outs[2][:, at] = top, total, mix
            continue
        full, first, second = outs
        half = cap // 2
        attn = jnp.transpose(mix * (1.0 / total)).astype(BF16)
        full[:, lanes] = attn
        first[:, lanes] = attn[:half]
        second[:, lanes] = attn[half:]


def attend_more(step, last, q, kv, bias, carry):
    cap, nq = q.shape
    shapes = [arr((cap, nq), BF16), arr((cap // 2, nq), BF16), arr((cap // 2, nq), BF16)]
    return call(
        functools.partial(attend_kernel, step, last),
        "attend_more",
        (q, kv, bias, *carry),
        shapes if last else carry_shapes(cap, nq),
    )


def out_term(mine, twin, zz, core, w_ref):
    out = None
    for x, rows in halves(mine, twin, zz, core):
        out = add(out, jnp.dot(x, w_ref[rows, :], preferred_element_type=F32))
    return out


def out_own_kernel(n_mine, n_twin, *refs):
    mine, twin, refs = refs[:n_mine], refs[n_mine : n_mine + n_twin], refs[n_mine + n_twin :]
    n_ride = (len(refs) - 6) // 2
    w, hidden = refs[n_ride : n_ride + 2]
    total_ref, w_ref, hid_ref, sems = refs[-4:]
    z, core = place()
    copies = fetch([(w, w_ref), (hidden, hid_ref)], sems)
    copies[0].wait()
    total_ref[...] = out_term(joined(mine), joined(twin), z, core, w_ref)
    copies[1].wait()


def out_own(mine, twin, rides, w_out, hidden):
    cap = sum(x.shape[0] for x in mine)
    at = len(mine) + len(twin)
    return call(
        functools.partial(out_own_kernel, len(mine), len(twin)),
        "out_own",
        (*mine, *twin, *rides, w_out, hidden),
        [
            *(arr(r.shape, BF16) for r in rides),
            arr((cap, w_out.shape[1]), F32),
            arr(w_out.shape, BF16),
            arr(hidden.shape, BF16),
        ],
        scratch=[pltpu.SemaphoreType.DMA((2,))],
        rides={at + i: i for i in range(len(rides))},
        hbm=(w_out, hidden),
        flops=PART_COST,
    )


def out_more_kernel(n_mine, n_twin, flip, *refs):
    mine, twin, refs = refs[:n_mine], refs[n_mine : n_mine + n_twin], refs[n_mine + n_twin :]
    w_ref, total_in = refs[:2]
    total_out = refs[2 + (len(refs) - 3) // 2]
    z, core = place()
    total_out[...] = total_in[...] + out_term(joined(mine), joined(twin), flip(z), core, w_ref)


def out_more(mine, twin, w, total, rides, flip, flops):
    at = len(mine) + len(twin) + 1
    return call(
        functools.partial(out_more_kernel, len(mine), len(twin), flip),
        "out_more",
        (*mine, *twin, w, total, *rides),
        [arr(total.shape, F32), *(arr(r.shape, BF16) for r in rides)],
        rides={at + i: i for i in range(1 + len(rides))},
        flops=flops,
    )


def out_last_kernel(mine_ref, twin_ref, w_ref, total_ref, stat_ref, hot_ref, hid_ref, out, out_ref, sems):
    z, core = place()
    projected = total_ref[...] + out_term(mine_ref[...], twin_ref[...], z ^ 2, core, w_ref)
    update = (stat_ref[:, 128:129] * projected).astype(BF16)
    block = 256
    copies = []
    for i in range(hid_ref.shape[0] // block):
        rows = slice(i * block, (i + 1) * block)
        placed = jnp.dot(hot_ref[rows, :], update, preferred_element_type=F32)
        out_ref[rows, :] = (hid_ref[rows, :].astype(F32) + placed).astype(BF16)
        copies += fetch([(out_ref.at[rows, :], out.at[rows, :])], sems, i)
    settle(copies)


def out_last(pair, w, total, stat, hot, hidden):
    return call(
        out_last_kernel,
        "out_last",
        (*pair, w, total, stat, hot, hidden),
        [arr(hidden.shape, BF16)],
        scratch=[pltpu.VMEM(hidden.shape, BF16), pltpu.SemaphoreType.DMA((hidden.shape[0] // 256,))],
        out_hbm=True,
    )[0]


def angles(row_pos):
    half = HEAD_SIZE // 2
    frequency = ROPE_BASE ** (-(jnp.arange(half, dtype=F32) * 2.0 / HEAD_SIZE))
    turned = row_pos.astype(F32) * jnp.concatenate([frequency, frequency])[None, :]
    sign = jnp.concatenate([-jnp.ones((half,), F32), jnp.ones((half,), F32)])
    return jnp.cos(turned), jnp.sin(turned) * sign[None, :]


def body(
    size,
    hidden_in,
    norm_gain,
    router_weight,
    w_query,
    w_key,
    value_weight,
    w_out,
    keep_flags,
    keep_counts,
    keep_positions,
):
    shards = lax.axis_size("ctx")
    tok = hidden_in.shape[0]
    nq = w_query.shape[1]
    flags = keep_flags.reshape(-1, 128)
    weights = (norm_gain.reshape(1, -1), router_weight.reshape(1, -1), w_query, w_key, value_weight)

    full, first, second, rowpos = pick(keep_counts, keep_positions, hidden_in)
    cos, sin = angles(rowpos)
    held = {}

    def own(mine, twin, rides):
        *rides, held["sums"], held["bias"], held["hot"], g, r, w = own_part(
            mine, twin, rides, weights, keep_counts, keep_positions, flags, tok
        )
        held["staged"] = (g, r, w)
        return rides

    def far(mine, twin, rides):
        held["sums"], *rides = more_part(
            mine, twin, held["staged"], held["sums"], rides, lambda z: 3 - z, PART_COST
        )
        return rides

    def beside(mine, twin):
        (held["sums"],) = more_part(mine, twin, held["staged"], held["sums"], (), lambda z: z ^ 1, PART_COST)

    pair = spread(size, full, first, second, own, far, beside)
    sums, staged, bias = held["sums"], held["staged"], held["bias"]
    kv, stat = kv_last(pair, staged, sums, cos, sin, nq)
    ring = [(s, (s + 1) % shards) for s in range(shards)]
    moved = lax.ppermute(kv, "ctx", ring)
    q, *carry = q_last(pair, staged, sums, stat, cos, sin, kv, bias, nq)
    for step in range(1, shards):
        last = step == shards - 1
        carry = attend_more(step, last, q, moved, bias, carry)
        if not last:
            moved = lax.ppermute(moved, "ctx", ring)

    def own_out(mine, twin, rides):
        *rides, held["total"], held["w"], held["hidden"] = out_own(mine, twin, rides, w_out, hidden_in)
        return rides

    def far_out(mine, twin, rides):
        held["total"], *rides = out_more(mine, twin, held["w"], held["total"], rides, lambda z: 3 - z, PART_COST)
        return rides

    def beside_out(mine, twin):
        (held["total"],) = out_more(mine, twin, held["w"], held["total"], (), lambda z: z ^ 1, PART_COST)

    pair = spread(size, *carry, own_out, far_out, beside_out)
    return out_last(pair, held["w"], held["total"], stat, held["hot"], held["hidden"])


def solution(mesh):
    in_specs = (
        P(("groups", "ctx"), "heads"),
        P(),
        P(),
        P(None, "heads"),
        P(None, "heads"),
        P(None, "heads"),
        P(None, "heads"),
        P(("groups", "ctx")),
        P("groups"),
        P("groups", None),
    )
    out_specs = P(("groups", "ctx"), "heads")
    return jax.shard_map(
        functools.partial(body, mesh.shape["heads"]),
        mesh=mesh,
        in_specs=in_specs,
        out_specs=out_specs,
        check_vma=False,
    )
```

```python
import functools

import jax
import jax.numpy as jnp
from jax import lax
from jax.experimental import pallas as pl
from jax.experimental.pallas import tpu as pltpu
from jax.sharding import PartitionSpec as P

HEAD_SIZE = 128
ROPE_BASE = 500000.0
NORM_EPS = 1e-05
LOG2E = 1.4426950408889634
VMEM_LIMIT = 24 * 1024 * 1024
F32 = jnp.float32
BF16 = jnp.bfloat16
I32 = jnp.int32
COST = 400_000_000
PART_COST = 1_500_000_000
OWN_COST = 400_000_000
FAR_COST = 1_500_000_000
BESIDE_COST = 1_000_000
KV_COST = 400_000_000
Q_COST = 400_000_000
QA_COST = 1_500_000_000
ATTEND_COST = 400_000_000


VMEM = pl.BlockSpec(memory_space=pltpu.VMEM)
HBM = pl.BlockSpec(memory_space=pltpu.HBM)


def arr(shape, dtype):
    return jax.ShapeDtypeStruct(shape, dtype)


def call(kernel, name, operands, out_shape, scratch=(), rides=None, hbm=(), out_hbm=False, flops=COST):
    operands = [(o, any(o is h for h in hbm)) for o in operands]
    return pl.pallas_call(
        kernel,
        out_shape=out_shape,
        in_specs=[HBM if far else VMEM for _, far in operands],
        out_specs=[HBM if out_hbm else VMEM] * len(out_shape),
        scratch_shapes=list(scratch),
        input_output_aliases=rides or {},
        compiler_params=pltpu.CompilerParams(vmem_limit_bytes=VMEM_LIMIT),
        cost_estimate=pl.CostEstimate(flops=flops, bytes_accessed=1, transcendentals=0),
        name=name,
    )(*(pltpu.with_memory_space_constraint(o, pltpu.HBM) if far else o for o, far in operands))


def fetch(pairs, sems, base=0):
    copies = [pltpu.make_async_copy(src, dst, sems.at[base + i]) for i, (src, dst) in enumerate(pairs)]
    for copy in copies:
        copy.start()
    return copies


def place():
    d = lax.axis_index("heads")
    return d // 2, lax.rem(d, 2)


def live_row(pos_ref, cnt_ref, shard, dead):
    pos = pos_ref[pl.ds(shard, 1), :]
    slot = lax.broadcasted_iota(I32, pos.shape, 1)
    return jnp.where(slot < cnt_ref[shard], pos, dead)


def column(row):
    return jnp.transpose(jnp.broadcast_to(row, (128, row.shape[1])))


def pick_kernel(pos_hbm, hid_hbm, x_ref, xa_ref, xb_ref, rowpos_ref, pos_ref, hid_ref, sems):
    copies = fetch([(pos_hbm, pos_ref), (hid_hbm, hid_ref)], sems)
    own, shards = lax.axis_index("ctx"), lax.axis_size("ctx")
    tok, cap = hid_ref.shape[0], x_ref.shape[0]
    copies[0].wait()
    pos = column(pos_ref[pl.ds(own, 1), :])
    rowpos_ref[...] = jnp.where(pos < 0, shards * tok, pos)
    local = pos[:, :1] - own * tok
    hot = (lax.broadcasted_iota(I32, (cap, tok), 1) == local).astype(F32).astype(BF16)
    copies[1].wait()
    x = jnp.dot(hot, hid_ref[...], preferred_element_type=F32).astype(BF16)
    x_ref[...] = x
    xa_ref[...] = x[: cap // 2]
    xb_ref[...] = x[cap // 2 :]


def pick(positions, hidden):
    cap, width = positions.shape[1], hidden.shape[1]
    return call(
        pick_kernel,
        "pick",
        (positions, hidden),
        [arr((cap, width), BF16), arr((cap // 2, width), BF16), arr((cap // 2, width), BF16), arr((cap, 128), I32)],
        scratch=[
            pltpu.VMEM(positions.shape, I32),
            pltpu.VMEM(hidden.shape, BF16),
            pltpu.SemaphoreType.DMA((2,)),
        ],
        hbm=(positions, hidden),
    )


def sender(perm):
    return functools.partial(lax.ppermute, axis_name="heads", perm=perm)


def chip_sender(size, f):
    return sender([(2 * z + c, 2 * f(z) + c) for z in range(size // 2) for c in range(2)])


def spread(size, full, first, second, use_own, use_far, use_beside):
    cross = chip_sender(size, lambda z: 3 - z)
    near = chip_sender(size, lambda z: z ^ 1)
    twin = sender([(d, d ^ 1) for d in range(size)])
    far = cross(full)
    mates = twin(first), twin(second)
    beside = near(first), near(second)
    last = near(far)
    beside = use_own((full,), mates, beside)
    beside = use_far((far,), (twin(far),), beside)
    use_beside(beside, (twin(beside[0]), twin(beside[1])))
    return last, twin(last)


def spread_halves(size, full, first, second, use_own, use_far, use_beside):
    cross = chip_sender(size, lambda z: 3 - z)
    near = chip_sender(size, lambda z: z ^ 1)
    twin = sender([(d, d ^ 1) for d in range(size)])
    far = cross(first), cross(second)
    beside = near(use_own((full,), (twin(full),), full))
    last_a, last_b = near(far[0]), near(far[1])
    (last_a,) = use_far(far, (twin(far[0]), twin(far[1])), (last_a,))
    use_beside((beside,), (twin(beside),))
    return (last_a, twin(last_a)), (last_b, twin(last_b))


def joined(refs):
    parts = [ref[...] for ref in refs]
    return parts[0] if len(parts) == 1 else jnp.concatenate(parts, axis=0)


def lanes_sum(x):
    total = x[:, :128]
    for at in range(128, x.shape[1], 128):
        total = total + x[:, at : at + 128]
    return total


def halves(mine, twin, zz, core):
    width = mine.shape[1]
    rows = [pl.ds(pl.multiple_of((2 * zz + at) * width, width), width) for at in (core, 1 - core)]
    return zip((mine, twin), rows)


def add(a, b):
    return b if a is None else a + b


def project(mine, twin, zz, core, gain_ref, router_ref, w_ref, columns, stats=True):
    product = squares = routed = None
    for x, rows in halves(mine, twin, zz, core):
        xf = x.astype(F32)
        gained = (xf * gain_ref[:, rows]).astype(BF16)
        product = add(product, jnp.dot(gained, w_ref[rows, columns], preferred_element_type=F32))
        if stats:
            squares = add(squares, lanes_sum(xf * xf))
            routed = add(routed, lanes_sum(xf * router_ref[:, rows]))
    return product, squares, routed


def settle(copies):
    for copy in copies:
        copy.wait()


def own_kernel(x_ref, twin_ref, gain, router, wq, wk, wv, _, sums_ref, gain_ref, router_ref, w_ref, sems):
    z, core = place()
    nq, nk, depth = wq.shape[1], wk.shape[1], wq.shape[0]
    lanes = ((wq, slice(0, nq)), (wk, slice(nq, nq + nk)), (wv, slice(nq + nk, nq + 2 * nk)))
    block = 2 * x_ref.shape[1]
    blocks = depth // block
    vectors = fetch([(gain, gain_ref), (router, router_ref)], sems, 3 * blocks)
    copies = []
    for i in range(blocks):
        rows = pl.ds(pl.multiple_of((z ^ i) * block, block), block)
        copies.append(fetch([(w.at[rows, :], w_ref.at[rows, at]) for w, at in lanes], sems, 3 * i))
    settle(vectors)
    settle(copies[0])
    product, squares, routed = project(x_ref[...], twin_ref[...], z, core, gain_ref, router_ref, w_ref, slice(None))
    n = product.shape[1]
    sums_ref[:, 0:n] = product
    sums_ref[:, n : n + 128] = squares
    sums_ref[:, n + 128 : n + 256] = routed
    for later in copies[1:]:
        settle(later)


def own_part(full, twin, weights):
    cap, width = full.shape
    depth = weights[2].shape[0]
    columns = sum(w.shape[1] for w in weights[2:])
    return call(
        own_kernel,
        "own_part",
        (full, twin, *weights),
        [
            arr(full.shape, BF16),
            arr((cap, columns + 256), F32),
            arr((1, depth), F32),
            arr((1, depth), F32),
            arr((depth, columns), BF16),
        ],
        scratch=[pltpu.SemaphoreType.DMA((3 * depth // (2 * width) + 2,))],
        rides={0: 0},
        hbm=weights,
        flops=OWN_COST,
    )


def masks_kernel(cnt_hbm, pos_hbm, flag_hbm, bias_ref, hot_ref, cnt_ref, pos_ref, flag_ref, sems):
    settle(fetch([(cnt_hbm, cnt_ref), (pos_hbm, pos_ref), (flag_hbm, flag_ref)], sems))
    own, shards = lax.axis_index("ctx"), lax.axis_size("ctx")
    tok = hot_ref.shape[0]
    seq = shards * tok
    row = live_row(pos_ref, cnt_ref, own, seq)
    for step in range(shards):
        source = lax.rem(own + shards - step, shards)
        keys = column(live_row(pos_ref, cnt_ref, source, seq + 1))[:, :1]
        bias_ref[step] = jnp.where(keys <= row, 0.0, -jnp.inf).astype(F32)
    flags = jnp.transpose(flag_ref[...].astype(F32))
    local = row - own * tok
    for r in range(tok // 128):
        at = lax.broadcasted_iota(I32, (128, row.shape[1]), 0) + r * 128
        hot = jnp.where(at == local, flags[:, r : r + 1], 0.0)
        hot_ref[r * 128 : (r + 1) * 128, :] = hot.astype(BF16)


def more_kernel(n_mine, n_twin, n_ride, flip, masks, *refs):
    mine, twin, refs = refs[:n_mine], refs[n_mine : n_mine + n_twin], refs[n_mine + n_twin :]
    gain_ref, router_ref, w_ref, sums_in = refs[:4]
    refs = refs[4 + n_ride :]
    n_far = 3 if masks else 0
    sums_out = refs[n_far]
    z, core = place()
    product, squares, routed = project(
        joined(mine), joined(twin), flip(z), core, gain_ref, router_ref, w_ref, slice(None)
    )
    n = product.shape[1]
    sums_out[:, 0:n] = sums_in[:, 0:n] + product
    sums_out[:, n : n + 128] = sums_in[:, n : n + 128] + squares
    sums_out[:, n + 128 : n + 256] = sums_in[:, n + 128 : n + 256] + routed
    if masks:
        masks_kernel(*refs[:3], *refs[4 + n_ride :])


def more_part(mine, twin, staged, sums, rides, flip, flops, masks=None):
    at = len(mine) + len(twin) + 3
    shapes, scratch, far = [], [], ()
    if masks:
        *far, tok = masks
        shards, cap = far[1].shape
        shapes = [arr((shards, cap, cap), F32), arr((tok, cap), BF16)]
        scratch = [
            pltpu.SMEM(far[0].shape, I32),
            pltpu.VMEM(far[1].shape, I32),
            pltpu.VMEM(far[2].shape, I32),
            pltpu.SemaphoreType.DMA((3,)),
        ]
    return call(
        functools.partial(more_kernel, len(mine), len(twin), len(rides), flip, bool(masks)),
        "more_part",
        (*mine, *twin, *staged, sums, *rides, *far),
        [arr(sums.shape, F32), *(arr(r.shape, r.dtype) for r in rides), *shapes],
        scratch=scratch,
        rides={at + i: i for i in range(1 + len(rides))},
        hbm=far,
        flops=flops,
    )


def turn(x, cos, sin):
    return x * cos + pltpu.roll(x, HEAD_SIZE // 2, 1) * sin


def kv_last_kernel(nq, at, mine_ref, twin_ref, gain_ref, router_ref, w_ref, sums, cos_ref, sin_ref, kv_out, stat_out):
    z, core = place()
    n, features = w_ref.shape[1], w_ref.shape[0]
    rows = slice(at, at + mine_ref.shape[0])
    product, squares, routed = project(
        mine_ref[...], twin_ref[...], z ^ 2, core, gain_ref, router_ref, w_ref, slice(nq, n)
    )
    squares = jnp.sum(sums[rows, n : n + 128] + squares, axis=1, keepdims=True)
    routed = jnp.sum(sums[rows, n + 128 : n + 256] + routed, axis=1, keepdims=True)
    inverse = lax.rsqrt(squares * (1.0 / features) + NORM_EPS)
    kv = (sums[rows, nq:n] + product) * inverse
    kv_out[:, 0:128] = turn(kv[:, 0:128], cos_ref[rows, :], sin_ref[rows, :]).astype(BF16)
    kv_out[:, 128:256] = kv[:, 128:256].astype(BF16)
    stat_out[:, 0:128] = jnp.broadcast_to(inverse, (inverse.shape[0], 128))
    gate = 1.0 / (1.0 + jnp.exp(-routed))
    stat_out[:, 128:256] = jnp.broadcast_to(gate, (gate.shape[0], 128))


def kv_last(at, pair, staged, sums, cos, sin, nq, flops):
    cap = pair[0].shape[0]
    return call(
        functools.partial(kv_last_kernel, nq, at),
        "kv_last",
        (*pair, *staged, sums, cos, sin),
        [arr((cap, 256), BF16), arr((cap, 256), F32)],
        flops=flops,
    )


def attend(q, kv, bias, carry):
    k, v = kv[:, 0:128], kv[:, 128:256]
    scale = LOG2E / HEAD_SIZE**0.5
    s = lax.dot_general(k, q, (((1,), (1,)), ((), ())), preferred_element_type=F32) * scale + bias
    top = jnp.max(s, axis=0, keepdims=True)
    if carry is not None:
        top = jnp.maximum(top, carry[0])
    e = jnp.exp2(s - top)
    total = jnp.sum(e, axis=0, keepdims=True)
    mix = lax.dot_general(v, e.astype(BF16), (((0,), (0,)), ((), ())), preferred_element_type=F32)
    if carry is not None:
        fade = jnp.exp2(carry[0] - top)
        total = total + carry[1] * fade
        mix = mix + carry[2] * fade
    return top, total, mix


def q_kernel(i, n_kv, mine_ref, twin_ref, gain_ref, w_ref, sums, stat_ref, cos_ref, sin_ref, bias_ref, *refs):
    kv_refs, (q_out, top_ref, total_ref, mix_ref) = refs[:n_kv], refs[n_kv:]
    z, core = place()
    half, nq = q_out.shape
    rows, keys = slice(i * half, (i + 1) * half), slice(0, (i + 1) * half)
    product, _, _ = project(
        mine_ref[...], twin_ref[...], z ^ 2, core, gain_ref, None, w_ref, slice(0, nq), stats=False
    )
    q = (sums[rows, 0:nq] + product) * stat_ref[:, 0:1]
    cos, sin, kv = cos_ref[rows, :], sin_ref[rows, :], joined(kv_refs)
    for h in range(nq // HEAD_SIZE):
        lanes = slice(h * HEAD_SIZE, (h + 1) * HEAD_SIZE)
        turned = turn(q[:, lanes], cos, sin).astype(BF16)
        q_out[:, lanes] = turned
        top, total, mix = attend(turned, kv, bias_ref[0, keys, rows], None)
        at = slice(h * half, (h + 1) * half)
        top_ref[:, at], total_ref[:, at], mix_ref[:, at] = top, total, mix


def carry_shapes(cap, nq):
    heads = nq // HEAD_SIZE
    return [arr((1, heads * cap), F32), arr((1, heads * cap), F32), arr((HEAD_SIZE, heads * cap), F32)]


def q_part(i, pair, staged, sums, stat, cos, sin, kvs, bias, nq, flops):
    half = pair[0].shape[0]
    return call(
        functools.partial(q_kernel, i, len(kvs)),
        "q_part",
        (*pair, staged[0], staged[2], sums, stat, cos, sin, bias, *kvs),
        [arr((half, nq), BF16), *carry_shapes(half, nq)],
        flops=flops,
    )


def attend_kernel(step, first_key, n_carry, last, qa_ref, qb_ref, kv_ref, bias_ref, *refs):
    carries, outs = refs[: 3 * n_carry], refs[3 * n_carry :]
    half, nq = qa_ref.shape
    cap = 2 * half
    keys = slice(first_key, first_key + kv_ref.shape[0])
    for h in range(nq // HEAD_SIZE):
        lanes = slice(h * HEAD_SIZE, (h + 1) * HEAD_SIZE)
        at = slice(h * cap, (h + 1) * cap)
        part = slice(h * cap // n_carry, (h + 1) * cap // n_carry)
        carry = [
            jnp.concatenate([carries[j][:, part] for j in range(k, 3 * n_carry, 3)], axis=1) for k in range(3)
        ]
        q = jnp.concatenate([qa_ref[:, lanes], qb_ref[:, lanes]], axis=0)
        top, total, mix = attend(q, kv_ref[...], bias_ref[step, keys, :], carry)
        if not last:
            outs[0][:, at], outs[1][:, at], outs[2][:, at] = top, total, mix
            continue
        full, first, second = outs
        attn = jnp.transpose(mix * (1.0 / total)).astype(BF16)
        full[:, lanes] = attn
        first[:, lanes] = attn[:half]
        second[:, lanes] = attn[half:]


def attend_more(step, first_key, last, qs, kv, bias, carry, flops):
    half, nq = qs[0].shape
    cap = 2 * half
    shapes = [arr((cap, nq), BF16), arr((half, nq), BF16), arr((half, nq), BF16)]
    return call(
        functools.partial(attend_kernel, step, first_key, len(carry) // 3, last),
        "attend_more",
        (*qs, kv, bias, *carry),
        shapes if last else carry_shapes(cap, nq),
        flops=flops,
    )


def out_term(mine, twin, zz, core, w_ref):
    out = None
    for x, rows in halves(mine, twin, zz, core):
        out = add(out, jnp.dot(x, w_ref[rows, :], preferred_element_type=F32))
    return out


def out_own_kernel(n_mine, n_twin, *refs):
    mine, twin, refs = refs[:n_mine], refs[n_mine : n_mine + n_twin], refs[n_mine + n_twin :]
    n_ride = (len(refs) - 6) // 2
    w, hidden = refs[n_ride : n_ride + 2]
    total_ref, w_ref, hid_ref, sems = refs[-4:]
    z, core = place()
    copies = fetch([(w, w_ref), (hidden, hid_ref)], sems)
    copies[0].wait()
    total_ref[...] = out_term(joined(mine), joined(twin), z, core, w_ref)
    copies[1].wait()


def out_own(mine, twin, rides, w_out, hidden):
    cap = sum(x.shape[0] for x in mine)
    at = len(mine) + len(twin)
    return call(
        functools.partial(out_own_kernel, len(mine), len(twin)),
        "out_own",
        (*mine, *twin, *rides, w_out, hidden),
        [
            *(arr(r.shape, r.dtype) for r in rides),
            arr((cap, w_out.shape[1]), F32),
            arr(w_out.shape, BF16),
            arr(hidden.shape, BF16),
        ],
        scratch=[pltpu.SemaphoreType.DMA((2,))],
        rides={at + i: i for i in range(len(rides))},
        hbm=(w_out, hidden),
        flops=PART_COST,
    )


def out_more_kernel(n_mine, n_twin, flip, *refs):
    mine, twin, refs = refs[:n_mine], refs[n_mine : n_mine + n_twin], refs[n_mine + n_twin :]
    w_ref, total_in = refs[:2]
    total_out = refs[2 + (len(refs) - 3) // 2]
    z, core = place()
    total_out[...] = total_in[...] + out_term(joined(mine), joined(twin), flip(z), core, w_ref)


def out_more(mine, twin, w, total, rides, flip, flops):
    at = len(mine) + len(twin) + 1
    return call(
        functools.partial(out_more_kernel, len(mine), len(twin), flip),
        "out_more",
        (*mine, *twin, w, total, *rides),
        [arr(total.shape, F32), *(arr(r.shape, r.dtype) for r in rides)],
        rides={at + i: i for i in range(1 + len(rides))},
        flops=flops,
    )


def out_last_kernel(mine_ref, twin_ref, w_ref, total_ref, sa_ref, sb_ref, hot_ref, hid_ref, out, out_ref, sems):
    z, core = place()
    projected = total_ref[...] + out_term(mine_ref[...], twin_ref[...], z ^ 2, core, w_ref)
    gate = jnp.concatenate([sa_ref[:, 128:129], sb_ref[:, 128:129]], axis=0)
    update = (gate * projected).astype(BF16)
    block = 256
    copies = []
    for i in range(hid_ref.shape[0] // block):
        rows = slice(i * block, (i + 1) * block)
        placed = jnp.dot(hot_ref[rows, :], update, preferred_element_type=F32)
        out_ref[rows, :] = (hid_ref[rows, :].astype(F32) + placed).astype(BF16)
        copies += fetch([(out_ref.at[rows, :], out.at[rows, :])], sems, i)
    settle(copies)


def out_last(pair, w, total, stats, hot, hidden):
    return call(
        out_last_kernel,
        "out_last",
        (*pair, w, total, *stats, hot, hidden),
        [arr(hidden.shape, BF16)],
        scratch=[pltpu.VMEM(hidden.shape, BF16), pltpu.SemaphoreType.DMA((hidden.shape[0] // 256,))],
        out_hbm=True,
    )[0]


def angles(row_pos):
    half = HEAD_SIZE // 2
    frequency = ROPE_BASE ** (-(jnp.arange(half, dtype=F32) * 2.0 / HEAD_SIZE))
    turned = row_pos.astype(F32) * jnp.concatenate([frequency, frequency])[None, :]
    sign = jnp.concatenate([-jnp.ones((half,), F32), jnp.ones((half,), F32)])
    return jnp.cos(turned), jnp.sin(turned) * sign[None, :]


def body(
    size,
    hidden_in,
    norm_gain,
    router_weight,
    w_query,
    w_key,
    value_weight,
    w_out,
    keep_flags,
    keep_counts,
    keep_positions,
):
    shards = lax.axis_size("ctx")
    tok = hidden_in.shape[0]
    nq = w_query.shape[1]
    flags = keep_flags.reshape(-1, 128)
    weights = (norm_gain.reshape(1, -1), router_weight.reshape(1, -1), w_query, w_key, value_weight)

    full, first, second, rowpos = pick(keep_positions, hidden_in)
    held = {}

    def own(mine, twin, _):
        ride, held["sums"], *held["staged"] = own_part(*mine, *twin, weights)
        return ride

    def far(mine, twin, rides):
        held["sums"], ride, held["cos"], held["sin"], held["bias"], held["hot"] = more_part(
            mine,
            twin,
            held["staged"],
            held["sums"],
            (*rides, *angles(rowpos)),
            lambda z: 3 - z,
            FAR_COST,
            (keep_counts, keep_positions, flags, tok),
        )
        return (ride,)

    def beside(mine, twin):
        (held["sums"],) = more_part(mine, twin, held["staged"], held["sums"], (), lambda z: z ^ 1, BESIDE_COST)

    pairs = spread_halves(size, full, first, second, own, far, beside)
    sums, staged, bias = held["sums"], held["staged"], held["bias"]
    cos, sin = held["cos"], held["sin"]
    half = first.shape[0]
    ring = [(s, (s + 1) % shards) for s in range(shards)]
    kvs, stats, moved, qs, carry = [], [], [], [], []
    for i in range(2):
        kv, stat = kv_last(i * half, pairs[i], staged, sums, cos, sin, nq, KV_COST)
        kvs.append(kv)
        stats.append(stat)
        moved.append(lax.ppermute(kv, "ctx", ring))
        q, *terms = q_part(i, pairs[i], staged, sums, stat, cos, sin, kvs, bias, nq, QA_COST if i == 0 else Q_COST)
        qs.append(q)
        carry += terms
    for step in range(1, shards):
        for i in range(2):
            last = step == shards - 1 and i == 1
            carry = attend_more(step, i * half, last, qs, moved[i], bias, carry, ATTEND_COST)
        if step < shards - 1:
            moved = [lax.ppermute(kv, "ctx", ring) for kv in moved]

    def own_out(mine, twin, rides):
        *rides, held["total"], held["w"], held["hidden"] = out_own(mine, twin, rides, w_out, hidden_in)
        return rides

    def far_out(mine, twin, rides):
        held["total"], *rides = out_more(mine, twin, held["w"], held["total"], rides, lambda z: 3 - z, PART_COST)
        return rides

    def beside_out(mine, twin):
        (held["total"],) = out_more(mine, twin, held["w"], held["total"], (), lambda z: z ^ 1, PART_COST)

    pair = spread(size, *carry, own_out, far_out, beside_out)
    return out_last(pair, held["w"], held["total"], stats, held["hot"], held["hidden"])


def solution(mesh):
    in_specs = (
        P(("groups", "ctx"), "heads"),
        P(),
        P(),
        P(None, "heads"),
        P(None, "heads"),
        P(None, "heads"),
        P(None, "heads"),
        P(("groups", "ctx")),
        P("groups"),
        P("groups", None),
    )
    out_specs = P(("groups", "ctx"), "heads")
    return jax.shard_map(
        functools.partial(body, mesh.shape["heads"]),
        mesh=mesh,
        in_specs=in_specs,
        out_specs=out_specs,
        check_vma=False,
    )
```

```python
import functools

import jax
import jax.numpy as jnp
from jax import lax
from jax.experimental import pallas as pl
from jax.experimental.pallas import tpu as pltpu
from jax.sharding import PartitionSpec as P

HEAD_SIZE = 128
ROPE_BASE = 500000.0
NORM_EPS = 1e-05
LOG2E = 1.4426950408889634
VMEM_LIMIT = 24 * 1024 * 1024
F32 = jnp.float32
BF16 = jnp.bfloat16
I32 = jnp.int32
COST = 400_000_000
PART_COST = 1_500_000_000
OWN_COST = 1_500_000_000
GATE_COST = 1_000_000
FAR_COST = 1_500_000_000
BESIDE_COST = 1_000_000
KV_COST = 400_000_000
Q_COST = 400_000_000
QA_COST = 1_500_000_000
ATTEND_COST = 400_000_000


VMEM = pl.BlockSpec(memory_space=pltpu.VMEM)
HBM = pl.BlockSpec(memory_space=pltpu.HBM)


def arr(shape, dtype):
    return jax.ShapeDtypeStruct(shape, dtype)


def call(kernel, name, operands, out_shape, scratch=(), rides=None, hbm=(), out_hbm=False, flops=COST):
    operands = [(o, any(o is h for h in hbm)) for o in operands]
    return pl.pallas_call(
        kernel,
        out_shape=out_shape,
        in_specs=[HBM if far else VMEM for _, far in operands],
        out_specs=[HBM if out_hbm else VMEM] * len(out_shape),
        scratch_shapes=list(scratch),
        input_output_aliases=rides or {},
        compiler_params=pltpu.CompilerParams(vmem_limit_bytes=VMEM_LIMIT),
        cost_estimate=pl.CostEstimate(flops=flops, bytes_accessed=1, transcendentals=0),
        name=name,
    )(*(pltpu.with_memory_space_constraint(o, pltpu.HBM) if far else o for o, far in operands))


def fetch(pairs, sems, base=0):
    copies = [pltpu.make_async_copy(src, dst, sems.at[base + i]) for i, (src, dst) in enumerate(pairs)]
    for copy in copies:
        copy.start()
    return copies


def place():
    d = lax.axis_index("heads")
    return d // 2, lax.rem(d, 2)


def live_row(pos_ref, cnt_ref, shard, dead):
    pos = pos_ref[pl.ds(shard, 1), :]
    slot = lax.broadcasted_iota(I32, pos.shape, 1)
    return jnp.where(slot < cnt_ref[shard], pos, dead)


def column(row):
    return jnp.transpose(jnp.broadcast_to(row, (128, row.shape[1])))


def pick_kernel(pos_hbm, hid_hbm, x_ref, xa_ref, xb_ref, rowpos_ref, pos_ref, hid_ref, sems):
    own, shards = lax.axis_index("ctx"), lax.axis_size("ctx")
    tok, cap = hid_ref.shape[0], x_ref.shape[0]
    pieces = [slice(at, at + 256) for at in range(0, tok, 256)]
    copies = fetch([(pos_hbm, pos_ref), *((hid_hbm.at[p, :], hid_ref.at[p, :]) for p in pieces)], sems)
    copies[0].wait()
    pos = column(pos_ref[pl.ds(own, 1), :])
    rowpos_ref[...] = jnp.where(pos < 0, shards * tok, pos)
    local = pos[:, :1] - own * tok
    total = None
    for piece, copy in zip(pieces, copies[1:]):
        at = lax.broadcasted_iota(I32, (cap, 256), 1) + piece.start
        hot = jnp.where(at == local, 1.0, 0.0).astype(BF16)
        copy.wait()
        total = add(total, jnp.dot(hot, hid_ref[piece, :], preferred_element_type=F32))
    x = total.astype(BF16)
    x_ref[...] = x
    xa_ref[...] = x[: cap // 2]
    xb_ref[...] = x[cap // 2 :]


def pick(positions, hidden):
    cap, width = positions.shape[1], hidden.shape[1]
    return call(
        pick_kernel,
        "pick",
        (positions, hidden),
        [arr((cap, width), BF16), arr((cap // 2, width), BF16), arr((cap // 2, width), BF16), arr((cap, 128), I32)],
        scratch=[
            pltpu.VMEM(positions.shape, I32),
            pltpu.VMEM(hidden.shape, BF16),
            pltpu.SemaphoreType.DMA((1 + hidden.shape[0] // 256,)),
        ],
        hbm=(positions, hidden),
    )


def sender(perm):
    return functools.partial(lax.ppermute, axis_name="heads", perm=perm)


def chip_sender(size, f):
    return sender([(2 * z + c, 2 * f(z) + c) for z in range(size // 2) for c in range(2)])


def gate(ride, other):
    return call(lambda *_: None, "gate", (ride, other), [arr(ride.shape, ride.dtype)], rides={0: 0}, flops=GATE_COST)[0]


def spread(size, full, first, second, use_own, use_far, use_beside):
    cross = chip_sender(size, lambda z: 3 - z)
    near = chip_sender(size, lambda z: z ^ 1)
    twin = sender([(d, d ^ 1) for d in range(size)])
    far = cross(full)
    mates = twin(first), twin(second)
    beside = near(first), near(second)
    last = near(far)
    beside = use_own((full,), mates, beside)
    beside = use_far((far,), (twin(far),), beside)
    use_beside(beside, (twin(beside[0]), twin(beside[1])))
    return last, twin(last)


def spread_halves(size, full, first, second, use_own, use_far, use_beside):
    cross = chip_sender(size, lambda z: 3 - z)
    near = chip_sender(size, lambda z: z ^ 1)
    twin = sender([(d, d ^ 1) for d in range(size)])
    far = cross(first), cross(second)
    mate = twin(full)
    full = gate(full, mate)
    beside = use_own((full,), (mate,), near(full))
    last_a, last_b = near(far[0]), near(far[1])
    (last_a,) = use_far(far, (twin(far[0]), twin(far[1])), (last_a,))
    use_beside((beside,), (twin(beside),))
    return (last_a, twin(last_a)), (last_b, twin(last_b))


def joined(refs):
    parts = [ref[...] for ref in refs]
    return parts[0] if len(parts) == 1 else jnp.concatenate(parts, axis=0)


def lanes_sum(x):
    total = x[:, :128]
    for at in range(128, x.shape[1], 128):
        total = total + x[:, at : at + 128]
    return total


def halves(mine, twin, zz, core):
    width = mine.shape[1]
    rows = [pl.ds(pl.multiple_of((2 * zz + at) * width, width), width) for at in (core, 1 - core)]
    return zip((mine, twin), rows)


def add(a, b):
    return b if a is None else a + b


def project(mine, twin, zz, core, gain_ref, router_ref, w_ref, columns, stats=True):
    product = squares = routed = None
    for x, rows in halves(mine, twin, zz, core):
        xf = x.astype(F32)
        gained = (xf * gain_ref[:, rows]).astype(BF16)
        product = add(product, jnp.dot(gained, w_ref[rows, columns], preferred_element_type=F32))
        if stats:
            squares = add(squares, lanes_sum(xf * xf))
            routed = add(routed, lanes_sum(xf * router_ref[:, rows]))
    return product, squares, routed


def settle(copies):
    for copy in copies:
        copy.wait()


def own_kernel(x_ref, twin_ref, _, gain, router, wq, wk, wv, cnt, pos, flag, *refs):
    _, sums_ref, gain_ref, router_ref, w_ref, bias_ref, hot_ref, sems = refs[:8]
    z, core = place()
    nq, nk, depth = wq.shape[1], wk.shape[1], wq.shape[0]
    lanes = ((wq, slice(0, nq)), (wk, slice(nq, nq + nk)), (wv, slice(nq + nk, nq + 2 * nk)))
    block = 2 * x_ref.shape[1]
    blocks = depth // block
    vectors = fetch([(gain, gain_ref), (router, router_ref)], sems, 3 * blocks)
    copies = []
    for i in range(blocks):
        rows = pl.ds(pl.multiple_of((z ^ i) * block, block), block)
        copies.append(fetch([(w.at[rows, :], w_ref.at[rows, at]) for w, at in lanes], sems, 3 * i))
    settle(vectors)
    settle(copies[0])
    product, squares, routed = project(x_ref[...], twin_ref[...], z, core, gain_ref, router_ref, w_ref, slice(None))
    n = product.shape[1]
    sums_ref[:, 0:n] = product
    sums_ref[:, n : n + 128] = squares
    sums_ref[:, n + 128 : n + 256] = routed
    masks_kernel(cnt, pos, flag, bias_ref, hot_ref, *refs[8:])
    for later in copies[1:]:
        settle(later)


def own_part(full, twin, ride, weights, counts, positions, flags, tok):
    cap, width = full.shape
    depth = weights[2].shape[0]
    columns = sum(w.shape[1] for w in weights[2:])
    shards = positions.shape[0]
    return call(
        own_kernel,
        "own_part",
        (full, twin, ride, *weights, counts, positions, flags),
        [
            arr(ride.shape, BF16),
            arr((cap, columns + 256), F32),
            arr((1, depth), F32),
            arr((1, depth), F32),
            arr((depth, columns), BF16),
            arr((shards, cap, cap), F32),
            arr((tok, cap), BF16),
        ],
        scratch=[
            pltpu.SemaphoreType.DMA((3 * depth // (2 * width) + 2,)),
            pltpu.SMEM(counts.shape, I32),
            pltpu.VMEM(positions.shape, I32),
            pltpu.VMEM(flags.shape, I32),
            pltpu.SemaphoreType.DMA((3,)),
        ],
        rides={2: 0},
        hbm=(*weights, counts, positions, flags),
        flops=OWN_COST,
    )


def masks_kernel(cnt_hbm, pos_hbm, flag_hbm, bias_ref, hot_ref, cnt_ref, pos_ref, flag_ref, sems):
    settle(fetch([(cnt_hbm, cnt_ref), (pos_hbm, pos_ref), (flag_hbm, flag_ref)], sems))
    own, shards = lax.axis_index("ctx"), lax.axis_size("ctx")
    tok = hot_ref.shape[0]
    seq = shards * tok
    row = live_row(pos_ref, cnt_ref, own, seq)
    for step in range(shards):
        source = lax.rem(own + shards - step, shards)
        keys = column(live_row(pos_ref, cnt_ref, source, seq + 1))[:, :1]
        bias_ref[step] = jnp.where(keys <= row, 0.0, -jnp.inf).astype(F32)
    flags = jnp.transpose(flag_ref[...].astype(F32))
    local = row - own * tok
    for r in range(tok // 128):
        at = lax.broadcasted_iota(I32, (128, row.shape[1]), 0) + r * 128
        hot = jnp.where(at == local, flags[:, r : r + 1], 0.0)
        hot_ref[r * 128 : (r + 1) * 128, :] = hot.astype(BF16)


def more_kernel(n_mine, n_twin, n_ride, flip, *refs):
    mine, twin, refs = refs[:n_mine], refs[n_mine : n_mine + n_twin], refs[n_mine + n_twin :]
    gain_ref, router_ref, w_ref, sums_in = refs[:4]
    sums_out = refs[4 + n_ride]
    z, core = place()
    product, squares, routed = project(
        joined(mine), joined(twin), flip(z), core, gain_ref, router_ref, w_ref, slice(None)
    )
    n = product.shape[1]
    sums_out[:, 0:n] = sums_in[:, 0:n] + product
    sums_out[:, n : n + 128] = sums_in[:, n : n + 128] + squares
    sums_out[:, n + 128 : n + 256] = sums_in[:, n + 128 : n + 256] + routed


def more_part(mine, twin, staged, sums, rides, flip, flops):
    at = len(mine) + len(twin) + 3
    return call(
        functools.partial(more_kernel, len(mine), len(twin), len(rides), flip),
        "more_part",
        (*mine, *twin, *staged, sums, *rides),
        [arr(sums.shape, F32), *(arr(r.shape, r.dtype) for r in rides)],
        rides={at + i: i for i in range(1 + len(rides))},
        flops=flops,
    )


def turn(x, cos, sin):
    return x * cos + pltpu.roll(x, HEAD_SIZE // 2, 1) * sin


def kv_last_kernel(nq, at, mine_ref, twin_ref, gain_ref, router_ref, w_ref, sums, cos_ref, sin_ref, kv_out, stat_out):
    z, core = place()
    n, features = w_ref.shape[1], w_ref.shape[0]
    rows = slice(at, at + mine_ref.shape[0])
    product, squares, routed = project(
        mine_ref[...], twin_ref[...], z ^ 2, core, gain_ref, router_ref, w_ref, slice(nq, n)
    )
    squares = jnp.sum(sums[rows, n : n + 128] + squares, axis=1, keepdims=True)
    routed = jnp.sum(sums[rows, n + 128 : n + 256] + routed, axis=1, keepdims=True)
    inverse = lax.rsqrt(squares * (1.0 / features) + NORM_EPS)
    kv = (sums[rows, nq:n] + product) * inverse
    kv_out[:, 0:128] = turn(kv[:, 0:128], cos_ref[rows, :], sin_ref[rows, :]).astype(BF16)
    kv_out[:, 128:256] = kv[:, 128:256].astype(BF16)
    stat_out[:, 0:128] = jnp.broadcast_to(inverse, (inverse.shape[0], 128))
    gate = 1.0 / (1.0 + jnp.exp(-routed))
    stat_out[:, 128:256] = jnp.broadcast_to(gate, (gate.shape[0], 128))


def kv_last(at, pair, staged, sums, cos, sin, nq, flops):
    cap = pair[0].shape[0]
    return call(
        functools.partial(kv_last_kernel, nq, at),
        "kv_last",
        (*pair, *staged, sums, cos, sin),
        [arr((cap, 256), BF16), arr((cap, 256), F32)],
        flops=flops,
    )


def attend(q, kv, bias, carry):
    k, v = kv[:, 0:128], kv[:, 128:256]
    scale = LOG2E / HEAD_SIZE**0.5
    s = lax.dot_general(k, q, (((1,), (1,)), ((), ())), preferred_element_type=F32) * scale + bias
    top = jnp.max(s, axis=0, keepdims=True)
    if carry is not None:
        top = jnp.maximum(top, carry[0])
    e = jnp.exp2(s - top)
    total = jnp.sum(e, axis=0, keepdims=True)
    mix = lax.dot_general(v, e.astype(BF16), (((0,), (0,)), ((), ())), preferred_element_type=F32)
    if carry is not None:
        fade = jnp.exp2(carry[0] - top)
        total = total + carry[1] * fade
        mix = mix + carry[2] * fade
    return top, total, mix


def q_kernel(i, n_kv, mine_ref, twin_ref, gain_ref, w_ref, sums, stat_ref, cos_ref, sin_ref, bias_ref, *refs):
    kv_refs, (q_out, top_ref, total_ref, mix_ref) = refs[:n_kv], refs[n_kv:]
    z, core = place()
    half, nq = q_out.shape
    rows, keys = slice(i * half, (i + 1) * half), slice(0, (i + 1) * half)
    product, _, _ = project(
        mine_ref[...], twin_ref[...], z ^ 2, core, gain_ref, None, w_ref, slice(0, nq), stats=False
    )
    q = (sums[rows, 0:nq] + product) * stat_ref[:, 0:1]
    cos, sin, kv = cos_ref[rows, :], sin_ref[rows, :], joined(kv_refs)
    for h in range(nq // HEAD_SIZE):
        lanes = slice(h * HEAD_SIZE, (h + 1) * HEAD_SIZE)
        turned = turn(q[:, lanes], cos, sin).astype(BF16)
        q_out[:, lanes] = turned
        top, total, mix = attend(turned, kv, bias_ref[0, keys, rows], None)
        at = slice(h * half, (h + 1) * half)
        top_ref[:, at], total_ref[:, at], mix_ref[:, at] = top, total, mix


def carry_shapes(cap, nq):
    heads = nq // HEAD_SIZE
    return [arr((1, heads * cap), F32), arr((1, heads * cap), F32), arr((HEAD_SIZE, heads * cap), F32)]


def q_part(i, pair, staged, sums, stat, cos, sin, kvs, bias, nq, flops):
    half = pair[0].shape[0]
    return call(
        functools.partial(q_kernel, i, len(kvs)),
        "q_part",
        (*pair, staged[0], staged[2], sums, stat, cos, sin, bias, *kvs),
        [arr((half, nq), BF16), *carry_shapes(half, nq)],
        flops=flops,
    )


def attend_kernel(step, first_key, n_carry, last, qa_ref, qb_ref, kv_ref, bias_ref, *refs):
    carries, outs = refs[: 3 * n_carry], refs[3 * n_carry :]
    half, nq = qa_ref.shape
    cap = 2 * half
    keys = slice(first_key, first_key + kv_ref.shape[0])
    for h in range(nq // HEAD_SIZE):
        lanes = slice(h * HEAD_SIZE, (h + 1) * HEAD_SIZE)
        at = slice(h * cap, (h + 1) * cap)
        part = slice(h * cap // n_carry, (h + 1) * cap // n_carry)
        carry = [
            jnp.concatenate([carries[j][:, part] for j in range(k, 3 * n_carry, 3)], axis=1) for k in range(3)
        ]
        q = jnp.concatenate([qa_ref[:, lanes], qb_ref[:, lanes]], axis=0)
        top, total, mix = attend(q, kv_ref[...], bias_ref[step, keys, :], carry)
        if not last:
            outs[0][:, at], outs[1][:, at], outs[2][:, at] = top, total, mix
            continue
        full, first, second = outs
        attn = jnp.transpose(mix * (1.0 / total)).astype(BF16)
        full[:, lanes] = attn
        first[:, lanes] = attn[:half]
        second[:, lanes] = attn[half:]


def attend_more(step, first_key, last, qs, kv, bias, carry, flops):
    half, nq = qs[0].shape
    cap = 2 * half
    shapes = [arr((cap, nq), BF16), arr((half, nq), BF16), arr((half, nq), BF16)]
    return call(
        functools.partial(attend_kernel, step, first_key, len(carry) // 3, last),
        "attend_more",
        (*qs, kv, bias, *carry),
        shapes if last else carry_shapes(cap, nq),
        flops=flops,
    )


def out_term(mine, twin, zz, core, w_ref):
    out = None
    for x, rows in halves(mine, twin, zz, core):
        out = add(out, jnp.dot(x, w_ref[rows, :], preferred_element_type=F32))
    return out


def out_own_kernel(n_mine, n_twin, *refs):
    mine, twin, refs = refs[:n_mine], refs[n_mine : n_mine + n_twin], refs[n_mine + n_twin :]
    n_ride = (len(refs) - 6) // 2
    w, hidden = refs[n_ride : n_ride + 2]
    total_ref, w_ref, hid_ref, sems = refs[-4:]
    z, core = place()
    copies = fetch([(w, w_ref), (hidden, hid_ref)], sems)
    copies[0].wait()
    total_ref[...] = out_term(joined(mine), joined(twin), z, core, w_ref)
    copies[1].wait()


def out_own(mine, twin, rides, w_out, hidden):
    cap = sum(x.shape[0] for x in mine)
    at = len(mine) + len(twin)
    return call(
        functools.partial(out_own_kernel, len(mine), len(twin)),
        "out_own",
        (*mine, *twin, *rides, w_out, hidden),
        [
            *(arr(r.shape, r.dtype) for r in rides),
            arr((cap, w_out.shape[1]), F32),
            arr(w_out.shape, BF16),
            arr(hidden.shape, BF16),
        ],
        scratch=[pltpu.SemaphoreType.DMA((2,))],
        rides={at + i: i for i in range(len(rides))},
        hbm=(w_out, hidden),
        flops=PART_COST,
    )


def out_more_kernel(n_mine, n_twin, flip, *refs):
    mine, twin, refs = refs[:n_mine], refs[n_mine : n_mine + n_twin], refs[n_mine + n_twin :]
    w_ref, total_in = refs[:2]
    total_out = refs[2 + (len(refs) - 3) // 2]
    z, core = place()
    total_out[...] = total_in[...] + out_term(joined(mine), joined(twin), flip(z), core, w_ref)


def out_more(mine, twin, w, total, rides, flip, flops):
    at = len(mine) + len(twin) + 1
    return call(
        functools.partial(out_more_kernel, len(mine), len(twin), flip),
        "out_more",
        (*mine, *twin, w, total, *rides),
        [arr(total.shape, F32), *(arr(r.shape, r.dtype) for r in rides)],
        rides={at + i: i for i in range(1 + len(rides))},
        flops=flops,
    )


def out_last_kernel(mine_ref, twin_ref, w_ref, total_ref, sa_ref, sb_ref, hot_ref, hid_ref, out, out_ref, sems):
    z, core = place()
    projected = total_ref[...] + out_term(mine_ref[...], twin_ref[...], z ^ 2, core, w_ref)
    gate = jnp.concatenate([sa_ref[:, 128:129], sb_ref[:, 128:129]], axis=0)
    update = (gate * projected).astype(BF16)
    block = 256
    copies = []
    for i in range(hid_ref.shape[0] // block):
        rows = slice(i * block, (i + 1) * block)
        placed = jnp.dot(hot_ref[rows, :], update, preferred_element_type=F32)
        out_ref[rows, :] = (hid_ref[rows, :].astype(F32) + placed).astype(BF16)
        copies += fetch([(out_ref.at[rows, :], out.at[rows, :])], sems, i)
    settle(copies)


def out_last(pair, w, total, stats, hot, hidden):
    return call(
        out_last_kernel,
        "out_last",
        (*pair, w, total, *stats, hot, hidden),
        [arr(hidden.shape, BF16)],
        scratch=[pltpu.VMEM(hidden.shape, BF16), pltpu.SemaphoreType.DMA((hidden.shape[0] // 256,))],
        out_hbm=True,
    )[0]


def angles(row_pos):
    half = HEAD_SIZE // 2
    frequency = ROPE_BASE ** (-(jnp.arange(half, dtype=F32) * 2.0 / HEAD_SIZE))
    turned = row_pos.astype(F32) * jnp.concatenate([frequency, frequency])[None, :]
    sign = jnp.concatenate([-jnp.ones((half,), F32), jnp.ones((half,), F32)])
    return jnp.cos(turned), jnp.sin(turned) * sign[None, :]


def body(
    size,
    hidden_in,
    norm_gain,
    router_weight,
    w_query,
    w_key,
    value_weight,
    w_out,
    keep_flags,
    keep_counts,
    keep_positions,
):
    shards = lax.axis_size("ctx")
    tok = hidden_in.shape[0]
    nq = w_query.shape[1]
    flags = keep_flags.reshape(-1, 128)
    weights = (norm_gain.reshape(1, -1), router_weight.reshape(1, -1), w_query, w_key, value_weight)

    full, first, second, rowpos = pick(keep_positions, hidden_in)
    held = {}

    def own(mine, twin, ride):
        ride, held["sums"], *held["staged"], held["bias"], held["hot"] = own_part(
            *mine, *twin, ride, weights, keep_counts, keep_positions, flags, tok
        )
        return ride

    def far(mine, twin, rides):
        held["sums"], ride, held["cos"], held["sin"] = more_part(
            mine, twin, held["staged"], held["sums"], (*rides, *angles(rowpos)), lambda z: 3 - z, FAR_COST
        )
        return (ride,)

    def beside(mine, twin):
        (held["sums"],) = more_part(mine, twin, held["staged"], held["sums"], (), lambda z: z ^ 1, BESIDE_COST)

    pairs = spread_halves(size, full, first, second, own, far, beside)
    sums, staged, bias = held["sums"], held["staged"], held["bias"]
    cos, sin = held["cos"], held["sin"]
    half = first.shape[0]
    onward = [(s, s + 1) for s in range(shards - 1)]
    kvs, stats, moved, qs, carry = [], [], [], [], []
    for i in range(2):
        kv, stat = kv_last(i * half, pairs[i], staged, sums, cos, sin, nq, KV_COST)
        kvs.append(kv)
        stats.append(stat)
        moved.append(lax.ppermute(kv, "ctx", onward))
        q, *terms = q_part(i, pairs[i], staged, sums, stat, cos, sin, kvs, bias, nq, QA_COST if i == 0 else Q_COST)
        qs.append(q)
        carry += terms
    for step in range(1, shards):
        for i in range(2):
            last = step == shards - 1 and i == 1
            carry = attend_more(step, i * half, last, qs, moved[i], bias, carry, ATTEND_COST)
        if step < shards - 1:
            moved = [lax.ppermute(kv, "ctx", onward) for kv in moved]

    def own_out(mine, twin, rides):
        *rides, held["total"], held["w"], held["hidden"] = out_own(mine, twin, rides, w_out, hidden_in)
        return rides

    def far_out(mine, twin, rides):
        held["total"], *rides = out_more(mine, twin, held["w"], held["total"], rides, lambda z: 3 - z, PART_COST)
        return rides

    def beside_out(mine, twin):
        (held["total"],) = out_more(mine, twin, held["w"], held["total"], (), lambda z: z ^ 1, PART_COST)

    pair = spread(size, *carry, own_out, far_out, beside_out)
    return out_last(pair, held["w"], held["total"], stats, held["hot"], held["hidden"])


def solution(mesh):
    in_specs = (
        P(("groups", "ctx"), "heads"),
        P(),
        P(),
        P(None, "heads"),
        P(None, "heads"),
        P(None, "heads"),
        P(None, "heads"),
        P(("groups", "ctx")),
        P("groups"),
        P("groups", None),
    )
    out_specs = P(("groups", "ctx"), "heads")
    return jax.shard_map(
        functools.partial(body, mesh.shape["heads"]),
        mesh=mesh,
        in_specs=in_specs,
        out_specs=out_specs,
        check_vma=False,
    )
```

```python
import functools

import jax
import jax.numpy as jnp
from jax import lax
from jax.experimental import pallas as pl
from jax.experimental.pallas import tpu as pltpu
from jax.sharding import PartitionSpec as P

HEAD_SIZE = 128
ROPE_BASE = 500000.0
NORM_EPS = 1e-05
LOG2E = 1.4426950408889634
VMEM_LIMIT = 24 * 1024 * 1024
F32 = jnp.float32
BF16 = jnp.bfloat16
I32 = jnp.int32
COST = 400_000_000
PART_COST = 1_500_000_000
OWN_COST = 1_500_000_000
FAR_COST = 1_500_000_000
BESIDE_COST = 1_000_000
KV_COST = 400_000_000
Q_COST = 400_000_000
QA_COST = 1_500_000_000
ATTEND_COST = 400_000_000


VMEM = pl.BlockSpec(memory_space=pltpu.VMEM)
HBM = pl.BlockSpec(memory_space=pltpu.HBM)


def arr(shape, dtype):
    return jax.ShapeDtypeStruct(shape, dtype)


def call(kernel, name, operands, out_shape, scratch=(), rides=None, hbm=(), out_hbm=False, flops=COST):
    operands = [(o, any(o is h for h in hbm)) for o in operands]
    return pl.pallas_call(
        kernel,
        out_shape=out_shape,
        in_specs=[HBM if far else VMEM for _, far in operands],
        out_specs=[HBM if out_hbm else VMEM] * len(out_shape),
        scratch_shapes=list(scratch),
        input_output_aliases=rides or {},
        compiler_params=pltpu.CompilerParams(vmem_limit_bytes=VMEM_LIMIT),
        cost_estimate=pl.CostEstimate(flops=flops, bytes_accessed=1, transcendentals=0),
        name=name,
    )(*(pltpu.with_memory_space_constraint(o, pltpu.HBM) if far else o for o, far in operands))


def fetch(pairs, sems, base=0):
    copies = [pltpu.make_async_copy(src, dst, sems.at[base + i]) for i, (src, dst) in enumerate(pairs)]
    for copy in copies:
        copy.start()
    return copies


def place():
    d = lax.axis_index("heads")
    return d // 2, lax.rem(d, 2)


def live_row(pos_ref, cnt_ref, shard, dead):
    pos = pos_ref[pl.ds(shard, 1), :]
    slot = lax.broadcasted_iota(I32, pos.shape, 1)
    return jnp.where(slot < cnt_ref[shard], pos, dead)


def column(row):
    return jnp.transpose(jnp.broadcast_to(row, (128, row.shape[1])))


def pick_kernel(pos_hbm, hid_hbm, x_ref, xa_ref, xb_ref, rowpos_ref, pos_ref, hid_ref, sems):
    own, shards = lax.axis_index("ctx"), lax.axis_size("ctx")
    tok, cap = hid_ref.shape[0], x_ref.shape[0]
    pieces = [slice(at, at + 256) for at in range(0, tok, 256)]
    copies = fetch([(pos_hbm, pos_ref), *((hid_hbm.at[p, :], hid_ref.at[p, :]) for p in pieces)], sems)
    copies[0].wait()
    pos = column(pos_ref[pl.ds(own, 1), :])
    rowpos_ref[...] = jnp.where(pos < 0, shards * tok, pos)
    local = pos[:, :1] - own * tok
    total = None
    for piece, copy in zip(pieces, copies[1:]):
        at = lax.broadcasted_iota(I32, (cap, 256), 1) + piece.start
        hot = jnp.where(at == local, 1.0, 0.0).astype(BF16)
        copy.wait()
        total = add(total, jnp.dot(hot, hid_ref[piece, :], preferred_element_type=F32))
    x = total.astype(BF16)
    x_ref[...] = x
    xa_ref[...] = x[: cap // 2]
    xb_ref[...] = x[cap // 2 :]


def pick(positions, hidden):
    cap, width = positions.shape[1], hidden.shape[1]
    return call(
        pick_kernel,
        "pick",
        (positions, hidden),
        [arr((cap, width), BF16), arr((cap // 2, width), BF16), arr((cap // 2, width), BF16), arr((cap, 128), I32)],
        scratch=[
            pltpu.VMEM(positions.shape, I32),
            pltpu.VMEM(hidden.shape, BF16),
            pltpu.SemaphoreType.DMA((1 + hidden.shape[0] // 256,)),
        ],
        hbm=(positions, hidden),
    )


def sender(perm):
    return functools.partial(lax.ppermute, axis_name="heads", perm=perm)


def chip_sender(size, f):
    return sender([(2 * z + c, 2 * f(z) + c) for z in range(size // 2) for c in range(2)])


def spread(size, full, first, second, use_own, use_far, use_beside):
    cross = chip_sender(size, lambda z: 3 - z)
    near = chip_sender(size, lambda z: z ^ 1)
    twin = sender([(d, d ^ 1) for d in range(size)])
    far = cross(full)
    mates = twin(first), twin(second)
    beside = near(first), near(second)
    last = near(far)
    beside = use_own((full,), mates, beside)
    beside = use_far((far,), (twin(far),), beside)
    use_beside(beside, (twin(beside[0]), twin(beside[1])))
    return last, twin(last)


def spread_halves(size, full, first, second, use_own, use_far, use_beside):
    cross = chip_sender(size, lambda z: 3 - z)
    near = chip_sender(size, lambda z: z ^ 1)
    twin = sender([(d, d ^ 1) for d in range(size)])
    far = cross(first), cross(second)
    beside = near(use_own((full,), (twin(full),)))
    last_a, last_b = near(far[0]), near(far[1])
    (last_a,) = use_far(far, (twin(far[0]), twin(far[1])), (last_a,))
    use_beside((beside,), (twin(beside),))
    return (last_a, twin(last_a)), (last_b, twin(last_b))


def joined(refs):
    parts = [ref[...] for ref in refs]
    return parts[0] if len(parts) == 1 else jnp.concatenate(parts, axis=0)


def lanes_sum(x):
    total = x[:, :128]
    for at in range(128, x.shape[1], 128):
        total = total + x[:, at : at + 128]
    return total


def halves(mine, twin, zz, core):
    width = mine.shape[1]
    rows = [pl.ds(pl.multiple_of((2 * zz + at) * width, width), width) for at in (core, 1 - core)]
    return zip((mine, twin), rows)


def add(a, b):
    return b if a is None else a + b


def project(mine, twin, zz, core, gain_ref, router_ref, w_ref, columns, stats=True):
    product = squares = routed = None
    for x, rows in halves(mine, twin, zz, core):
        xf = x.astype(F32)
        gained = (xf * gain_ref[:, rows]).astype(BF16)
        product = add(product, jnp.dot(gained, w_ref[rows, columns], preferred_element_type=F32))
        if stats:
            squares = add(squares, lanes_sum(xf * xf))
            routed = add(routed, lanes_sum(xf * router_ref[:, rows]))
    return product, squares, routed


def settle(copies):
    for copy in copies:
        copy.wait()


def own_kernel(x_ref, twin_ref, gain, router, wq, wk, wv, cnt, pos, flag, *refs):
    _, sums_ref, gain_ref, router_ref, w_ref, bias_ref, hot_ref, sems = refs[:8]
    z, core = place()
    nq, nk, depth = wq.shape[1], wk.shape[1], wq.shape[0]
    lanes = ((wq, slice(0, nq)), (wk, slice(nq, nq + nk)), (wv, slice(nq + nk, nq + 2 * nk)))
    block = 2 * x_ref.shape[1]
    blocks = depth // block
    vectors = fetch([(gain, gain_ref), (router, router_ref)], sems, 3 * blocks)
    copies = []
    for i in range(blocks):
        rows = pl.ds(pl.multiple_of((z ^ i) * block, block), block)
        copies.append(fetch([(w.at[rows, :], w_ref.at[rows, at]) for w, at in lanes], sems, 3 * i))
    settle(vectors)
    settle(copies[0])
    product, squares, routed = project(x_ref[...], twin_ref[...], z, core, gain_ref, router_ref, w_ref, slice(None))
    n = product.shape[1]
    sums_ref[:, 0:n] = product
    sums_ref[:, n : n + 128] = squares
    sums_ref[:, n + 128 : n + 256] = routed
    masks_kernel(cnt, pos, flag, bias_ref, hot_ref, *refs[8:])
    for later in copies[1:]:
        settle(later)


def own_part(full, twin, weights, counts, positions, flags, tok):
    cap, width = full.shape
    depth = weights[2].shape[0]
    columns = sum(w.shape[1] for w in weights[2:])
    shards = positions.shape[0]
    return call(
        own_kernel,
        "own_part",
        (full, twin, *weights, counts, positions, flags),
        [
            arr(full.shape, BF16),
            arr((cap, columns + 256), F32),
            arr((1, depth), F32),
            arr((1, depth), F32),
            arr((depth, columns), BF16),
            arr((shards, cap, cap), F32),
            arr((tok, cap), BF16),
        ],
        scratch=[
            pltpu.SemaphoreType.DMA((3 * depth // (2 * width) + 2,)),
            pltpu.SMEM(counts.shape, I32),
            pltpu.VMEM(positions.shape, I32),
            pltpu.VMEM(flags.shape, I32),
            pltpu.SemaphoreType.DMA((3,)),
        ],
        rides={0: 0},
        hbm=(*weights, counts, positions, flags),
        flops=OWN_COST,
    )


def masks_kernel(cnt_hbm, pos_hbm, flag_hbm, bias_ref, hot_ref, cnt_ref, pos_ref, flag_ref, sems):
    settle(fetch([(cnt_hbm, cnt_ref), (pos_hbm, pos_ref), (flag_hbm, flag_ref)], sems))
    own, shards = lax.axis_index("ctx"), lax.axis_size("ctx")
    tok = hot_ref.shape[0]
    seq = shards * tok
    row = live_row(pos_ref, cnt_ref, own, seq)
    for step in range(shards):
        source = lax.rem(own + shards - step, shards)
        keys = column(live_row(pos_ref, cnt_ref, source, seq + 1))[:, :1]
        bias_ref[step] = jnp.where(keys <= row, 0.0, -jnp.inf).astype(F32)
    flags = jnp.transpose(flag_ref[...].astype(F32))
    local = row - own * tok
    for r in range(tok // 128):
        at = lax.broadcasted_iota(I32, (128, row.shape[1]), 0) + r * 128
        hot = jnp.where(at == local, flags[:, r : r + 1], 0.0)
        hot_ref[r * 128 : (r + 1) * 128, :] = hot.astype(BF16)


def more_kernel(n_mine, n_twin, n_ride, flip, *refs):
    mine, twin, refs = refs[:n_mine], refs[n_mine : n_mine + n_twin], refs[n_mine + n_twin :]
    gain_ref, router_ref, w_ref, sums_in = refs[:4]
    sums_out = refs[4 + n_ride]
    z, core = place()
    product, squares, routed = project(
        joined(mine), joined(twin), flip(z), core, gain_ref, router_ref, w_ref, slice(None)
    )
    n = product.shape[1]
    sums_out[:, 0:n] = sums_in[:, 0:n] + product
    sums_out[:, n : n + 128] = sums_in[:, n : n + 128] + squares
    sums_out[:, n + 128 : n + 256] = sums_in[:, n + 128 : n + 256] + routed


def more_part(mine, twin, staged, sums, rides, flip, flops):
    at = len(mine) + len(twin) + 3
    return call(
        functools.partial(more_kernel, len(mine), len(twin), len(rides), flip),
        "more_part",
        (*mine, *twin, *staged, sums, *rides),
        [arr(sums.shape, F32), *(arr(r.shape, r.dtype) for r in rides)],
        rides={at + i: i for i in range(1 + len(rides))},
        flops=flops,
    )


def turn(x, cos, sin):
    return x * cos + pltpu.roll(x, HEAD_SIZE // 2, 1) * sin


def kv_last_kernel(nq, at, mine_ref, twin_ref, gain_ref, router_ref, w_ref, sums, cos_ref, sin_ref, *outs):
    kv_out, stat_out = outs[-2:] if len(outs) == 2 else outs[1:3]
    z, core = place()
    n, features = w_ref.shape[1], w_ref.shape[0]
    rows = slice(at, at + mine_ref.shape[0])
    product, squares, routed = project(
        mine_ref[...], twin_ref[...], z ^ 2, core, gain_ref, router_ref, w_ref, slice(nq, n)
    )
    squares = jnp.sum(sums[rows, n : n + 128] + squares, axis=1, keepdims=True)
    routed = jnp.sum(sums[rows, n + 128 : n + 256] + routed, axis=1, keepdims=True)
    inverse = lax.rsqrt(squares * (1.0 / features) + NORM_EPS)
    kv = (sums[rows, nq:n] + product) * inverse
    kv_out[:, 0:128] = turn(kv[:, 0:128], cos_ref[rows, :], sin_ref[rows, :]).astype(BF16)
    kv_out[:, 128:256] = kv[:, 128:256].astype(BF16)
    stat_out[:, 0:128] = jnp.broadcast_to(inverse, (inverse.shape[0], 128))
    gate = 1.0 / (1.0 + jnp.exp(-routed))
    stat_out[:, 128:256] = jnp.broadcast_to(gate, (gate.shape[0], 128))


def kv_last(at, pair, staged, sums, cos, sin, rides, nq, flops):
    cap = pair[0].shape[0]
    operands = (*pair, *staged, sums, cos, sin, *rides)
    return call(
        functools.partial(kv_last_kernel, nq, at),
        "kv_last",
        operands,
        [arr((cap, 256), BF16), arr((cap, 256), F32), *(arr(r.shape, r.dtype) for r in rides)],
        rides={len(operands) - len(rides) + i: 2 + i for i in range(len(rides))},
        flops=flops,
    )


def attend(q, kv, bias, carry):
    k, v = kv[:, 0:128], kv[:, 128:256]
    scale = LOG2E / HEAD_SIZE**0.5
    s = lax.dot_general(k, q, (((1,), (1,)), ((), ())), preferred_element_type=F32) * scale + bias
    top = jnp.max(s, axis=0, keepdims=True)
    if carry is not None:
        top = jnp.maximum(top, carry[0])
    e = jnp.exp2(s - top)
    total = jnp.sum(e, axis=0, keepdims=True)
    mix = lax.dot_general(v, e.astype(BF16), (((0,), (0,)), ((), ())), preferred_element_type=F32)
    if carry is not None:
        fade = jnp.exp2(carry[0] - top)
        total = total + carry[1] * fade
        mix = mix + carry[2] * fade
    return top, total, mix


def q_kernel(i, n_kv, mine_ref, twin_ref, gain_ref, w_ref, sums, stat_ref, cos_ref, sin_ref, bias_ref, *refs):
    kv_refs, (q_out, top_ref, total_ref, mix_ref) = refs[:n_kv], refs[n_kv:]
    z, core = place()
    half, nq = q_out.shape
    rows, keys = slice(i * half, (i + 1) * half), slice(0, (i + 1) * half)
    product, _, _ = project(
        mine_ref[...], twin_ref[...], z ^ 2, core, gain_ref, None, w_ref, slice(0, nq), stats=False
    )
    q = (sums[rows, 0:nq] + product) * stat_ref[:, 0:1]
    cos, sin, kv = cos_ref[rows, :], sin_ref[rows, :], joined(kv_refs)
    for h in range(nq // HEAD_SIZE):
        lanes = slice(h * HEAD_SIZE, (h + 1) * HEAD_SIZE)
        turned = turn(q[:, lanes], cos, sin).astype(BF16)
        q_out[:, lanes] = turned
        top, total, mix = attend(turned, kv, bias_ref[0, keys, rows], None)
        at = slice(h * half, (h + 1) * half)
        top_ref[:, at], total_ref[:, at], mix_ref[:, at] = top, total, mix


def carry_shapes(cap, nq):
    heads = nq // HEAD_SIZE
    return [arr((1, heads * cap), F32), arr((1, heads * cap), F32), arr((HEAD_SIZE, heads * cap), F32)]


def q_part(i, pair, staged, sums, stat, cos, sin, kvs, bias, nq, flops):
    half = pair[0].shape[0]
    return call(
        functools.partial(q_kernel, i, len(kvs)),
        "q_part",
        (*pair, staged[0], staged[2], sums, stat, cos, sin, bias, *kvs),
        [arr((half, nq), BF16), *carry_shapes(half, nq)],
        flops=flops,
    )


def attend_kernel(step, first_key, n_carry, last, qa_ref, qb_ref, kv_ref, bias_ref, *refs):
    carries, outs = refs[: 3 * n_carry], refs[3 * n_carry :]
    half, nq = qa_ref.shape
    cap = 2 * half
    keys = slice(first_key, first_key + kv_ref.shape[0])
    for h in range(nq // HEAD_SIZE):
        lanes = slice(h * HEAD_SIZE, (h + 1) * HEAD_SIZE)
        at = slice(h * cap, (h + 1) * cap)
        part = slice(h * cap // n_carry, (h + 1) * cap // n_carry)
        carry = [
            jnp.concatenate([carries[j][:, part] for j in range(k, 3 * n_carry, 3)], axis=1) for k in range(3)
        ]
        q = jnp.concatenate([qa_ref[:, lanes], qb_ref[:, lanes]], axis=0)
        top, total, mix = attend(q, kv_ref[...], bias_ref[step, keys, :], carry)
        if not last:
            outs[0][:, at], outs[1][:, at], outs[2][:, at] = top, total, mix
            continue
        full, first, second = outs
        attn = jnp.transpose(mix * (1.0 / total)).astype(BF16)
        full[:, lanes] = attn
        first[:, lanes] = attn[:half]
        second[:, lanes] = attn[half:]


def attend_more(step, first_key, last, qs, kv, bias, carry, flops):
    half, nq = qs[0].shape
    cap = 2 * half
    shapes = [arr((cap, nq), BF16), arr((half, nq), BF16), arr((half, nq), BF16)]
    return call(
        functools.partial(attend_kernel, step, first_key, len(carry) // 3, last),
        "attend_more",
        (*qs, kv, bias, *carry),
        shapes if last else carry_shapes(cap, nq),
        flops=flops,
    )


def out_term(mine, twin, zz, core, w_ref):
    out = None
    for x, rows in halves(mine, twin, zz, core):
        out = add(out, jnp.dot(x, w_ref[rows, :], preferred_element_type=F32))
    return out


def out_own_kernel(n_mine, n_twin, *refs):
    mine, twin, refs = refs[:n_mine], refs[n_mine : n_mine + n_twin], refs[n_mine + n_twin :]
    n_ride = (len(refs) - 6) // 2
    w, hidden = refs[n_ride : n_ride + 2]
    total_ref, w_ref, hid_ref, sems = refs[-4:]
    z, core = place()
    copies = fetch([(w, w_ref), (hidden, hid_ref)], sems)
    copies[0].wait()
    total_ref[...] = out_term(joined(mine), joined(twin), z, core, w_ref)
    copies[1].wait()


def out_own(mine, twin, rides, w_out, hidden):
    cap = sum(x.shape[0] for x in mine)
    at = len(mine) + len(twin)
    return call(
        functools.partial(out_own_kernel, len(mine), len(twin)),
        "out_own",
        (*mine, *twin, *rides, w_out, hidden),
        [
            *(arr(r.shape, r.dtype) for r in rides),
            arr((cap, w_out.shape[1]), F32),
            arr(w_out.shape, BF16),
            arr(hidden.shape, BF16),
        ],
        scratch=[pltpu.SemaphoreType.DMA((2,))],
        rides={at + i: i for i in range(len(rides))},
        hbm=(w_out, hidden),
        flops=PART_COST,
    )


def out_more_kernel(n_mine, n_twin, flip, *refs):
    mine, twin, refs = refs[:n_mine], refs[n_mine : n_mine + n_twin], refs[n_mine + n_twin :]
    w_ref, total_in = refs[:2]
    total_out = refs[2 + (len(refs) - 3) // 2]
    z, core = place()
    total_out[...] = total_in[...] + out_term(joined(mine), joined(twin), flip(z), core, w_ref)


def out_more(mine, twin, w, total, rides, flip, flops):
    at = len(mine) + len(twin) + 1
    return call(
        functools.partial(out_more_kernel, len(mine), len(twin), flip),
        "out_more",
        (*mine, *twin, w, total, *rides),
        [arr(total.shape, F32), *(arr(r.shape, r.dtype) for r in rides)],
        rides={at + i: i for i in range(1 + len(rides))},
        flops=flops,
    )


def out_last_kernel(mine_ref, twin_ref, w_ref, total_ref, sa_ref, sb_ref, hot_ref, hid_ref, out, out_ref, sems):
    z, core = place()
    projected = total_ref[...] + out_term(mine_ref[...], twin_ref[...], z ^ 2, core, w_ref)
    gate = jnp.concatenate([sa_ref[:, 128:129], sb_ref[:, 128:129]], axis=0)
    update = (gate * projected).astype(BF16)
    block = 256
    copies = []
    for i in range(hid_ref.shape[0] // block):
        rows = slice(i * block, (i + 1) * block)
        placed = jnp.dot(hot_ref[rows, :], update, preferred_element_type=F32)
        out_ref[rows, :] = (hid_ref[rows, :].astype(F32) + placed).astype(BF16)
        copies += fetch([(out_ref.at[rows, :], out.at[rows, :])], sems, i)
    settle(copies)


def out_last(pair, w, total, stats, hot, hidden):
    return call(
        out_last_kernel,
        "out_last",
        (*pair, w, total, *stats, hot, hidden),
        [arr(hidden.shape, BF16)],
        scratch=[pltpu.VMEM(hidden.shape, BF16), pltpu.SemaphoreType.DMA((hidden.shape[0] // 256,))],
        out_hbm=True,
    )[0]


def angles(row_pos):
    half = HEAD_SIZE // 2
    frequency = ROPE_BASE ** (-(jnp.arange(half, dtype=F32) * 2.0 / HEAD_SIZE))
    turned = row_pos.astype(F32) * jnp.concatenate([frequency, frequency])[None, :]
    sign = jnp.concatenate([-jnp.ones((half,), F32), jnp.ones((half,), F32)])
    return jnp.cos(turned), jnp.sin(turned) * sign[None, :]


def body(
    size,
    hidden_in,
    norm_gain,
    router_weight,
    w_query,
    w_key,
    value_weight,
    w_out,
    keep_flags,
    keep_counts,
    keep_positions,
):
    shards = lax.axis_size("ctx")
    tok = hidden_in.shape[0]
    nq = w_query.shape[1]
    flags = keep_flags.reshape(-1, 128)
    weights = (norm_gain.reshape(1, -1), router_weight.reshape(1, -1), w_query, w_key, value_weight)

    full, first, second, rowpos = pick(keep_positions, hidden_in)
    held = {}

    def own(mine, mate):
        ride, held["sums"], *held["staged"], held["bias"], held["hot"] = own_part(
            *mine, *mate, weights, keep_counts, keep_positions, flags, tok
        )
        return ride

    def far(mine, twin, rides):
        held["sums"], ride, held["cos"], held["sin"] = more_part(
            mine, twin, held["staged"], held["sums"], (*rides, *angles(rowpos)), lambda z: 3 - z, FAR_COST
        )
        return (ride,)

    def beside(mine, twin):
        (held["sums"],) = more_part(mine, twin, held["staged"], held["sums"], (), lambda z: z ^ 1, BESIDE_COST)

    pairs = spread_halves(size, full, first, second, own, far, beside)
    sums, staged, bias = held["sums"], held["staged"], held["bias"]
    cos, sin = held["cos"], held["sin"]
    half = first.shape[0]
    ring = [(s, (s + 1) % shards) for s in range(shards)]
    kvs, stats, qs, carry = [], [], [], []
    for i in range(2):
        kv, stat, *kvs = kv_last(i * half, pairs[i], staged, sums, cos, sin, kvs, nq, KV_COST)
        kvs.append(kv)
        stats.append(stat)
    moved = [lax.ppermute(kv, "ctx", ring) for kv in kvs]
    for i in range(2):
        q, *terms = q_part(
            i, pairs[i], staged, sums, stats[i], cos, sin, kvs[: i + 1], bias, nq, Q_COST if i else QA_COST
        )
        qs.append(q)
        carry += terms
    for step in range(1, shards):
        for i in range(2):
            last = step == shards - 1 and i == 1
            carry = attend_more(step, i * half, last, qs, moved[i], bias, carry, ATTEND_COST)
        if step < shards - 1:
            moved = [lax.ppermute(kv, "ctx", ring) for kv in moved]

    def own_out(mine, twin, rides):
        *rides, held["total"], held["w"], held["hidden"] = out_own(mine, twin, rides, w_out, hidden_in)
        return rides

    def far_out(mine, twin, rides):
        held["total"], *rides = out_more(mine, twin, held["w"], held["total"], rides, lambda z: 3 - z, PART_COST)
        return rides

    def beside_out(mine, twin):
        (held["total"],) = out_more(mine, twin, held["w"], held["total"], (), lambda z: z ^ 1, PART_COST)

    pair = spread(size, *carry, own_out, far_out, beside_out)
    return out_last(pair, held["w"], held["total"], stats, held["hot"], held["hidden"])


def solution(mesh):
    in_specs = (
        P(("groups", "ctx"), "heads"),
        P(),
        P(),
        P(None, "heads"),
        P(None, "heads"),
        P(None, "heads"),
        P(None, "heads"),
        P(("groups", "ctx")),
        P("groups"),
        P("groups", None),
    )
    out_specs = P(("groups", "ctx"), "heads")
    return jax.shard_map(
        functools.partial(body, mesh.shape["heads"]),
        mesh=mesh,
        in_specs=in_specs,
        out_specs=out_specs,
        check_vma=False,
    )
```

```python
import functools

import jax
import jax.numpy as jnp
from jax import lax
from jax.experimental import pallas as pl
from jax.experimental.pallas import tpu as pltpu
from jax.sharding import PartitionSpec as P

HEAD_SIZE = 128
ROPE_BASE = 500000.0
NORM_EPS = 1e-05
LOG2E = 1.4426950408889634
VMEM_LIMIT = 24 * 1024 * 1024
PIECES = 2
F32 = jnp.float32
BF16 = jnp.bfloat16
I32 = jnp.int32
COST = 400_000_000
PART_COST = 1_500_000_000
OWN_COST = 1_500_000_000
GATE_COST = 1_000_000
FAR_COST = 3_000_000_000
BESIDE_COST = 1_000_000
KV_COST = 1_000_000
Q_COST = 400_000_000
QA_COST = 1_500_000_000
ATTEND_COST = 400_000_000


VMEM = pl.BlockSpec(memory_space=pltpu.VMEM)
HBM = pl.BlockSpec(memory_space=pltpu.HBM)


def arr(shape, dtype):
    return jax.ShapeDtypeStruct(shape, dtype)


def call(kernel, name, operands, out_shape, scratch=(), rides=None, hbm=(), out_hbm=False, flops=COST):
    operands = [(o, any(o is h for h in hbm)) for o in operands]
    return pl.pallas_call(
        kernel,
        out_shape=out_shape,
        in_specs=[HBM if far else VMEM for _, far in operands],
        out_specs=[HBM if out_hbm else VMEM] * len(out_shape),
        scratch_shapes=list(scratch),
        input_output_aliases=rides or {},
        compiler_params=pltpu.CompilerParams(vmem_limit_bytes=VMEM_LIMIT),
        cost_estimate=pl.CostEstimate(flops=flops, bytes_accessed=1, transcendentals=0),
        name=name,
    )(*(pltpu.with_memory_space_constraint(o, pltpu.HBM) if far else o for o, far in operands))


def fetch(pairs, sems, base=0):
    copies = [pltpu.make_async_copy(src, dst, sems.at[base + i]) for i, (src, dst) in enumerate(pairs)]
    for copy in copies:
        copy.start()
    return copies


def place():
    d = lax.axis_index("heads")
    return d // 2, lax.rem(d, 2)


def live_row(pos_ref, cnt_ref, shard, dead):
    pos = pos_ref[pl.ds(shard, 1), :]
    slot = lax.broadcasted_iota(I32, pos.shape, 1)
    return jnp.where(slot < cnt_ref[shard], pos, dead)


def column(row):
    return jnp.transpose(jnp.broadcast_to(row, (128, row.shape[1])))


def pick_kernel(pos_hbm, hid_hbm, x_ref, xa_ref, xb_ref, rowpos_ref, pos_ref, hid_ref, sems):
    own, shards = lax.axis_index("ctx"), lax.axis_size("ctx")
    tok, cap = hid_ref.shape[0], x_ref.shape[0]
    pieces = [slice(at, at + 256) for at in range(0, tok, 256)]
    copies = fetch([(pos_hbm, pos_ref), *((hid_hbm.at[p, :], hid_ref.at[p, :]) for p in pieces)], sems)
    copies[0].wait()
    pos = column(pos_ref[pl.ds(own, 1), :])
    rowpos_ref[...] = jnp.where(pos < 0, shards * tok, pos)
    local = pos[:, :1] - own * tok
    total = None
    for piece, copy in zip(pieces, copies[1:]):
        at = lax.broadcasted_iota(I32, (cap, 256), 1) + piece.start
        hot = jnp.where(at == local, 1.0, 0.0).astype(BF16)
        copy.wait()
        total = add(total, jnp.dot(hot, hid_ref[piece, :], preferred_element_type=F32))
    x = total.astype(BF16)
    x_ref[...] = x
    xa_ref[...] = x[: cap // 2]
    xb_ref[...] = x[cap // 2 :]


def pick(positions, hidden):
    cap, width = positions.shape[1], hidden.shape[1]
    return call(
        pick_kernel,
        "pick",
        (positions, hidden),
        [arr((cap, width), BF16), arr((cap // 2, width), BF16), arr((cap // 2, width), BF16), arr((cap, 128), I32)],
        scratch=[
            pltpu.VMEM(positions.shape, I32),
            pltpu.VMEM(hidden.shape, BF16),
            pltpu.SemaphoreType.DMA((1 + hidden.shape[0] // 256,)),
        ],
        hbm=(positions, hidden),
    )


def sender(perm):
    return functools.partial(lax.ppermute, axis_name="heads", perm=perm)


def chip_sender(size, f):
    return sender([(2 * z + c, 2 * f(z) + c) for z in range(size // 2) for c in range(2)])


def gate(ride, other):
    return call(lambda *_: None, "gate", (ride, other), [arr(ride.shape, ride.dtype)], rides={0: 0}, flops=GATE_COST)[0]


def spread(size, full, first, second, use_own, use_far, use_beside):
    cross = chip_sender(size, lambda z: 3 - z)
    near = chip_sender(size, lambda z: z ^ 1)
    twin = sender([(d, d ^ 1) for d in range(size)])
    far = cross(full)
    mates = twin(first), twin(second)
    beside = near(first), near(second)
    last = near(far)
    beside = use_own((full,), mates, beside)
    beside = use_far((far,), (twin(far),), beside)
    use_beside(beside, (twin(beside[0]), twin(beside[1])))
    return last, twin(last)


def spread_halves(size, full, first, second, use_own, use_far, use_beside):
    cross = chip_sender(size, lambda z: 3 - z)
    near = chip_sender(size, lambda z: z ^ 1)
    twin = sender([(d, d ^ 1) for d in range(size)])
    far = cross(first), cross(second)
    beside = near(use_own((full,), (twin(full),)))
    last_a, last_b = near(far[0]), near(far[1])
    last_a = use_far(far, (twin(far[0]), twin(far[1])), last_a)
    use_beside((beside,), (twin(beside),))
    return (last_a, tuple(twin(x) for x in last_a)), last_b, twin


def joined(refs):
    parts = [ref[...] for ref in refs]
    return parts[0] if len(parts) == 1 else jnp.concatenate(parts, axis=0)


def lanes_sum(x):
    total = x[:, :128]
    for at in range(128, x.shape[1], 128):
        total = total + x[:, at : at + 128]
    return total


def halves(mine, twin, zz, core):
    width = mine.shape[1]
    rows = [pl.ds(pl.multiple_of((2 * zz + at) * width, width), width) for at in (core, 1 - core)]
    return zip((mine, twin), rows)


def add(a, b):
    return b if a is None else a + b


def project(mine, twin, zz, core, gain_ref, router_ref, w_ref, columns, stats=True):
    product = squares = routed = None
    for x, rows in halves(mine, twin, zz, core):
        xf = x.astype(F32)
        gained = (xf * gain_ref[:, rows]).astype(BF16)
        product = add(product, jnp.dot(gained, w_ref[rows, columns], preferred_element_type=F32))
        if stats:
            squares = add(squares, lanes_sum(xf * xf))
            routed = add(routed, lanes_sum(xf * router_ref[:, rows]))
    return product, squares, routed


def settle(copies):
    for copy in copies:
        copy.wait()


def own_kernel(x_ref, twin_ref, gain, router, wq, wk, wv, cnt, pos, flag, *refs):
    _, sums_ref, gain_ref, router_ref, w_ref, bias_ref, hot_ref, sems = refs[:8]
    z, core = place()
    nq, nk, depth = wq.shape[1], wk.shape[1], wq.shape[0]
    lanes = ((wq, slice(0, nq)), (wk, slice(nq, nq + nk)), (wv, slice(nq + nk, nq + 2 * nk)))
    block = 2 * x_ref.shape[1]
    blocks = depth // block
    vectors = fetch([(gain, gain_ref), (router, router_ref)], sems, 3 * blocks)
    copies = []
    for i in range(blocks):
        rows = pl.ds(pl.multiple_of((z ^ i) * block, block), block)
        copies.append(fetch([(w.at[rows, :], w_ref.at[rows, at]) for w, at in lanes], sems, 3 * i))
    settle(vectors)
    settle(copies[0])
    product, squares, routed = project(x_ref[...], twin_ref[...], z, core, gain_ref, router_ref, w_ref, slice(None))
    n = product.shape[1]
    sums_ref[:, 0:n] = product
    sums_ref[:, n : n + 128] = squares
    sums_ref[:, n + 128 : n + 256] = routed
    masks_kernel(cnt, pos, flag, bias_ref, hot_ref, *refs[8:])
    for later in copies[1:]:
        settle(later)


def own_part(full, twin, weights, counts, positions, flags, tok):
    cap, width = full.shape
    depth = weights[2].shape[0]
    columns = sum(w.shape[1] for w in weights[2:])
    shards = positions.shape[0]
    return call(
        own_kernel,
        "own_part",
        (full, twin, *weights, counts, positions, flags),
        [
            arr(full.shape, BF16),
            arr((cap, columns + 256), F32),
            arr((1, depth), F32),
            arr((1, depth), F32),
            arr((depth, columns), BF16),
            arr((shards, cap, cap), F32),
            arr((tok, cap), BF16),
        ],
        scratch=[
            pltpu.SemaphoreType.DMA((3 * depth // (2 * width) + 2,)),
            pltpu.SMEM(counts.shape, I32),
            pltpu.VMEM(positions.shape, I32),
            pltpu.VMEM(flags.shape, I32),
            pltpu.SemaphoreType.DMA((3,)),
        ],
        rides={0: 0},
        hbm=(*weights, counts, positions, flags),
        flops=OWN_COST,
    )


def masks_kernel(cnt_hbm, pos_hbm, flag_hbm, bias_ref, hot_ref, cnt_ref, pos_ref, flag_ref, sems):
    settle(fetch([(cnt_hbm, cnt_ref), (pos_hbm, pos_ref), (flag_hbm, flag_ref)], sems))
    own, shards = lax.axis_index("ctx"), lax.axis_size("ctx")
    tok = hot_ref.shape[0]
    seq = shards * tok
    row = live_row(pos_ref, cnt_ref, own, seq)
    for step in range(shards):
        source = lax.rem(own + shards - step, shards)
        keys = column(live_row(pos_ref, cnt_ref, source, seq + 1))[:, :1]
        bias_ref[step] = jnp.where(keys <= row, 0.0, -jnp.inf).astype(F32)
    flags = jnp.transpose(flag_ref[...].astype(F32))
    local = row - own * tok
    for r in range(tok // 128):
        at = lax.broadcasted_iota(I32, (128, row.shape[1]), 0) + r * 128
        hot = jnp.where(at == local, flags[:, r : r + 1], 0.0)
        hot_ref[r * 128 : (r + 1) * 128, :] = hot.astype(BF16)


def more_kernel(n_mine, n_twin, n_ride, flip, split, *refs):
    mine, twin, refs = refs[:n_mine], refs[n_mine : n_mine + n_twin], refs[n_mine + n_twin :]
    gain_ref, router_ref, w_ref, sums_in = refs[:4]
    refs = refs[4 + n_ride :]
    if split:
        whole_ref, refs = refs[0], refs[1:]
        pieces = refs[1 + n_ride :]
        for i, piece in enumerate(pieces):
            piece[...] = whole_ref[i * piece.shape[0] : (i + 1) * piece.shape[0], :]
    sums_out = refs[0]
    z, core = place()
    product, squares, routed = project(
        joined(mine), joined(twin), flip(z), core, gain_ref, router_ref, w_ref, slice(None)
    )
    n = product.shape[1]
    sums_out[:, 0:n] = sums_in[:, 0:n] + product
    sums_out[:, n : n + 128] = sums_in[:, n : n + 128] + squares
    sums_out[:, n + 128 : n + 256] = sums_in[:, n + 128 : n + 256] + routed


def more_part(mine, twin, staged, sums, rides, flip, flops, split=()):
    at = len(mine) + len(twin) + 3
    shapes = [arr((x.shape[0] // PIECES, x.shape[1]), x.dtype) for x in split for _ in range(PIECES)]
    return call(
        functools.partial(more_kernel, len(mine), len(twin), len(rides), flip, bool(split)),
        "more_part",
        (*mine, *twin, *staged, sums, *rides, *split),
        [arr(sums.shape, F32), *(arr(r.shape, r.dtype) for r in rides), *shapes],
        rides={at + i: i for i in range(1 + len(rides))},
        flops=flops,
    )


def turn(x, cos, sin):
    return x * cos + pltpu.roll(x, HEAD_SIZE // 2, 1) * sin


def kv_last_kernel(nq, at, n_mine, *refs):
    mine, twin, refs = joined(refs[:n_mine]), joined(refs[n_mine : 2 * n_mine]), refs[2 * n_mine :]
    gain_ref, router_ref, w_ref, sums, cos_ref, sin_ref, kv_out, stat_out = refs
    z, core = place()
    n, features = w_ref.shape[1], w_ref.shape[0]
    rows = slice(at, at + mine.shape[0])
    product, squares, routed = project(mine, twin, z ^ 2, core, gain_ref, router_ref, w_ref, slice(nq, n))
    squares = jnp.sum(sums[rows, n : n + 128] + squares, axis=1, keepdims=True)
    routed = jnp.sum(sums[rows, n + 128 : n + 256] + routed, axis=1, keepdims=True)
    inverse = lax.rsqrt(squares * (1.0 / features) + NORM_EPS)
    kv = (sums[rows, nq:n] + product) * inverse
    kv_out[:, 0:128] = turn(kv[:, 0:128], cos_ref[rows, :], sin_ref[rows, :]).astype(BF16)
    kv_out[:, 128:256] = kv[:, 128:256].astype(BF16)
    stat_out[:, 0:128] = jnp.broadcast_to(inverse, (inverse.shape[0], 128))
    gate_value = 1.0 / (1.0 + jnp.exp(-routed))
    stat_out[:, 128:256] = jnp.broadcast_to(gate_value, (gate_value.shape[0], 128))


def kv_last(at, pair, staged, sums, cos, sin, nq, flops):
    mine, twin = pair
    cap = sum(x.shape[0] for x in mine)
    return call(
        functools.partial(kv_last_kernel, nq, at, len(mine)),
        "kv_last",
        (*mine, *twin, *staged, sums, cos, sin),
        [arr((cap, 256), BF16), arr((cap, 256), F32)],
        flops=flops,
    )


def attend(q, kv, bias, carry):
    k, v = kv[:, 0:128], kv[:, 128:256]
    scale = LOG2E / HEAD_SIZE**0.5
    s = lax.dot_general(k, q, (((1,), (1,)), ((), ())), preferred_element_type=F32) * scale + bias
    top = jnp.max(s, axis=0, keepdims=True)
    if carry is not None:
        top = jnp.maximum(top, carry[0])
    e = jnp.exp2(s - top)
    total = jnp.sum(e, axis=0, keepdims=True)
    mix = lax.dot_general(v, e.astype(BF16), (((0,), (0,)), ((), ())), preferred_element_type=F32)
    if carry is not None:
        fade = jnp.exp2(carry[0] - top)
        total = total + carry[1] * fade
        mix = mix + carry[2] * fade
    return top, total, mix


def q_kernel(i, n_mine, n_kv, *refs):
    mine, twin, refs = joined(refs[:n_mine]), joined(refs[n_mine : 2 * n_mine]), refs[2 * n_mine :]
    gain_ref, w_ref, sums, stat_ref, cos_ref, sin_ref, bias_ref, *refs = refs
    kv_refs, (q_out, top_ref, total_ref, mix_ref) = refs[:n_kv], refs[n_kv:]
    z, core = place()
    half, nq = q_out.shape
    rows, keys = slice(i * half, (i + 1) * half), slice(0, (i + 1) * half)
    product, _, _ = project(
        mine, twin, z ^ 2, core, gain_ref, None, w_ref, slice(0, nq), stats=False
    )
    q = (sums[rows, 0:nq] + product) * stat_ref[:, 0:1]
    cos, sin, kv = cos_ref[rows, :], sin_ref[rows, :], joined(kv_refs)
    for h in range(nq // HEAD_SIZE):
        lanes = slice(h * HEAD_SIZE, (h + 1) * HEAD_SIZE)
        turned = turn(q[:, lanes], cos, sin).astype(BF16)
        q_out[:, lanes] = turned
        top, total, mix = attend(turned, kv, bias_ref[0, keys, rows], None)
        at = slice(h * half, (h + 1) * half)
        top_ref[:, at], total_ref[:, at], mix_ref[:, at] = top, total, mix


def carry_shapes(cap, nq):
    heads = nq // HEAD_SIZE
    return [arr((1, heads * cap), F32), arr((1, heads * cap), F32), arr((HEAD_SIZE, heads * cap), F32)]


def q_part(i, pair, staged, sums, stat, cos, sin, kvs, bias, nq, flops):
    mine, twin = pair
    half = stat.shape[0]
    return call(
        functools.partial(q_kernel, i, len(mine), len(kvs)),
        "q_part",
        (*mine, *twin, staged[0], staged[2], sums, stat, cos, sin, bias, *kvs),
        [arr((half, nq), BF16), *carry_shapes(half, nq)],
        flops=flops,
    )


def attend_kernel(step, first_key, n_carry, last, qa_ref, qb_ref, kv_ref, bias_ref, *refs):
    carries, outs = refs[: 3 * n_carry], refs[3 * n_carry :]
    half, nq = qa_ref.shape
    cap = 2 * half
    keys = slice(first_key, first_key + kv_ref.shape[0])
    for h in range(nq // HEAD_SIZE):
        lanes = slice(h * HEAD_SIZE, (h + 1) * HEAD_SIZE)
        at = slice(h * cap, (h + 1) * cap)
        part = slice(h * cap // n_carry, (h + 1) * cap // n_carry)
        carry = [
            jnp.concatenate([carries[j][:, part] for j in range(k, 3 * n_carry, 3)], axis=1) for k in range(3)
        ]
        q = jnp.concatenate([qa_ref[:, lanes], qb_ref[:, lanes]], axis=0)
        top, total, mix = attend(q, kv_ref[...], bias_ref[step, keys, :], carry)
        if not last:
            outs[0][:, at], outs[1][:, at], outs[2][:, at] = top, total, mix
            continue
        full, first, second = outs
        attn = jnp.transpose(mix * (1.0 / total)).astype(BF16)
        full[:, lanes] = attn
        first[:, lanes] = attn[:half]
        second[:, lanes] = attn[half:]


def attend_more(step, first_key, last, qs, kv, bias, carry, flops):
    half, nq = qs[0].shape
    cap = 2 * half
    shapes = [arr((cap, nq), BF16), arr((half, nq), BF16), arr((half, nq), BF16)]
    return call(
        functools.partial(attend_kernel, step, first_key, len(carry) // 3, last),
        "attend_more",
        (*qs, kv, bias, *carry),
        shapes if last else carry_shapes(cap, nq),
        flops=flops,
    )


def out_term(mine, twin, zz, core, w_ref):
    out = None
    for x, rows in halves(mine, twin, zz, core):
        out = add(out, jnp.dot(x, w_ref[rows, :], preferred_element_type=F32))
    return out


def out_own_kernel(n_mine, n_twin, *refs):
    mine, twin, refs = refs[:n_mine], refs[n_mine : n_mine + n_twin], refs[n_mine + n_twin :]
    n_ride = (len(refs) - 6) // 2
    w, hidden = refs[n_ride : n_ride + 2]
    total_ref, w_ref, hid_ref, sems = refs[-4:]
    z, core = place()
    copies = fetch([(w, w_ref), (hidden, hid_ref)], sems)
    copies[0].wait()
    total_ref[...] = out_term(joined(mine), joined(twin), z, core, w_ref)
    copies[1].wait()


def out_own(mine, twin, rides, w_out, hidden):
    cap = sum(x.shape[0] for x in mine)
    at = len(mine) + len(twin)
    return call(
        functools.partial(out_own_kernel, len(mine), len(twin)),
        "out_own",
        (*mine, *twin, *rides, w_out, hidden),
        [
            *(arr(r.shape, r.dtype) for r in rides),
            arr((cap, w_out.shape[1]), F32),
            arr(w_out.shape, BF16),
            arr(hidden.shape, BF16),
        ],
        scratch=[pltpu.SemaphoreType.DMA((2,))],
        rides={at + i: i for i in range(len(rides))},
        hbm=(w_out, hidden),
        flops=PART_COST,
    )


def out_more_kernel(n_mine, n_twin, flip, *refs):
    mine, twin, refs = refs[:n_mine], refs[n_mine : n_mine + n_twin], refs[n_mine + n_twin :]
    w_ref, total_in = refs[:2]
    total_out = refs[2 + (len(refs) - 3) // 2]
    z, core = place()
    total_out[...] = total_in[...] + out_term(joined(mine), joined(twin), flip(z), core, w_ref)


def out_more(mine, twin, w, total, rides, flip, flops):
    at = len(mine) + len(twin) + 1
    return call(
        functools.partial(out_more_kernel, len(mine), len(twin), flip),
        "out_more",
        (*mine, *twin, w, total, *rides),
        [arr(total.shape, F32), *(arr(r.shape, r.dtype) for r in rides)],
        rides={at + i: i for i in range(1 + len(rides))},
        flops=flops,
    )


def out_last_kernel(mine_ref, twin_ref, w_ref, total_ref, sa_ref, sb_ref, hot_ref, hid_ref, out, out_ref, sems):
    z, core = place()
    projected = total_ref[...] + out_term(mine_ref[...], twin_ref[...], z ^ 2, core, w_ref)
    gate = jnp.concatenate([sa_ref[:, 128:129], sb_ref[:, 128:129]], axis=0)
    update = (gate * projected).astype(BF16)
    block = 256
    copies = []
    for i in range(hid_ref.shape[0] // block):
        rows = slice(i * block, (i + 1) * block)
        placed = jnp.dot(hot_ref[rows, :], update, preferred_element_type=F32)
        out_ref[rows, :] = (hid_ref[rows, :].astype(F32) + placed).astype(BF16)
        copies += fetch([(out_ref.at[rows, :], out.at[rows, :])], sems, i)
    settle(copies)


def out_last(pair, w, total, stats, hot, hidden):
    return call(
        out_last_kernel,
        "out_last",
        (*pair, w, total, *stats, hot, hidden),
        [arr(hidden.shape, BF16)],
        scratch=[pltpu.VMEM(hidden.shape, BF16), pltpu.SemaphoreType.DMA((hidden.shape[0] // 256,))],
        out_hbm=True,
    )[0]


def angles(row_pos):
    half = HEAD_SIZE // 2
    frequency = ROPE_BASE ** (-(jnp.arange(half, dtype=F32) * 2.0 / HEAD_SIZE))
    turned = row_pos.astype(F32) * jnp.concatenate([frequency, frequency])[None, :]
    sign = jnp.concatenate([-jnp.ones((half,), F32), jnp.ones((half,), F32)])
    return jnp.cos(turned), jnp.sin(turned) * sign[None, :]


def body(
    size,
    hidden_in,
    norm_gain,
    router_weight,
    w_query,
    w_key,
    value_weight,
    w_out,
    keep_flags,
    keep_counts,
    keep_positions,
):
    shards = lax.axis_size("ctx")
    tok = hidden_in.shape[0]
    nq = w_query.shape[1]
    flags = keep_flags.reshape(-1, 128)
    weights = (norm_gain.reshape(1, -1), router_weight.reshape(1, -1), w_query, w_key, value_weight)

    full, first, second, rowpos = pick(keep_positions, hidden_in)
    held = {}

    def own(mine, mate):
        ride, held["sums"], *held["staged"], held["bias"], held["hot"] = own_part(
            *mine, *mate, weights, keep_counts, keep_positions, flags, tok
        )
        return ride

    def far(mine, twin, last):
        held["sums"], held["cos"], held["sin"], *pieces = more_part(
            mine, twin, held["staged"], held["sums"], angles(rowpos), lambda z: 3 - z, FAR_COST, (last,)
        )
        return tuple(pieces)

    def beside(mine, twin):
        (held["sums"],) = more_part(mine, twin, held["staged"], held["sums"], (), lambda z: z ^ 1, BESIDE_COST)

    pair, last_b, twin = spread_halves(size, full, first, second, own, far, beside)
    sums, staged, bias = held["sums"], held["staged"], held["bias"]
    cos, sin = held["cos"], held["sin"]
    half = first.shape[0]
    ring = [(s, (s + 1) % shards) for s in range(shards)]
    kvs, stats, qs, carry = [], [], [], []
    moved = []
    for i in range(2):
        if i == 1:
            last_b = gate(last_b, kvs[0])
            pair = (last_b,), (twin(last_b),)
        kv, stat = kv_last(i * half, pair, staged, sums, cos, sin, nq, KV_COST)
        kvs.append(kv)
        stats.append(stat)
        moved.append(lax.ppermute(kv, "ctx", ring))
        q, *terms = q_part(
            i, pair, staged, sums, stat, cos, sin, kvs[: i + 1], bias, nq, Q_COST if i else QA_COST
        )
        qs.append(q)
        carry += terms
    for step in range(1, shards):
        for i in range(2):
            last = step == shards - 1 and i == 1
            carry = attend_more(step, i * half, last, qs, moved[i], bias, carry, ATTEND_COST)
        if step < shards - 1:
            moved = [lax.ppermute(kv, "ctx", ring) for kv in moved]

    def own_out(mine, twin, rides):
        *rides, held["total"], held["w"], held["hidden"] = out_own(mine, twin, rides, w_out, hidden_in)
        return rides

    def far_out(mine, twin, rides):
        held["total"], *rides = out_more(mine, twin, held["w"], held["total"], rides, lambda z: 3 - z, PART_COST)
        return rides

    def beside_out(mine, twin):
        (held["total"],) = out_more(mine, twin, held["w"], held["total"], (), lambda z: z ^ 1, PART_COST)

    pair = spread(size, *carry, own_out, far_out, beside_out)
    return out_last(pair, held["w"], held["total"], stats, held["hot"], held["hidden"])


def solution(mesh):
    in_specs = (
        P(("groups", "ctx"), "heads"),
        P(),
        P(),
        P(None, "heads"),
        P(None, "heads"),
        P(None, "heads"),
        P(None, "heads"),
        P(("groups", "ctx")),
        P("groups"),
        P("groups", None),
    )
    out_specs = P(("groups", "ctx"), "heads")
    return jax.shard_map(
        functools.partial(body, mesh.shape["heads"]),
        mesh=mesh,
        in_specs=in_specs,
        out_specs=out_specs,
        check_vma=False,
    )
```

```python
import functools

import jax
import jax.numpy as jnp
from jax import lax
from jax.experimental import pallas as pl
from jax.experimental.pallas import tpu as pltpu
from jax.sharding import PartitionSpec as P

HEAD_SIZE = 128
ROPE_BASE = 500000.0
NORM_EPS = 1e-05
LOG2E = 1.4426950408889634
VMEM_LIMIT = 24 * 1024 * 1024
PIECES = 2
F32 = jnp.float32
BF16 = jnp.bfloat16
I32 = jnp.int32
COST = 400_000_000
PART_COST = 1_500_000_000
OWN_COST = 1_500_000_000
GATE_COST = 1_000_000
FAR_COST = 3_000_000_000
BESIDE_COST = 1_000_000
KV_COST = 1_000_000
Q_COST = 1_000_000
QA_COST = 1_000_000
ATTEND_COST = 400_000_000


VMEM = pl.BlockSpec(memory_space=pltpu.VMEM)
HBM = pl.BlockSpec(memory_space=pltpu.HBM)


def arr(shape, dtype):
    return jax.ShapeDtypeStruct(shape, dtype)


def call(kernel, name, operands, out_shape, scratch=(), rides=None, hbm=(), out_hbm=False, flops=COST):
    operands = [(o, any(o is h for h in hbm)) for o in operands]
    return pl.pallas_call(
        kernel,
        out_shape=out_shape,
        in_specs=[HBM if far else VMEM for _, far in operands],
        out_specs=[HBM if out_hbm else VMEM] * len(out_shape),
        scratch_shapes=list(scratch),
        input_output_aliases=rides or {},
        compiler_params=pltpu.CompilerParams(vmem_limit_bytes=VMEM_LIMIT),
        cost_estimate=pl.CostEstimate(flops=flops, bytes_accessed=1, transcendentals=0),
        name=name,
    )(*(pltpu.with_memory_space_constraint(o, pltpu.HBM) if far else o for o, far in operands))


def fetch(pairs, sems, base=0):
    copies = [pltpu.make_async_copy(src, dst, sems.at[base + i]) for i, (src, dst) in enumerate(pairs)]
    for copy in copies:
        copy.start()
    return copies


def place():
    d = lax.axis_index("heads")
    return d // 2, lax.rem(d, 2)


def live_row(pos_ref, cnt_ref, shard, dead):
    pos = pos_ref[pl.ds(shard, 1), :]
    slot = lax.broadcasted_iota(I32, pos.shape, 1)
    return jnp.where(slot < cnt_ref[shard], pos, dead)


def column(row):
    return jnp.transpose(jnp.broadcast_to(row, (128, row.shape[1])))


def pick_kernel(pos_hbm, hid_hbm, x_ref, xa_ref, xb_ref, rowpos_ref, pos_ref, hid_ref, sems):
    own, shards = lax.axis_index("ctx"), lax.axis_size("ctx")
    tok, cap = hid_ref.shape[0], x_ref.shape[0]
    pieces = [slice(at, at + 256) for at in range(0, tok, 256)]
    copies = fetch([(pos_hbm, pos_ref), *((hid_hbm.at[p, :], hid_ref.at[p, :]) for p in pieces)], sems)
    copies[0].wait()
    pos = column(pos_ref[pl.ds(own, 1), :])
    rowpos_ref[...] = jnp.where(pos < 0, shards * tok, pos)
    local = pos[:, :1] - own * tok
    total = None
    for piece, copy in zip(pieces, copies[1:]):
        at = lax.broadcasted_iota(I32, (cap, 256), 1) + piece.start
        hot = jnp.where(at == local, 1.0, 0.0).astype(BF16)
        copy.wait()
        total = add(total, jnp.dot(hot, hid_ref[piece, :], preferred_element_type=F32))
    x = total.astype(BF16)
    x_ref[...] = x
    xa_ref[...] = x[: cap // 2]
    xb_ref[...] = x[cap // 2 :]


def pick(positions, hidden):
    cap, width = positions.shape[1], hidden.shape[1]
    return call(
        pick_kernel,
        "pick",
        (positions, hidden),
        [arr((cap, width), BF16), arr((cap // 2, width), BF16), arr((cap // 2, width), BF16), arr((cap, 128), I32)],
        scratch=[
            pltpu.VMEM(positions.shape, I32),
            pltpu.VMEM(hidden.shape, BF16),
            pltpu.SemaphoreType.DMA((1 + hidden.shape[0] // 256,)),
        ],
        hbm=(positions, hidden),
    )


def sender(perm):
    return functools.partial(lax.ppermute, axis_name="heads", perm=perm)


def chip_sender(size, f):
    return sender([(2 * z + c, 2 * f(z) + c) for z in range(size // 2) for c in range(2)])


def gate(*rides):
    shapes = [arr(r.shape, r.dtype) for r in rides]
    return call(lambda *_: None, "gate", rides, shapes, rides={i: i for i in range(len(rides))}, flops=GATE_COST)


def spread(size, full, first, second, use_own, use_far, use_beside):
    cross = chip_sender(size, lambda z: 3 - z)
    near = chip_sender(size, lambda z: z ^ 1)
    twin = sender([(d, d ^ 1) for d in range(size)])
    far = cross(full)
    mates = twin(first), twin(second)
    beside = near(first), near(second)
    last = near(far)
    beside = use_own((full,), mates, beside)
    beside = use_far((far,), (twin(far),), beside)
    use_beside(beside, (twin(beside[0]), twin(beside[1])))
    return last, twin(last)


def spread_halves(size, full, first, second, use_own, use_far, use_beside):
    cross = chip_sender(size, lambda z: 3 - z)
    near = chip_sender(size, lambda z: z ^ 1)
    twin = sender([(d, d ^ 1) for d in range(size)])
    far = cross(first), cross(second)
    beside = near(use_own((full,), (twin(full),)))
    last_a, last_b = near(far[0]), near(far[1])
    last_a = use_far(far, (twin(far[0]), twin(far[1])), last_a)
    use_beside((beside,), (twin(beside),))
    return (last_a, tuple(twin(x) for x in last_a)), last_b, twin


def joined(refs):
    parts = [ref[...] for ref in refs]
    return parts[0] if len(parts) == 1 else jnp.concatenate(parts, axis=0)


def lanes_sum(x):
    total = x[:, :128]
    for at in range(128, x.shape[1], 128):
        total = total + x[:, at : at + 128]
    return total


def halves(mine, twin, zz, core):
    width = mine.shape[1]
    rows = [pl.ds(pl.multiple_of((2 * zz + at) * width, width), width) for at in (core, 1 - core)]
    return zip((mine, twin), rows)


def add(a, b):
    return b if a is None else a + b


def project(mine, twin, zz, core, gain_ref, router_ref, w_ref, columns, stats=True):
    product = squares = routed = None
    for x, rows in halves(mine, twin, zz, core):
        xf = x.astype(F32)
        gained = (xf * gain_ref[:, rows]).astype(BF16)
        product = add(product, jnp.dot(gained, w_ref[rows, columns], preferred_element_type=F32))
        if stats:
            squares = add(squares, lanes_sum(xf * xf))
            routed = add(routed, lanes_sum(xf * router_ref[:, rows]))
    return product, squares, routed


def settle(copies):
    for copy in copies:
        copy.wait()


def own_kernel(x_ref, twin_ref, gain, router, wq, wk, wv, cnt, pos, flag, *refs):
    _, sums_ref, gain_ref, router_ref, w_ref, bias_ref, hot_ref, sems = refs[:8]
    z, core = place()
    nq, nk, depth = wq.shape[1], wk.shape[1], wq.shape[0]
    lanes = ((wq, slice(0, nq)), (wk, slice(nq, nq + nk)), (wv, slice(nq + nk, nq + 2 * nk)))
    block = 2 * x_ref.shape[1]
    blocks = depth // block
    vectors = fetch([(gain, gain_ref), (router, router_ref)], sems, 3 * blocks)
    copies = []
    for i in range(blocks):
        rows = pl.ds(pl.multiple_of((z ^ i) * block, block), block)
        copies.append(fetch([(w.at[rows, :], w_ref.at[rows, at]) for w, at in lanes], sems, 3 * i))
    settle(vectors)
    settle(copies[0])
    product, squares, routed = project(x_ref[...], twin_ref[...], z, core, gain_ref, router_ref, w_ref, slice(None))
    n = product.shape[1]
    sums_ref[:, 0:n] = product
    sums_ref[:, n : n + 128] = squares
    sums_ref[:, n + 128 : n + 256] = routed
    masks_kernel(cnt, pos, flag, bias_ref, hot_ref, *refs[8:])
    for later in copies[1:]:
        settle(later)


def own_part(full, twin, weights, counts, positions, flags, tok):
    cap, width = full.shape
    depth = weights[2].shape[0]
    columns = sum(w.shape[1] for w in weights[2:])
    shards = positions.shape[0]
    return call(
        own_kernel,
        "own_part",
        (full, twin, *weights, counts, positions, flags),
        [
            arr(full.shape, BF16),
            arr((cap, columns + 256), F32),
            arr((1, depth), F32),
            arr((1, depth), F32),
            arr((depth, columns), BF16),
            arr((shards, cap, cap), F32),
            arr((tok, cap), BF16),
        ],
        scratch=[
            pltpu.SemaphoreType.DMA((3 * depth // (2 * width) + 2,)),
            pltpu.SMEM(counts.shape, I32),
            pltpu.VMEM(positions.shape, I32),
            pltpu.VMEM(flags.shape, I32),
            pltpu.SemaphoreType.DMA((3,)),
        ],
        rides={0: 0},
        hbm=(*weights, counts, positions, flags),
        flops=OWN_COST,
    )


def masks_kernel(cnt_hbm, pos_hbm, flag_hbm, bias_ref, hot_ref, cnt_ref, pos_ref, flag_ref, sems):
    settle(fetch([(cnt_hbm, cnt_ref), (pos_hbm, pos_ref), (flag_hbm, flag_ref)], sems))
    own, shards = lax.axis_index("ctx"), lax.axis_size("ctx")
    tok = hot_ref.shape[0]
    seq = shards * tok
    row = live_row(pos_ref, cnt_ref, own, seq)
    for step in range(shards):
        source = lax.rem(own + shards - step, shards)
        keys = column(live_row(pos_ref, cnt_ref, source, seq + 1))[:, :1]
        bias_ref[step] = jnp.where(keys <= row, 0.0, -jnp.inf).astype(F32)
    flags = jnp.transpose(flag_ref[...].astype(F32))
    local = row - own * tok
    for r in range(tok // 128):
        at = lax.broadcasted_iota(I32, (128, row.shape[1]), 0) + r * 128
        hot = jnp.where(at == local, flags[:, r : r + 1], 0.0)
        hot_ref[r * 128 : (r + 1) * 128, :] = hot.astype(BF16)


def more_kernel(n_mine, n_twin, n_ride, flip, split, *refs):
    mine, twin, refs = refs[:n_mine], refs[n_mine : n_mine + n_twin], refs[n_mine + n_twin :]
    gain_ref, router_ref, w_ref, sums_in = refs[:4]
    refs = refs[4 + n_ride :]
    if split:
        whole_ref, refs = refs[0], refs[1:]
        pieces = refs[1 + n_ride :]
        for i, piece in enumerate(pieces):
            piece[...] = whole_ref[i * piece.shape[0] : (i + 1) * piece.shape[0], :]
    sums_out = refs[0]
    z, core = place()
    product, squares, routed = project(
        joined(mine), joined(twin), flip(z), core, gain_ref, router_ref, w_ref, slice(None)
    )
    n = product.shape[1]
    sums_out[:, 0:n] = sums_in[:, 0:n] + product
    sums_out[:, n : n + 128] = sums_in[:, n : n + 128] + squares
    sums_out[:, n + 128 : n + 256] = sums_in[:, n + 128 : n + 256] + routed


def more_part(mine, twin, staged, sums, rides, flip, flops, split=()):
    at = len(mine) + len(twin) + 3
    shapes = [arr((x.shape[0] // PIECES, x.shape[1]), x.dtype) for x in split for _ in range(PIECES)]
    return call(
        functools.partial(more_kernel, len(mine), len(twin), len(rides), flip, bool(split)),
        "more_part",
        (*mine, *twin, *staged, sums, *rides, *split),
        [arr(sums.shape, F32), *(arr(r.shape, r.dtype) for r in rides), *shapes],
        rides={at + i: i for i in range(1 + len(rides))},
        flops=flops,
    )


def turn(x, cos, sin):
    return x * cos + pltpu.roll(x, HEAD_SIZE // 2, 1) * sin


def kv_last_kernel(nq, at, n_mine, *refs):
    mine, twin, refs = joined(refs[:n_mine]), joined(refs[n_mine : 2 * n_mine]), refs[2 * n_mine :]
    gain_ref, router_ref, w_ref, sums, cos_ref, sin_ref, kv_out, stat_out = refs
    z, core = place()
    n, features = w_ref.shape[1], w_ref.shape[0]
    rows = slice(at, at + mine.shape[0])
    product, squares, routed = project(mine, twin, z ^ 2, core, gain_ref, router_ref, w_ref, slice(nq, n))
    squares = jnp.sum(sums[rows, n : n + 128] + squares, axis=1, keepdims=True)
    routed = jnp.sum(sums[rows, n + 128 : n + 256] + routed, axis=1, keepdims=True)
    inverse = lax.rsqrt(squares * (1.0 / features) + NORM_EPS)
    kv = (sums[rows, nq:n] + product) * inverse
    kv_out[:, 0:128] = turn(kv[:, 0:128], cos_ref[rows, :], sin_ref[rows, :]).astype(BF16)
    kv_out[:, 128:256] = kv[:, 128:256].astype(BF16)
    stat_out[:, 0:128] = jnp.broadcast_to(inverse, (inverse.shape[0], 128))
    gate_value = 1.0 / (1.0 + jnp.exp(-routed))
    stat_out[:, 128:256] = jnp.broadcast_to(gate_value, (gate_value.shape[0], 128))


def kv_last(at, pair, staged, sums, cos, sin, nq, flops):
    mine, twin = pair
    cap = sum(x.shape[0] for x in mine)
    return call(
        functools.partial(kv_last_kernel, nq, at, len(mine)),
        "kv_last",
        (*mine, *twin, *staged, sums, cos, sin),
        [arr((cap, 256), BF16), arr((cap, 256), F32)],
        flops=flops,
    )


def attend(q, kv, bias, carry):
    k, v = kv[:, 0:128], kv[:, 128:256]
    scale = LOG2E / HEAD_SIZE**0.5
    s = lax.dot_general(k, q, (((1,), (1,)), ((), ())), preferred_element_type=F32) * scale + bias
    top = jnp.max(s, axis=0, keepdims=True)
    if carry is not None:
        top = jnp.maximum(top, carry[0])
    e = jnp.exp2(s - top)
    total = jnp.sum(e, axis=0, keepdims=True)
    mix = lax.dot_general(v, e.astype(BF16), (((0,), (0,)), ((), ())), preferred_element_type=F32)
    if carry is not None:
        fade = jnp.exp2(carry[0] - top)
        total = total + carry[1] * fade
        mix = mix + carry[2] * fade
    return top, total, mix


def q_kernel(i, n_mine, n_kv, *refs):
    mine, twin, refs = joined(refs[:n_mine]), joined(refs[n_mine : 2 * n_mine]), refs[2 * n_mine :]
    gain_ref, w_ref, sums, stat_ref, cos_ref, sin_ref, bias_ref, *refs = refs
    kv_refs, (q_out, top_ref, total_ref, mix_ref) = refs[:n_kv], refs[n_kv:]
    z, core = place()
    half, nq = q_out.shape
    rows, keys = slice(i * half, (i + 1) * half), slice(0, (i + 1) * half)
    product, _, _ = project(
        mine, twin, z ^ 2, core, gain_ref, None, w_ref, slice(0, nq), stats=False
    )
    q = (sums[rows, 0:nq] + product) * stat_ref[:, 0:1]
    cos, sin, kv = cos_ref[rows, :], sin_ref[rows, :], joined(kv_refs)
    for h in range(nq // HEAD_SIZE):
        lanes = slice(h * HEAD_SIZE, (h + 1) * HEAD_SIZE)
        turned = turn(q[:, lanes], cos, sin).astype(BF16)
        q_out[:, lanes] = turned
        top, total, mix = attend(turned, kv, bias_ref[0, keys, rows], None)
        at = slice(h * half, (h + 1) * half)
        top_ref[:, at], total_ref[:, at], mix_ref[:, at] = top, total, mix


def carry_shapes(cap, nq):
    heads = nq // HEAD_SIZE
    return [arr((1, heads * cap), F32), arr((1, heads * cap), F32), arr((HEAD_SIZE, heads * cap), F32)]


def q_part(i, pair, staged, sums, stat, cos, sin, kvs, bias, nq, flops):
    mine, twin = pair
    half = stat.shape[0]
    return call(
        functools.partial(q_kernel, i, len(mine), len(kvs)),
        "q_part",
        (*mine, *twin, staged[0], staged[2], sums, stat, cos, sin, bias, *kvs),
        [arr((half, nq), BF16), *carry_shapes(half, nq)],
        flops=flops,
    )


def attend_kernel(step, first_key, n_carry, last, qa_ref, qb_ref, kv_ref, bias_ref, *refs):
    carries, outs = refs[: 3 * n_carry], refs[3 * n_carry :]
    half, nq = qa_ref.shape
    cap = 2 * half
    keys = slice(first_key, first_key + kv_ref.shape[0])
    for h in range(nq // HEAD_SIZE):
        lanes = slice(h * HEAD_SIZE, (h + 1) * HEAD_SIZE)
        at = slice(h * cap, (h + 1) * cap)
        part = slice(h * cap // n_carry, (h + 1) * cap // n_carry)
        carry = [
            jnp.concatenate([carries[j][:, part] for j in range(k, 3 * n_carry, 3)], axis=1) for k in range(3)
        ]
        q = jnp.concatenate([qa_ref[:, lanes], qb_ref[:, lanes]], axis=0)
        top, total, mix = attend(q, kv_ref[...], bias_ref[step, keys, :], carry)
        if not last:
            outs[0][:, at], outs[1][:, at], outs[2][:, at] = top, total, mix
            continue
        full, first, second = outs
        attn = jnp.transpose(mix * (1.0 / total)).astype(BF16)
        full[:, lanes] = attn
        first[:, lanes] = attn[:half]
        second[:, lanes] = attn[half:]


def attend_more(step, first_key, last, qs, kv, bias, carry, flops):
    half, nq = qs[0].shape
    cap = 2 * half
    shapes = [arr((cap, nq), BF16), arr((half, nq), BF16), arr((half, nq), BF16)]
    return call(
        functools.partial(attend_kernel, step, first_key, len(carry) // 3, last),
        "attend_more",
        (*qs, kv, bias, *carry),
        shapes if last else carry_shapes(cap, nq),
        flops=flops,
    )


def out_term(mine, twin, zz, core, w_ref):
    out = None
    for x, rows in halves(mine, twin, zz, core):
        out = add(out, jnp.dot(x, w_ref[rows, :], preferred_element_type=F32))
    return out


def out_own_kernel(n_mine, n_twin, *refs):
    mine, twin, refs = refs[:n_mine], refs[n_mine : n_mine + n_twin], refs[n_mine + n_twin :]
    n_ride = (len(refs) - 6) // 2
    w, hidden = refs[n_ride : n_ride + 2]
    total_ref, w_ref, hid_ref, sems = refs[-4:]
    z, core = place()
    copies = fetch([(w, w_ref), (hidden, hid_ref)], sems)
    copies[0].wait()
    total_ref[...] = out_term(joined(mine), joined(twin), z, core, w_ref)
    copies[1].wait()


def out_own(mine, twin, rides, w_out, hidden):
    cap = sum(x.shape[0] for x in mine)
    at = len(mine) + len(twin)
    return call(
        functools.partial(out_own_kernel, len(mine), len(twin)),
        "out_own",
        (*mine, *twin, *rides, w_out, hidden),
        [
            *(arr(r.shape, r.dtype) for r in rides),
            arr((cap, w_out.shape[1]), F32),
            arr(w_out.shape, BF16),
            arr(hidden.shape, BF16),
        ],
        scratch=[pltpu.SemaphoreType.DMA((2,))],
        rides={at + i: i for i in range(len(rides))},
        hbm=(w_out, hidden),
        flops=PART_COST,
    )


def out_more_kernel(n_mine, n_twin, flip, *refs):
    mine, twin, refs = refs[:n_mine], refs[n_mine : n_mine + n_twin], refs[n_mine + n_twin :]
    w_ref, total_in = refs[:2]
    total_out = refs[2 + (len(refs) - 3) // 2]
    z, core = place()
    total_out[...] = total_in[...] + out_term(joined(mine), joined(twin), flip(z), core, w_ref)


def out_more(mine, twin, w, total, rides, flip, flops):
    at = len(mine) + len(twin) + 1
    return call(
        functools.partial(out_more_kernel, len(mine), len(twin), flip),
        "out_more",
        (*mine, *twin, w, total, *rides),
        [arr(total.shape, F32), *(arr(r.shape, r.dtype) for r in rides)],
        rides={at + i: i for i in range(1 + len(rides))},
        flops=flops,
    )


def out_last_kernel(mine_ref, twin_ref, w_ref, total_ref, sa_ref, sb_ref, hot_ref, hid_ref, out, out_ref, sems):
    z, core = place()
    projected = total_ref[...] + out_term(mine_ref[...], twin_ref[...], z ^ 2, core, w_ref)
    gate = jnp.concatenate([sa_ref[:, 128:129], sb_ref[:, 128:129]], axis=0)
    update = (gate * projected).astype(BF16)
    block = 256
    copies = []
    for i in range(hid_ref.shape[0] // block):
        rows = slice(i * block, (i + 1) * block)
        placed = jnp.dot(hot_ref[rows, :], update, preferred_element_type=F32)
        out_ref[rows, :] = (hid_ref[rows, :].astype(F32) + placed).astype(BF16)
        copies += fetch([(out_ref.at[rows, :], out.at[rows, :])], sems, i)
    settle(copies)


def out_last(pair, w, total, stats, hot, hidden):
    return call(
        out_last_kernel,
        "out_last",
        (*pair, w, total, *stats, hot, hidden),
        [arr(hidden.shape, BF16)],
        scratch=[pltpu.VMEM(hidden.shape, BF16), pltpu.SemaphoreType.DMA((hidden.shape[0] // 256,))],
        out_hbm=True,
    )[0]


def angles(row_pos):
    half = HEAD_SIZE // 2
    frequency = ROPE_BASE ** (-(jnp.arange(half, dtype=F32) * 2.0 / HEAD_SIZE))
    turned = row_pos.astype(F32) * jnp.concatenate([frequency, frequency])[None, :]
    sign = jnp.concatenate([-jnp.ones((half,), F32), jnp.ones((half,), F32)])
    return jnp.cos(turned), jnp.sin(turned) * sign[None, :]


def body(
    size,
    hidden_in,
    norm_gain,
    router_weight,
    w_query,
    w_key,
    value_weight,
    w_out,
    keep_flags,
    keep_counts,
    keep_positions,
):
    shards = lax.axis_size("ctx")
    tok = hidden_in.shape[0]
    nq = w_query.shape[1]
    flags = keep_flags.reshape(-1, 128)
    weights = (norm_gain.reshape(1, -1), router_weight.reshape(1, -1), w_query, w_key, value_weight)

    full, first, second, rowpos = pick(keep_positions, hidden_in)
    held = {}

    def own(mine, mate):
        ride, held["sums"], *held["staged"], held["bias"], held["hot"] = own_part(
            *mine, *mate, weights, keep_counts, keep_positions, flags, tok
        )
        return ride

    def far(mine, twin, last):
        held["sums"], held["cos"], held["sin"], *pieces = more_part(
            mine, twin, held["staged"], held["sums"], angles(rowpos), lambda z: 3 - z, FAR_COST, (last,)
        )
        return tuple(pieces)

    def beside(mine, twin):
        (held["sums"],) = more_part(mine, twin, held["staged"], held["sums"], (), lambda z: z ^ 1, BESIDE_COST)

    pair, last_b, twin = spread_halves(size, full, first, second, own, far, beside)
    sums, staged, bias = held["sums"], held["staged"], held["bias"]
    cos, sin = held["cos"], held["sin"]
    half = first.shape[0]
    ring = [(s, (s + 1) % shards) for s in range(shards)]
    kvs, stats, pairs, qs, carry = [], [], [], [], []
    for i in range(2):
        if i == 1:
            kvs[0], last_b = gate(kvs[0], last_b)
            pair = (last_b,), (twin(last_b),)
        kv, stat = kv_last(i * half, pair, staged, sums, cos, sin, nq, KV_COST)
        kvs.append(kv)
        stats.append(stat)
        pairs.append(pair)
    moved = [lax.ppermute(kv, "ctx", ring) for kv in kvs]
    for i in range(2):
        q, *terms = q_part(
            i, pairs[i], staged, sums, stats[i], cos, sin, kvs[: i + 1], bias, nq, Q_COST if i else QA_COST
        )
        qs.append(q)
        carry += terms
    for step in range(1, shards):
        for i in range(2):
            last = step == shards - 1 and i == 1
            carry = attend_more(step, i * half, last, qs, moved[i], bias, carry, ATTEND_COST)
        if step < shards - 1:
            moved = [lax.ppermute(kv, "ctx", ring) for kv in moved]

    def own_out(mine, twin, rides):
        *rides, held["total"], held["w"], held["hidden"] = out_own(mine, twin, rides, w_out, hidden_in)
        return rides

    def far_out(mine, twin, rides):
        held["total"], *rides = out_more(mine, twin, held["w"], held["total"], rides, lambda z: 3 - z, PART_COST)
        return rides

    def beside_out(mine, twin):
        (held["total"],) = out_more(mine, twin, held["w"], held["total"], (), lambda z: z ^ 1, PART_COST)

    pair = spread(size, *carry, own_out, far_out, beside_out)
    return out_last(pair, held["w"], held["total"], stats, held["hot"], held["hidden"])


def solution(mesh):
    in_specs = (
        P(("groups", "ctx"), "heads"),
        P(),
        P(),
        P(None, "heads"),
        P(None, "heads"),
        P(None, "heads"),
        P(None, "heads"),
        P(("groups", "ctx")),
        P("groups"),
        P("groups", None),
    )
    out_specs = P(("groups", "ctx"), "heads")
    return jax.shard_map(
        functools.partial(body, mesh.shape["heads"]),
        mesh=mesh,
        in_specs=in_specs,
        out_specs=out_specs,
        check_vma=False,
    )
```

```python
import functools

import jax
import jax.numpy as jnp
from jax import lax
from jax.experimental import pallas as pl
from jax.experimental.pallas import tpu as pltpu
from jax.sharding import PartitionSpec as P

HEAD_SIZE = 128
ROPE_BASE = 500000.0
NORM_EPS = 1e-05
LOG2E = 1.4426950408889634
VMEM_LIMIT = 24 * 1024 * 1024
PIECES = 2
F32 = jnp.float32
BF16 = jnp.bfloat16
I32 = jnp.int32
COST = 400_000_000
PART_COST = 400_000_000
OWN_COST = 1_500_000_000
GATE_COST = 1_000_000
FAR_COST = 3_000_000_000
BESIDE_COST = 1_000_000
KV_COST = 1_000_000
Q_COST = 1_000_000
QA_COST = 1_000_000
ATTEND_COST = 400_000_000


VMEM = pl.BlockSpec(memory_space=pltpu.VMEM)
HBM = pl.BlockSpec(memory_space=pltpu.HBM)


def arr(shape, dtype):
    return jax.ShapeDtypeStruct(shape, dtype)


def call(kernel, name, operands, out_shape, scratch=(), rides=None, hbm=(), out_hbm=False, flops=COST):
    operands = [(o, any(o is h for h in hbm)) for o in operands]
    return pl.pallas_call(
        kernel,
        out_shape=out_shape,
        in_specs=[HBM if far else VMEM for _, far in operands],
        out_specs=[HBM if out_hbm else VMEM] * len(out_shape),
        scratch_shapes=list(scratch),
        input_output_aliases=rides or {},
        compiler_params=pltpu.CompilerParams(vmem_limit_bytes=VMEM_LIMIT),
        cost_estimate=pl.CostEstimate(flops=flops, bytes_accessed=1, transcendentals=0),
        name=name,
    )(*(pltpu.with_memory_space_constraint(o, pltpu.HBM) if far else o for o, far in operands))


def fetch(pairs, sems, base=0):
    copies = [pltpu.make_async_copy(src, dst, sems.at[base + i]) for i, (src, dst) in enumerate(pairs)]
    for copy in copies:
        copy.start()
    return copies


def place():
    d = lax.axis_index("heads")
    return d // 2, lax.rem(d, 2)


def live_row(pos_ref, cnt_ref, shard, dead):
    pos = pos_ref[pl.ds(shard, 1), :]
    slot = lax.broadcasted_iota(I32, pos.shape, 1)
    return jnp.where(slot < cnt_ref[shard], pos, dead)


def column(row):
    return jnp.transpose(jnp.broadcast_to(row, (128, row.shape[1])))


def pick_kernel(pos_hbm, hid_hbm, x_ref, xa_ref, xb_ref, rowpos_ref, pos_ref, hid_ref, sems):
    own, shards = lax.axis_index("ctx"), lax.axis_size("ctx")
    tok, cap = hid_ref.shape[0], x_ref.shape[0]
    pieces = [slice(at, at + 256) for at in range(0, tok, 256)]
    copies = fetch([(pos_hbm, pos_ref), *((hid_hbm.at[p, :], hid_ref.at[p, :]) for p in pieces)], sems)
    copies[0].wait()
    pos = column(pos_ref[pl.ds(own, 1), :])
    rowpos_ref[...] = jnp.where(pos < 0, shards * tok, pos)
    local = pos[:, :1] - own * tok
    total = None
    for piece, copy in zip(pieces, copies[1:]):
        at = lax.broadcasted_iota(I32, (cap, 256), 1) + piece.start
        hot = jnp.where(at == local, 1.0, 0.0).astype(BF16)
        copy.wait()
        total = add(total, jnp.dot(hot, hid_ref[piece, :], preferred_element_type=F32))
    x = total.astype(BF16)
    x_ref[...] = x
    xa_ref[...] = x[: cap // 2]
    xb_ref[...] = x[cap // 2 :]


def pick(positions, hidden):
    cap, width = positions.shape[1], hidden.shape[1]
    return call(
        pick_kernel,
        "pick",
        (positions, hidden),
        [arr((cap, width), BF16), arr((cap // 2, width), BF16), arr((cap // 2, width), BF16), arr((cap, 128), I32)],
        scratch=[
            pltpu.VMEM(positions.shape, I32),
            pltpu.VMEM(hidden.shape, BF16),
            pltpu.SemaphoreType.DMA((1 + hidden.shape[0] // 256,)),
        ],
        hbm=(positions, hidden),
    )


def sender(perm):
    return functools.partial(lax.ppermute, axis_name="heads", perm=perm)


def chip_sender(size, f):
    return sender([(2 * z + c, 2 * f(z) + c) for z in range(size // 2) for c in range(2)])


def gate(*rides):
    shapes = [arr(r.shape, r.dtype) for r in rides]
    return call(lambda *_: None, "gate", rides, shapes, rides={i: i for i in range(len(rides))}, flops=GATE_COST)


def spread(size, full, first, second, use_own, use_far, use_beside):
    cross = chip_sender(size, lambda z: 3 - z)
    near = chip_sender(size, lambda z: z ^ 1)
    twin = sender([(d, d ^ 1) for d in range(size)])
    far = cross(full)
    mates = twin(first), twin(second)
    beside = near(first), near(second)
    half = first.shape[0]
    last = near(far[:half]), near(far[half:])
    beside = use_own((full,), mates, beside)
    beside = use_far((far,), (twin(far),), beside)
    use_beside(beside, (twin(beside[0]), twin(beside[1])))
    return last, (twin(last[0]), twin(last[1]))


def spread_halves(size, full, first, second, use_own, use_far, use_beside):
    cross = chip_sender(size, lambda z: 3 - z)
    near = chip_sender(size, lambda z: z ^ 1)
    twin = sender([(d, d ^ 1) for d in range(size)])
    far = cross(first), cross(second)
    beside = near(use_own((full,), (twin(full),)))
    last_a, last_b = near(far[0]), near(far[1])
    last_a = use_far(far, (twin(far[0]), twin(far[1])), last_a)
    use_beside((beside,), (twin(beside),))
    return (last_a, tuple(twin(x) for x in last_a)), last_b, twin


def joined(refs):
    parts = [ref[...] for ref in refs]
    return parts[0] if len(parts) == 1 else jnp.concatenate(parts, axis=0)


def lanes_sum(x):
    total = x[:, :128]
    for at in range(128, x.shape[1], 128):
        total = total + x[:, at : at + 128]
    return total


def halves(mine, twin, zz, core):
    width = mine.shape[1]
    rows = [pl.ds(pl.multiple_of((2 * zz + at) * width, width), width) for at in (core, 1 - core)]
    return zip((mine, twin), rows)


def add(a, b):
    return b if a is None else a + b


def project(mine, twin, zz, core, gain_ref, router_ref, w_ref, columns, stats=True):
    product = squares = routed = None
    for x, rows in halves(mine, twin, zz, core):
        xf = x.astype(F32)
        gained = (xf * gain_ref[:, rows]).astype(BF16)
        product = add(product, jnp.dot(gained, w_ref[rows, columns], preferred_element_type=F32))
        if stats:
            squares = add(squares, lanes_sum(xf * xf))
            routed = add(routed, lanes_sum(xf * router_ref[:, rows]))
    return product, squares, routed


def settle(copies):
    for copy in copies:
        copy.wait()


def own_kernel(x_ref, twin_ref, gain, router, wq, wk, wv, cnt, pos, flag, *refs):
    _, sums_ref, gain_ref, router_ref, w_ref, bias_ref, hot_ref, sems = refs[:8]
    z, core = place()
    nq, nk, depth = wq.shape[1], wk.shape[1], wq.shape[0]
    lanes = ((wq, slice(0, nq)), (wk, slice(nq, nq + nk)), (wv, slice(nq + nk, nq + 2 * nk)))
    block = 2 * x_ref.shape[1]
    blocks = depth // block
    vectors = fetch([(gain, gain_ref), (router, router_ref)], sems, 3 * blocks)
    copies = []
    for i in range(blocks):
        rows = pl.ds(pl.multiple_of((z ^ i) * block, block), block)
        copies.append(fetch([(w.at[rows, :], w_ref.at[rows, at]) for w, at in lanes], sems, 3 * i))
    settle(vectors)
    settle(copies[0])
    product, squares, routed = project(x_ref[...], twin_ref[...], z, core, gain_ref, router_ref, w_ref, slice(None))
    n = product.shape[1]
    sums_ref[:, 0:n] = product
    sums_ref[:, n : n + 128] = squares
    sums_ref[:, n + 128 : n + 256] = routed
    masks_kernel(cnt, pos, flag, bias_ref, hot_ref, *refs[8:])
    for later in copies[1:]:
        settle(later)


def own_part(full, twin, weights, counts, positions, flags, tok):
    cap, width = full.shape
    depth = weights[2].shape[0]
    columns = sum(w.shape[1] for w in weights[2:])
    shards = positions.shape[0]
    return call(
        own_kernel,
        "own_part",
        (full, twin, *weights, counts, positions, flags),
        [
            arr(full.shape, BF16),
            arr((cap, columns + 256), F32),
            arr((1, depth), F32),
            arr((1, depth), F32),
            arr((depth, columns), BF16),
            arr((shards, cap, cap), F32),
            arr((tok, cap), BF16),
        ],
        scratch=[
            pltpu.SemaphoreType.DMA((3 * depth // (2 * width) + 2,)),
            pltpu.SMEM(counts.shape, I32),
            pltpu.VMEM(positions.shape, I32),
            pltpu.VMEM(flags.shape, I32),
            pltpu.SemaphoreType.DMA((3,)),
        ],
        rides={0: 0},
        hbm=(*weights, counts, positions, flags),
        flops=OWN_COST,
    )


def masks_kernel(cnt_hbm, pos_hbm, flag_hbm, bias_ref, hot_ref, cnt_ref, pos_ref, flag_ref, sems):
    settle(fetch([(cnt_hbm, cnt_ref), (pos_hbm, pos_ref), (flag_hbm, flag_ref)], sems))
    own, shards = lax.axis_index("ctx"), lax.axis_size("ctx")
    tok = hot_ref.shape[0]
    seq = shards * tok
    row = live_row(pos_ref, cnt_ref, own, seq)
    for step in range(shards):
        source = lax.rem(own + shards - step, shards)
        keys = column(live_row(pos_ref, cnt_ref, source, seq + 1))[:, :1]
        bias_ref[step] = jnp.where(keys <= row, 0.0, -jnp.inf).astype(F32)
    flags = jnp.transpose(flag_ref[...].astype(F32))
    local = row - own * tok
    for r in range(tok // 128):
        at = lax.broadcasted_iota(I32, (128, row.shape[1]), 0) + r * 128
        hot = jnp.where(at == local, flags[:, r : r + 1], 0.0)
        hot_ref[r * 128 : (r + 1) * 128, :] = hot.astype(BF16)


def more_kernel(n_mine, n_twin, n_ride, flip, split, *refs):
    mine, twin, refs = refs[:n_mine], refs[n_mine : n_mine + n_twin], refs[n_mine + n_twin :]
    gain_ref, router_ref, w_ref, sums_in = refs[:4]
    refs = refs[4 + n_ride :]
    if split:
        whole_ref, refs = refs[0], refs[1:]
        pieces = refs[1 + n_ride :]
        for i, piece in enumerate(pieces):
            piece[...] = whole_ref[i * piece.shape[0] : (i + 1) * piece.shape[0], :]
    sums_out = refs[0]
    z, core = place()
    product, squares, routed = project(
        joined(mine), joined(twin), flip(z), core, gain_ref, router_ref, w_ref, slice(None)
    )
    n = product.shape[1]
    sums_out[:, 0:n] = sums_in[:, 0:n] + product
    sums_out[:, n : n + 128] = sums_in[:, n : n + 128] + squares
    sums_out[:, n + 128 : n + 256] = sums_in[:, n + 128 : n + 256] + routed


def more_part(mine, twin, staged, sums, rides, flip, flops, split=()):
    at = len(mine) + len(twin) + 3
    shapes = [arr((x.shape[0] // PIECES, x.shape[1]), x.dtype) for x in split for _ in range(PIECES)]
    return call(
        functools.partial(more_kernel, len(mine), len(twin), len(rides), flip, bool(split)),
        "more_part",
        (*mine, *twin, *staged, sums, *rides, *split),
        [arr(sums.shape, F32), *(arr(r.shape, r.dtype) for r in rides), *shapes],
        rides={at + i: i for i in range(1 + len(rides))},
        flops=flops,
    )


def turn(x, cos, sin):
    return x * cos + pltpu.roll(x, HEAD_SIZE // 2, 1) * sin


def kv_last_kernel(nq, at, n_mine, *refs):
    mine, twin, refs = joined(refs[:n_mine]), joined(refs[n_mine : 2 * n_mine]), refs[2 * n_mine :]
    gain_ref, router_ref, w_ref, sums, cos_ref, sin_ref, kv_out, stat_out = refs
    z, core = place()
    n, features = w_ref.shape[1], w_ref.shape[0]
    rows = slice(at, at + mine.shape[0])
    product, squares, routed = project(mine, twin, z ^ 2, core, gain_ref, router_ref, w_ref, slice(nq, n))
    squares = jnp.sum(sums[rows, n : n + 128] + squares, axis=1, keepdims=True)
    routed = jnp.sum(sums[rows, n + 128 : n + 256] + routed, axis=1, keepdims=True)
    inverse = lax.rsqrt(squares * (1.0 / features) + NORM_EPS)
    kv = (sums[rows, nq:n] + product) * inverse
    kv_out[:, 0:128] = turn(kv[:, 0:128], cos_ref[rows, :], sin_ref[rows, :]).astype(BF16)
    kv_out[:, 128:256] = kv[:, 128:256].astype(BF16)
    stat_out[:, 0:128] = jnp.broadcast_to(inverse, (inverse.shape[0], 128))
    gate_value = 1.0 / (1.0 + jnp.exp(-routed))
    stat_out[:, 128:256] = jnp.broadcast_to(gate_value, (gate_value.shape[0], 128))


def kv_last(at, pair, staged, sums, cos, sin, nq, flops):
    mine, twin = pair
    cap = sum(x.shape[0] for x in mine)
    return call(
        functools.partial(kv_last_kernel, nq, at, len(mine)),
        "kv_last",
        (*mine, *twin, *staged, sums, cos, sin),
        [arr((cap, 256), BF16), arr((cap, 256), F32)],
        flops=flops,
    )


def attend(q, kv, bias, carry):
    k, v = kv[:, 0:128], kv[:, 128:256]
    scale = LOG2E / HEAD_SIZE**0.5
    s = lax.dot_general(k, q, (((1,), (1,)), ((), ())), preferred_element_type=F32) * scale + bias
    top = jnp.max(s, axis=0, keepdims=True)
    if carry is not None:
        top = jnp.maximum(top, carry[0])
    e = jnp.exp2(s - top)
    total = jnp.sum(e, axis=0, keepdims=True)
    mix = lax.dot_general(v, e.astype(BF16), (((0,), (0,)), ((), ())), preferred_element_type=F32)
    if carry is not None:
        fade = jnp.exp2(carry[0] - top)
        total = total + carry[1] * fade
        mix = mix + carry[2] * fade
    return top, total, mix


def q_kernel(i, n_mine, n_kv, *refs):
    mine, twin, refs = joined(refs[:n_mine]), joined(refs[n_mine : 2 * n_mine]), refs[2 * n_mine :]
    gain_ref, w_ref, sums, stat_ref, cos_ref, sin_ref, bias_ref, *refs = refs
    kv_refs, (q_out, top_ref, total_ref, mix_ref) = refs[:n_kv], refs[n_kv:]
    z, core = place()
    half, nq = q_out.shape
    rows, keys = slice(i * half, (i + 1) * half), slice(0, (i + 1) * half)
    product, _, _ = project(
        mine, twin, z ^ 2, core, gain_ref, None, w_ref, slice(0, nq), stats=False
    )
    q = (sums[rows, 0:nq] + product) * stat_ref[:, 0:1]
    cos, sin, kv = cos_ref[rows, :], sin_ref[rows, :], joined(kv_refs)
    for h in range(nq // HEAD_SIZE):
        lanes = slice(h * HEAD_SIZE, (h + 1) * HEAD_SIZE)
        turned = turn(q[:, lanes], cos, sin).astype(BF16)
        q_out[:, lanes] = turned
        top, total, mix = attend(turned, kv, bias_ref[0, keys, rows], None)
        at = slice(h * half, (h + 1) * half)
        top_ref[:, at], total_ref[:, at], mix_ref[:, at] = top, total, mix


def carry_shapes(cap, nq):
    heads = nq // HEAD_SIZE
    return [arr((1, heads * cap), F32), arr((1, heads * cap), F32), arr((HEAD_SIZE, heads * cap), F32)]


def q_part(i, pair, staged, sums, stat, cos, sin, kvs, bias, nq, flops):
    mine, twin = pair
    half = stat.shape[0]
    return call(
        functools.partial(q_kernel, i, len(mine), len(kvs)),
        "q_part",
        (*mine, *twin, staged[0], staged[2], sums, stat, cos, sin, bias, *kvs),
        [arr((half, nq), BF16), *carry_shapes(half, nq)],
        flops=flops,
    )


def attend_kernel(step, first_key, n_carry, last, qa_ref, qb_ref, kv_ref, bias_ref, *refs):
    carries, outs = refs[: 3 * n_carry], refs[3 * n_carry :]
    half, nq = qa_ref.shape
    cap = 2 * half
    keys = slice(first_key, first_key + kv_ref.shape[0])
    for h in range(nq // HEAD_SIZE):
        lanes = slice(h * HEAD_SIZE, (h + 1) * HEAD_SIZE)
        at = slice(h * cap, (h + 1) * cap)
        part = slice(h * cap // n_carry, (h + 1) * cap // n_carry)
        carry = [
            jnp.concatenate([carries[j][:, part] for j in range(k, 3 * n_carry, 3)], axis=1) for k in range(3)
        ]
        q = jnp.concatenate([qa_ref[:, lanes], qb_ref[:, lanes]], axis=0)
        top, total, mix = attend(q, kv_ref[...], bias_ref[step, keys, :], carry)
        if not last:
            outs[0][:, at], outs[1][:, at], outs[2][:, at] = top, total, mix
            continue
        full, first, second = outs
        attn = jnp.transpose(mix * (1.0 / total)).astype(BF16)
        full[:, lanes] = attn
        first[:, lanes] = attn[:half]
        second[:, lanes] = attn[half:]


def attend_more(step, first_key, last, qs, kv, bias, carry, flops):
    half, nq = qs[0].shape
    cap = 2 * half
    shapes = [arr((cap, nq), BF16), arr((half, nq), BF16), arr((half, nq), BF16)]
    return call(
        functools.partial(attend_kernel, step, first_key, len(carry) // 3, last),
        "attend_more",
        (*qs, kv, bias, *carry),
        shapes if last else carry_shapes(cap, nq),
        flops=flops,
    )


def out_term(mine, twin, zz, core, w_ref):
    out = None
    for x, rows in halves(mine, twin, zz, core):
        out = add(out, jnp.dot(x, w_ref[rows, :], preferred_element_type=F32))
    return out


def out_own_kernel(n_mine, n_twin, *refs):
    mine, twin, refs = refs[:n_mine], refs[n_mine : n_mine + n_twin], refs[n_mine + n_twin :]
    n_ride = (len(refs) - 6) // 2
    w, hidden = refs[n_ride : n_ride + 2]
    total_ref, w_ref, hid_ref, sems = refs[-4:]
    z, core = place()
    copies = fetch([(w, w_ref), (hidden, hid_ref)], sems)
    copies[0].wait()
    total_ref[...] = out_term(joined(mine), joined(twin), z, core, w_ref)
    copies[1].wait()


def out_own(mine, twin, rides, w_out, hidden):
    cap = sum(x.shape[0] for x in mine)
    at = len(mine) + len(twin)
    return call(
        functools.partial(out_own_kernel, len(mine), len(twin)),
        "out_own",
        (*mine, *twin, *rides, w_out, hidden),
        [
            *(arr(r.shape, r.dtype) for r in rides),
            arr((cap, w_out.shape[1]), F32),
            arr(w_out.shape, BF16),
            arr(hidden.shape, BF16),
        ],
        scratch=[pltpu.SemaphoreType.DMA((2,))],
        rides={at + i: i for i in range(len(rides))},
        hbm=(w_out, hidden),
        flops=PART_COST,
    )


def out_more_kernel(n_mine, n_twin, flip, *refs):
    mine, twin, refs = refs[:n_mine], refs[n_mine : n_mine + n_twin], refs[n_mine + n_twin :]
    w_ref, total_in = refs[:2]
    total_out = refs[2 + (len(refs) - 3) // 2]
    z, core = place()
    total_out[...] = total_in[...] + out_term(joined(mine), joined(twin), flip(z), core, w_ref)


def out_more(mine, twin, w, total, rides, flip, flops):
    at = len(mine) + len(twin) + 1
    return call(
        functools.partial(out_more_kernel, len(mine), len(twin), flip),
        "out_more",
        (*mine, *twin, w, total, *rides),
        [arr(total.shape, F32), *(arr(r.shape, r.dtype) for r in rides)],
        rides={at + i: i for i in range(1 + len(rides))},
        flops=flops,
    )


def out_last_kernel(a, b, c, d, w_ref, total_ref, sa_ref, sb_ref, hot_ref, hid_ref, out, out_ref, sems):
    z, core = place()
    projected = total_ref[...] + out_term(joined((a, b)), joined((c, d)), z ^ 2, core, w_ref)
    gate = jnp.concatenate([sa_ref[:, 128:129], sb_ref[:, 128:129]], axis=0)
    update = (gate * projected).astype(BF16)
    block = 256
    copies = []
    for i in range(hid_ref.shape[0] // block):
        rows = slice(i * block, (i + 1) * block)
        placed = jnp.dot(hot_ref[rows, :], update, preferred_element_type=F32)
        out_ref[rows, :] = (hid_ref[rows, :].astype(F32) + placed).astype(BF16)
        copies += fetch([(out_ref.at[rows, :], out.at[rows, :])], sems, i)
    settle(copies)


def out_last(pair, w, total, stats, hot, hidden):
    return call(
        out_last_kernel,
        "out_last",
        (*pair[0], *pair[1], w, total, *stats, hot, hidden),
        [arr(hidden.shape, BF16)],
        scratch=[pltpu.VMEM(hidden.shape, BF16), pltpu.SemaphoreType.DMA((hidden.shape[0] // 256,))],
        out_hbm=True,
    )[0]


def angles(row_pos):
    half = HEAD_SIZE // 2
    frequency = ROPE_BASE ** (-(jnp.arange(half, dtype=F32) * 2.0 / HEAD_SIZE))
    turned = row_pos.astype(F32) * jnp.concatenate([frequency, frequency])[None, :]
    sign = jnp.concatenate([-jnp.ones((half,), F32), jnp.ones((half,), F32)])
    return jnp.cos(turned), jnp.sin(turned) * sign[None, :]


def body(
    size,
    hidden_in,
    norm_gain,
    router_weight,
    w_query,
    w_key,
    value_weight,
    w_out,
    keep_flags,
    keep_counts,
    keep_positions,
):
    shards = lax.axis_size("ctx")
    tok = hidden_in.shape[0]
    nq = w_query.shape[1]
    flags = keep_flags.reshape(-1, 128)
    weights = (norm_gain.reshape(1, -1), router_weight.reshape(1, -1), w_query, w_key, value_weight)

    full, first, second, rowpos = pick(keep_positions, hidden_in)
    held = {}

    def own(mine, mate):
        ride, held["sums"], *held["staged"], held["bias"], held["hot"] = own_part(
            *mine, *mate, weights, keep_counts, keep_positions, flags, tok
        )
        return ride

    def far(mine, twin, last):
        held["sums"], held["cos"], held["sin"], *pieces = more_part(
            mine, twin, held["staged"], held["sums"], angles(rowpos), lambda z: 3 - z, FAR_COST, (last,)
        )
        return tuple(pieces)

    def beside(mine, twin):
        (held["sums"],) = more_part(mine, twin, held["staged"], held["sums"], (), lambda z: z ^ 1, BESIDE_COST)

    pair, last_b, twin = spread_halves(size, full, first, second, own, far, beside)
    sums, staged, bias = held["sums"], held["staged"], held["bias"]
    cos, sin = held["cos"], held["sin"]
    half = first.shape[0]
    ring = [(s, (s + 1) % shards) for s in range(shards)]
    kvs, stats, pairs, qs, carry = [], [], [], [], []
    for i in range(2):
        if i == 1:
            kvs[0], last_b = gate(kvs[0], last_b)
            pair = (last_b,), (twin(last_b),)
        kv, stat = kv_last(i * half, pair, staged, sums, cos, sin, nq, KV_COST)
        kvs.append(kv)
        stats.append(stat)
        pairs.append(pair)
    moved = [lax.ppermute(kv, "ctx", ring) for kv in kvs]
    for i in range(2):
        q, *terms = q_part(
            i, pairs[i], staged, sums, stats[i], cos, sin, kvs[: i + 1], bias, nq, Q_COST if i else QA_COST
        )
        qs.append(q)
        carry += terms
    for step in range(1, shards):
        for i in range(2):
            last = step == shards - 1 and i == 1
            carry = attend_more(step, i * half, last, qs, moved[i], bias, carry, ATTEND_COST)
        if step < shards - 1:
            moved = [lax.ppermute(kv, "ctx", ring) for kv in moved]

    def own_out(mine, twin, rides):
        *rides, held["total"], held["w"], held["hidden"] = out_own(mine, twin, rides, w_out, hidden_in)
        return rides

    def far_out(mine, twin, rides):
        held["total"], *rides = out_more(mine, twin, held["w"], held["total"], rides, lambda z: 3 - z, PART_COST)
        return rides

    def beside_out(mine, twin):
        (held["total"],) = out_more(mine, twin, held["w"], held["total"], (), lambda z: z ^ 1, PART_COST)

    pair = spread(size, *carry, own_out, far_out, beside_out)
    return out_last(pair, held["w"], held["total"], stats, held["hot"], held["hidden"])


def solution(mesh):
    in_specs = (
        P(("groups", "ctx"), "heads"),
        P(),
        P(),
        P(None, "heads"),
        P(None, "heads"),
        P(None, "heads"),
        P(None, "heads"),
        P(("groups", "ctx")),
        P("groups"),
        P("groups", None),
    )
    out_specs = P(("groups", "ctx"), "heads")
    return jax.shard_map(
        functools.partial(body, mesh.shape["heads"]),
        mesh=mesh,
        in_specs=in_specs,
        out_specs=out_specs,
        check_vma=False,
    )
```

```python
import functools

import jax
import jax.numpy as jnp
from jax import lax
from jax.experimental import pallas as pl
from jax.experimental.pallas import tpu as pltpu
from jax.sharding import PartitionSpec as P

HEAD_SIZE = 128
ROPE_BASE = 500000.0
NORM_EPS = 1e-05
LOG2E = 1.4426950408889634
VMEM_LIMIT = 24 * 1024 * 1024
PIECES = 2
F32 = jnp.float32
BF16 = jnp.bfloat16
I32 = jnp.int32
COST = 400_000_000
PART_COST = 400_000_000
OWN_COST = 1_500_000_000
GATE_COST = 1_000_000
FAR_COST = 3_000_000_000
BESIDE_COST = 1_000_000
KV_COST = 1_000_000
Q_COST = 1_000_000
QA_COST = 1_000_000
ATTEND_COST = 400_000_000


VMEM = pl.BlockSpec(memory_space=pltpu.VMEM)
HBM = pl.BlockSpec(memory_space=pltpu.HBM)


def arr(shape, dtype):
    return jax.ShapeDtypeStruct(shape, dtype)


def call(kernel, name, operands, out_shape, scratch=(), rides=None, hbm=(), out_hbm=False, flops=COST):
    operands = [(o, any(o is h for h in hbm)) for o in operands]
    return pl.pallas_call(
        kernel,
        out_shape=out_shape,
        in_specs=[HBM if far else VMEM for _, far in operands],
        out_specs=[HBM if out_hbm else VMEM] * len(out_shape),
        scratch_shapes=list(scratch),
        input_output_aliases=rides or {},
        compiler_params=pltpu.CompilerParams(vmem_limit_bytes=VMEM_LIMIT),
        cost_estimate=pl.CostEstimate(flops=flops, bytes_accessed=1, transcendentals=0),
        name=name,
    )(*(pltpu.with_memory_space_constraint(o, pltpu.HBM) if far else o for o, far in operands))


def fetch(pairs, sems, base=0):
    copies = [pltpu.make_async_copy(src, dst, sems.at[base + i]) for i, (src, dst) in enumerate(pairs)]
    for copy in copies:
        copy.start()
    return copies


def place():
    d = lax.axis_index("heads")
    return d // 2, lax.rem(d, 2)


def live_row(pos_ref, cnt_ref, shard, dead):
    pos = pos_ref[pl.ds(shard, 1), :]
    slot = lax.broadcasted_iota(I32, pos.shape, 1)
    return jnp.where(slot < cnt_ref[shard], pos, dead)


def column(row):
    return jnp.transpose(jnp.broadcast_to(row, (128, row.shape[1])))


def pick_kernel(pos_hbm, hid_hbm, x_ref, xa_ref, xb_ref, rowpos_ref, pos_ref, hid_ref, sems):
    own, shards = lax.axis_index("ctx"), lax.axis_size("ctx")
    tok, cap = hid_ref.shape[0], x_ref.shape[0]
    pieces = [slice(at, at + 256) for at in range(0, tok, 256)]
    copies = fetch([(pos_hbm, pos_ref), *((hid_hbm.at[p, :], hid_ref.at[p, :]) for p in pieces)], sems)
    copies[0].wait()
    pos = column(pos_ref[pl.ds(own, 1), :])
    rowpos_ref[...] = jnp.where(pos < 0, shards * tok, pos)
    local = pos[:, :1] - own * tok
    total = None
    for piece, copy in zip(pieces, copies[1:]):
        at = lax.broadcasted_iota(I32, (cap, 256), 1) + piece.start
        hot = jnp.where(at == local, 1.0, 0.0).astype(BF16)
        copy.wait()
        total = add(total, jnp.dot(hot, hid_ref[piece, :], preferred_element_type=F32))
    x = total.astype(BF16)
    x_ref[...] = x
    xa_ref[...] = x[: cap // 2]
    xb_ref[...] = x[cap // 2 :]


def pick(positions, hidden):
    cap, width = positions.shape[1], hidden.shape[1]
    return call(
        pick_kernel,
        "pick",
        (positions, hidden),
        [arr((cap, width), BF16), arr((cap // 2, width), BF16), arr((cap // 2, width), BF16), arr((cap, 128), I32)],
        scratch=[
            pltpu.VMEM(positions.shape, I32),
            pltpu.VMEM(hidden.shape, BF16),
            pltpu.SemaphoreType.DMA((1 + hidden.shape[0] // 256,)),
        ],
        hbm=(positions, hidden),
    )


def sender(perm):
    return functools.partial(lax.ppermute, axis_name="heads", perm=perm)


def chip_sender(size, f):
    return sender([(2 * z + c, 2 * f(z) + c) for z in range(size // 2) for c in range(2)])


def gate(*rides):
    shapes = [arr(r.shape, r.dtype) for r in rides]
    return call(lambda *_: None, "gate", rides, shapes, rides={i: i for i in range(len(rides))}, flops=GATE_COST)


def spread(size, full, first, second, use_own, use_far, use_beside):
    cross = chip_sender(size, lambda z: 3 - z)
    near = chip_sender(size, lambda z: z ^ 1)
    twin = sender([(d, d ^ 1) for d in range(size)])
    far = cross(full)
    mates = twin(first), twin(second)
    beside = near(first), near(second)
    half = first.shape[0]
    last = near(far[:half]), near(far[half:])
    beside = use_own((full,), mates, beside)
    beside = use_far((far,), (twin(far),), beside)
    use_beside(beside, (twin(beside[0]), twin(beside[1])), last, twin(last[0]))
    return twin(last[1])


def spread_halves(size, full, first, second, use_own, use_far, use_beside):
    cross = chip_sender(size, lambda z: 3 - z)
    near = chip_sender(size, lambda z: z ^ 1)
    twin = sender([(d, d ^ 1) for d in range(size)])
    far = cross(first), cross(second)
    beside = near(use_own((full,), (twin(full),)))
    last_a, last_b = near(far[0]), near(far[1])
    last_a = use_far(far, (twin(far[0]), twin(far[1])), last_a)
    use_beside((beside,), (twin(beside),))
    return (last_a, tuple(twin(x) for x in last_a)), last_b, twin


def joined(refs):
    parts = [ref[...] for ref in refs]
    return parts[0] if len(parts) == 1 else jnp.concatenate(parts, axis=0)


def lanes_sum(x):
    total = x[:, :128]
    for at in range(128, x.shape[1], 128):
        total = total + x[:, at : at + 128]
    return total


def halves(mine, twin, zz, core):
    width = mine.shape[1]
    rows = [pl.ds(pl.multiple_of((2 * zz + at) * width, width), width) for at in (core, 1 - core)]
    return zip((mine, twin), rows)


def add(a, b):
    return b if a is None else a + b


def project(mine, twin, zz, core, gain_ref, router_ref, w_ref, columns, stats=True):
    product = squares = routed = None
    for x, rows in halves(mine, twin, zz, core):
        xf = x.astype(F32)
        gained = (xf * gain_ref[:, rows]).astype(BF16)
        product = add(product, jnp.dot(gained, w_ref[rows, columns], preferred_element_type=F32))
        if stats:
            squares = add(squares, lanes_sum(xf * xf))
            routed = add(routed, lanes_sum(xf * router_ref[:, rows]))
    return product, squares, routed


def settle(copies):
    for copy in copies:
        copy.wait()


def own_kernel(x_ref, twin_ref, gain, router, wq, wk, wv, cnt, pos, flag, *refs):
    _, sums_ref, gain_ref, router_ref, w_ref, bias_ref, hot_ref, sems = refs[:8]
    z, core = place()
    nq, nk, depth = wq.shape[1], wk.shape[1], wq.shape[0]
    lanes = ((wq, slice(0, nq)), (wk, slice(nq, nq + nk)), (wv, slice(nq + nk, nq + 2 * nk)))
    block = 2 * x_ref.shape[1]
    blocks = depth // block
    vectors = fetch([(gain, gain_ref), (router, router_ref)], sems, 3 * blocks)
    copies = []
    for i in range(blocks):
        rows = pl.ds(pl.multiple_of((z ^ i) * block, block), block)
        copies.append(fetch([(w.at[rows, :], w_ref.at[rows, at]) for w, at in lanes], sems, 3 * i))
    settle(vectors)
    settle(copies[0])
    product, squares, routed = project(x_ref[...], twin_ref[...], z, core, gain_ref, router_ref, w_ref, slice(None))
    n = product.shape[1]
    sums_ref[:, 0:n] = product
    sums_ref[:, n : n + 128] = squares
    sums_ref[:, n + 128 : n + 256] = routed
    masks_kernel(cnt, pos, flag, bias_ref, hot_ref, *refs[8:])
    for later in copies[1:]:
        settle(later)


def own_part(full, twin, weights, counts, positions, flags, tok):
    cap, width = full.shape
    depth = weights[2].shape[0]
    columns = sum(w.shape[1] for w in weights[2:])
    shards = positions.shape[0]
    return call(
        own_kernel,
        "own_part",
        (full, twin, *weights, counts, positions, flags),
        [
            arr(full.shape, BF16),
            arr((cap, columns + 256), F32),
            arr((1, depth), F32),
            arr((1, depth), F32),
            arr((depth, columns), BF16),
            arr((shards, cap, cap), F32),
            arr((tok, cap), BF16),
        ],
        scratch=[
            pltpu.SemaphoreType.DMA((3 * depth // (2 * width) + 2,)),
            pltpu.SMEM(counts.shape, I32),
            pltpu.VMEM(positions.shape, I32),
            pltpu.VMEM(flags.shape, I32),
            pltpu.SemaphoreType.DMA((3,)),
        ],
        rides={0: 0},
        hbm=(*weights, counts, positions, flags),
        flops=OWN_COST,
    )


def masks_kernel(cnt_hbm, pos_hbm, flag_hbm, bias_ref, hot_ref, cnt_ref, pos_ref, flag_ref, sems):
    settle(fetch([(cnt_hbm, cnt_ref), (pos_hbm, pos_ref), (flag_hbm, flag_ref)], sems))
    own, shards = lax.axis_index("ctx"), lax.axis_size("ctx")
    tok = hot_ref.shape[0]
    seq = shards * tok
    row = live_row(pos_ref, cnt_ref, own, seq)
    for step in range(shards):
        source = lax.rem(own + shards - step, shards)
        keys = column(live_row(pos_ref, cnt_ref, source, seq + 1))[:, :1]
        bias_ref[step] = jnp.where(keys <= row, 0.0, -jnp.inf).astype(F32)
    flags = jnp.transpose(flag_ref[...].astype(F32))
    local = row - own * tok
    for r in range(tok // 128):
        at = lax.broadcasted_iota(I32, (128, row.shape[1]), 0) + r * 128
        hot = jnp.where(at == local, flags[:, r : r + 1], 0.0)
        hot_ref[r * 128 : (r + 1) * 128, :] = hot.astype(BF16)


def more_kernel(n_mine, n_twin, n_ride, flip, split, *refs):
    mine, twin, refs = refs[:n_mine], refs[n_mine : n_mine + n_twin], refs[n_mine + n_twin :]
    gain_ref, router_ref, w_ref, sums_in = refs[:4]
    refs = refs[4 + n_ride :]
    if split:
        whole_ref, refs = refs[0], refs[1:]
        pieces = refs[1 + n_ride :]
        for i, piece in enumerate(pieces):
            piece[...] = whole_ref[i * piece.shape[0] : (i + 1) * piece.shape[0], :]
    sums_out = refs[0]
    z, core = place()
    product, squares, routed = project(
        joined(mine), joined(twin), flip(z), core, gain_ref, router_ref, w_ref, slice(None)
    )
    n = product.shape[1]
    sums_out[:, 0:n] = sums_in[:, 0:n] + product
    sums_out[:, n : n + 128] = sums_in[:, n : n + 128] + squares
    sums_out[:, n + 128 : n + 256] = sums_in[:, n + 128 : n + 256] + routed


def more_part(mine, twin, staged, sums, rides, flip, flops, split=()):
    at = len(mine) + len(twin) + 3
    shapes = [arr((x.shape[0] // PIECES, x.shape[1]), x.dtype) for x in split for _ in range(PIECES)]
    return call(
        functools.partial(more_kernel, len(mine), len(twin), len(rides), flip, bool(split)),
        "more_part",
        (*mine, *twin, *staged, sums, *rides, *split),
        [arr(sums.shape, F32), *(arr(r.shape, r.dtype) for r in rides), *shapes],
        rides={at + i: i for i in range(1 + len(rides))},
        flops=flops,
    )


def turn(x, cos, sin):
    return x * cos + pltpu.roll(x, HEAD_SIZE // 2, 1) * sin


def kv_last_kernel(nq, at, n_mine, *refs):
    mine, twin, refs = joined(refs[:n_mine]), joined(refs[n_mine : 2 * n_mine]), refs[2 * n_mine :]
    gain_ref, router_ref, w_ref, sums, cos_ref, sin_ref, kv_out, stat_out = refs
    z, core = place()
    n, features = w_ref.shape[1], w_ref.shape[0]
    rows = slice(at, at + mine.shape[0])
    product, squares, routed = project(mine, twin, z ^ 2, core, gain_ref, router_ref, w_ref, slice(nq, n))
    squares = jnp.sum(sums[rows, n : n + 128] + squares, axis=1, keepdims=True)
    routed = jnp.sum(sums[rows, n + 128 : n + 256] + routed, axis=1, keepdims=True)
    inverse = lax.rsqrt(squares * (1.0 / features) + NORM_EPS)
    kv = (sums[rows, nq:n] + product) * inverse
    kv_out[:, 0:128] = turn(kv[:, 0:128], cos_ref[rows, :], sin_ref[rows, :]).astype(BF16)
    kv_out[:, 128:256] = kv[:, 128:256].astype(BF16)
    stat_out[:, 0:128] = jnp.broadcast_to(inverse, (inverse.shape[0], 128))
    gate_value = 1.0 / (1.0 + jnp.exp(-routed))
    stat_out[:, 128:256] = jnp.broadcast_to(gate_value, (gate_value.shape[0], 128))


def kv_last(at, pair, staged, sums, cos, sin, nq, flops):
    mine, twin = pair
    cap = sum(x.shape[0] for x in mine)
    return call(
        functools.partial(kv_last_kernel, nq, at, len(mine)),
        "kv_last",
        (*mine, *twin, *staged, sums, cos, sin),
        [arr((cap, 256), BF16), arr((cap, 256), F32)],
        flops=flops,
    )


def attend(q, kv, bias, carry):
    k, v = kv[:, 0:128], kv[:, 128:256]
    scale = LOG2E / HEAD_SIZE**0.5
    s = lax.dot_general(k, q, (((1,), (1,)), ((), ())), preferred_element_type=F32) * scale + bias
    top = jnp.max(s, axis=0, keepdims=True)
    if carry is not None:
        top = jnp.maximum(top, carry[0])
    e = jnp.exp2(s - top)
    total = jnp.sum(e, axis=0, keepdims=True)
    mix = lax.dot_general(v, e.astype(BF16), (((0,), (0,)), ((), ())), preferred_element_type=F32)
    if carry is not None:
        fade = jnp.exp2(carry[0] - top)
        total = total + carry[1] * fade
        mix = mix + carry[2] * fade
    return top, total, mix


def q_kernel(i, n_mine, n_kv, *refs):
    mine, twin, refs = joined(refs[:n_mine]), joined(refs[n_mine : 2 * n_mine]), refs[2 * n_mine :]
    gain_ref, w_ref, sums, stat_ref, cos_ref, sin_ref, bias_ref, *refs = refs
    kv_refs, (q_out, top_ref, total_ref, mix_ref) = refs[:n_kv], refs[n_kv:]
    z, core = place()
    half, nq = q_out.shape
    rows, keys = slice(i * half, (i + 1) * half), slice(0, (i + 1) * half)
    product, _, _ = project(
        mine, twin, z ^ 2, core, gain_ref, None, w_ref, slice(0, nq), stats=False
    )
    q = (sums[rows, 0:nq] + product) * stat_ref[:, 0:1]
    cos, sin, kv = cos_ref[rows, :], sin_ref[rows, :], joined(kv_refs)
    for h in range(nq // HEAD_SIZE):
        lanes = slice(h * HEAD_SIZE, (h + 1) * HEAD_SIZE)
        turned = turn(q[:, lanes], cos, sin).astype(BF16)
        q_out[:, lanes] = turned
        top, total, mix = attend(turned, kv, bias_ref[0, keys, rows], None)
        at = slice(h * half, (h + 1) * half)
        top_ref[:, at], total_ref[:, at], mix_ref[:, at] = top, total, mix


def carry_shapes(cap, nq):
    heads = nq // HEAD_SIZE
    return [arr((1, heads * cap), F32), arr((1, heads * cap), F32), arr((HEAD_SIZE, heads * cap), F32)]


def q_part(i, pair, staged, sums, stat, cos, sin, kvs, bias, nq, flops):
    mine, twin = pair
    half = stat.shape[0]
    return call(
        functools.partial(q_kernel, i, len(mine), len(kvs)),
        "q_part",
        (*mine, *twin, staged[0], staged[2], sums, stat, cos, sin, bias, *kvs),
        [arr((half, nq), BF16), *carry_shapes(half, nq)],
        flops=flops,
    )


def attend_kernel(step, first_key, n_carry, last, qa_ref, qb_ref, kv_ref, bias_ref, *refs):
    carries, outs = refs[: 3 * n_carry], refs[3 * n_carry :]
    half, nq = qa_ref.shape
    cap = 2 * half
    keys = slice(first_key, first_key + kv_ref.shape[0])
    for h in range(nq // HEAD_SIZE):
        lanes = slice(h * HEAD_SIZE, (h + 1) * HEAD_SIZE)
        at = slice(h * cap, (h + 1) * cap)
        part = slice(h * cap // n_carry, (h + 1) * cap // n_carry)
        carry = [
            jnp.concatenate([carries[j][:, part] for j in range(k, 3 * n_carry, 3)], axis=1) for k in range(3)
        ]
        q = jnp.concatenate([qa_ref[:, lanes], qb_ref[:, lanes]], axis=0)
        top, total, mix = attend(q, kv_ref[...], bias_ref[step, keys, :], carry)
        if not last:
            outs[0][:, at], outs[1][:, at], outs[2][:, at] = top, total, mix
            continue
        full, first, second = outs
        attn = jnp.transpose(mix * (1.0 / total)).astype(BF16)
        full[:, lanes] = attn
        first[:, lanes] = attn[:half]
        second[:, lanes] = attn[half:]


def attend_more(step, first_key, last, qs, kv, bias, carry, flops):
    half, nq = qs[0].shape
    cap = 2 * half
    shapes = [arr((cap, nq), BF16), arr((half, nq), BF16), arr((half, nq), BF16)]
    return call(
        functools.partial(attend_kernel, step, first_key, len(carry) // 3, last),
        "attend_more",
        (*qs, kv, bias, *carry),
        shapes if last else carry_shapes(cap, nq),
        flops=flops,
    )


def out_term(mine, twin, zz, core, w_ref):
    out = None
    for x, rows in halves(mine, twin, zz, core):
        out = add(out, jnp.dot(x, w_ref[rows, :], preferred_element_type=F32))
    return out


def out_own_kernel(n_mine, n_twin, *refs):
    mine, twin, refs = refs[:n_mine], refs[n_mine : n_mine + n_twin], refs[n_mine + n_twin :]
    n_ride = (len(refs) - 6) // 2
    w, hidden = refs[n_ride : n_ride + 2]
    total_ref, w_ref, hid_ref, sems = refs[-4:]
    z, core = place()
    copies = fetch([(w, w_ref), (hidden, hid_ref)], sems)
    copies[0].wait()
    total_ref[...] = out_term(joined(mine), joined(twin), z, core, w_ref)
    copies[1].wait()


def out_own(mine, twin, rides, w_out, hidden):
    cap = sum(x.shape[0] for x in mine)
    at = len(mine) + len(twin)
    return call(
        functools.partial(out_own_kernel, len(mine), len(twin)),
        "out_own",
        (*mine, *twin, *rides, w_out, hidden),
        [
            *(arr(r.shape, r.dtype) for r in rides),
            arr((cap, w_out.shape[1]), F32),
            arr(w_out.shape, BF16),
            arr(hidden.shape, BF16),
        ],
        scratch=[pltpu.SemaphoreType.DMA((2,))],
        rides={at + i: i for i in range(len(rides))},
        hbm=(w_out, hidden),
        flops=PART_COST,
    )


def out_more_kernel(n_mine, n_twin, flip, *refs):
    mine, twin, refs = refs[:n_mine], refs[n_mine : n_mine + n_twin], refs[n_mine + n_twin :]
    w_ref, total_in = refs[:2]
    total_out = refs[2 + (len(refs) - 3) // 2]
    z, core = place()
    total_out[...] = total_in[...] + out_term(joined(mine), joined(twin), flip(z), core, w_ref)


def out_more(mine, twin, w, total, rides, flip, flops):
    at = len(mine) + len(twin) + 1
    return call(
        functools.partial(out_more_kernel, len(mine), len(twin), flip),
        "out_more",
        (*mine, *twin, w, total, *rides),
        [arr(total.shape, F32), *(arr(r.shape, r.dtype) for r in rides)],
        rides={at + i: i for i in range(1 + len(rides))},
        flops=flops,
    )


def out_beside_kernel(a, b, c, d, last_a, last_b, last_twin, w_ref, total_in, total_out):
    z, core = place()
    half = last_a.shape[0]
    last, twin = (rows for _, rows in halves(last_a, last_b, z ^ 2, core))
    total = total_in[...] + out_term(joined((a, b)), joined((c, d)), z ^ 1, core, w_ref)
    total = total + jnp.dot(joined((last_a, last_b)), w_ref[last, :], preferred_element_type=F32)
    total_out[:half] = total[:half] + jnp.dot(last_twin[...], w_ref[twin, :], preferred_element_type=F32)
    total_out[half:] = total[half:]


def out_beside(mine, twin, last, last_twin, w, total, flops):
    return call(
        out_beside_kernel,
        "out_beside",
        (*mine, *twin, *last, last_twin, w, total),
        [arr(total.shape, F32)],
        rides={8: 0},
        flops=flops,
    )[0]


def out_last_kernel(twin_ref, w_ref, total_ref, sa_ref, sb_ref, hot_ref, hid_ref, out, out_ref, sems):
    z, core = place()
    half, width = twin_ref.shape
    rows = pl.ds(pl.multiple_of((2 * (z ^ 2) + 1 - core) * width, width), width)
    top = sa_ref[:, 128:129] * total_ref[:half]
    rest = total_ref[half:] + jnp.dot(twin_ref[...], w_ref[rows, :], preferred_element_type=F32)
    update = jnp.concatenate([top.astype(BF16), (sb_ref[:, 128:129] * rest).astype(BF16)], axis=0)
    block = 256
    copies = []
    for i in range(hid_ref.shape[0] // block):
        rows = slice(i * block, (i + 1) * block)
        placed = jnp.dot(hot_ref[rows, :], update, preferred_element_type=F32)
        out_ref[rows, :] = (hid_ref[rows, :].astype(F32) + placed).astype(BF16)
        copies += fetch([(out_ref.at[rows, :], out.at[rows, :])], sems, i)
    settle(copies)


def out_last(twin, w, total, stats, hot, hidden):
    return call(
        out_last_kernel,
        "out_last",
        (twin, w, total, *stats, hot, hidden),
        [arr(hidden.shape, BF16)],
        scratch=[pltpu.VMEM(hidden.shape, BF16), pltpu.SemaphoreType.DMA((hidden.shape[0] // 256,))],
        out_hbm=True,
    )[0]


def angles(row_pos):
    half = HEAD_SIZE // 2
    frequency = ROPE_BASE ** (-(jnp.arange(half, dtype=F32) * 2.0 / HEAD_SIZE))
    turned = row_pos.astype(F32) * jnp.concatenate([frequency, frequency])[None, :]
    sign = jnp.concatenate([-jnp.ones((half,), F32), jnp.ones((half,), F32)])
    return jnp.cos(turned), jnp.sin(turned) * sign[None, :]


def body(
    size,
    hidden_in,
    norm_gain,
    router_weight,
    w_query,
    w_key,
    value_weight,
    w_out,
    keep_flags,
    keep_counts,
    keep_positions,
):
    shards = lax.axis_size("ctx")
    tok = hidden_in.shape[0]
    nq = w_query.shape[1]
    flags = keep_flags.reshape(-1, 128)
    weights = (norm_gain.reshape(1, -1), router_weight.reshape(1, -1), w_query, w_key, value_weight)

    full, first, second, rowpos = pick(keep_positions, hidden_in)
    held = {}

    def own(mine, mate):
        ride, held["sums"], *held["staged"], held["bias"], held["hot"] = own_part(
            *mine, *mate, weights, keep_counts, keep_positions, flags, tok
        )
        return ride

    def far(mine, twin, last):
        held["sums"], held["cos"], held["sin"], *pieces = more_part(
            mine, twin, held["staged"], held["sums"], angles(rowpos), lambda z: 3 - z, FAR_COST, (last,)
        )
        return tuple(pieces)

    def beside(mine, twin):
        (held["sums"],) = more_part(mine, twin, held["staged"], held["sums"], (), lambda z: z ^ 1, BESIDE_COST)

    pair, last_b, twin = spread_halves(size, full, first, second, own, far, beside)
    sums, staged, bias = held["sums"], held["staged"], held["bias"]
    cos, sin = held["cos"], held["sin"]
    half = first.shape[0]
    ring = [(s, (s + 1) % shards) for s in range(shards)]
    kvs, stats, pairs, qs, carry = [], [], [], [], []
    for i in range(2):
        if i == 1:
            kvs[0], last_b = gate(kvs[0], last_b)
            pair = (last_b,), (twin(last_b),)
        kv, stat = kv_last(i * half, pair, staged, sums, cos, sin, nq, KV_COST)
        kvs.append(kv)
        stats.append(stat)
        pairs.append(pair)
    moved = [lax.ppermute(kv, "ctx", ring) for kv in kvs]
    for i in range(2):
        q, *terms = q_part(
            i, pairs[i], staged, sums, stats[i], cos, sin, kvs[: i + 1], bias, nq, Q_COST if i else QA_COST
        )
        qs.append(q)
        carry += terms
    for step in range(1, shards):
        for i in range(2):
            last = step == shards - 1 and i == 1
            carry = attend_more(step, i * half, last, qs, moved[i], bias, carry, ATTEND_COST)
        if step < shards - 1:
            moved = [lax.ppermute(kv, "ctx", ring) for kv in moved]

    def own_out(mine, twin, rides):
        *rides, held["total"], held["w"], held["hidden"] = out_own(mine, twin, rides, w_out, hidden_in)
        return rides

    def far_out(mine, twin, rides):
        held["total"], *rides = out_more(mine, twin, held["w"], held["total"], rides, lambda z: 3 - z, PART_COST)
        return rides

    def beside_out(mine, twin, last, last_twin):
        held["total"] = out_beside(mine, twin, last, last_twin, held["w"], held["total"], PART_COST)

    twin = spread(size, *carry, own_out, far_out, beside_out)
    return out_last(twin, held["w"], held["total"], stats, held["hot"], held["hidden"])


def solution(mesh):
    in_specs = (
        P(("groups", "ctx"), "heads"),
        P(),
        P(),
        P(None, "heads"),
        P(None, "heads"),
        P(None, "heads"),
        P(None, "heads"),
        P(("groups", "ctx")),
        P("groups"),
        P("groups", None),
    )
    out_specs = P(("groups", "ctx"), "heads")
    return jax.shard_map(
        functools.partial(body, mesh.shape["heads"]),
        mesh=mesh,
        in_specs=in_specs,
        out_specs=out_specs,
        check_vma=False,
    )
```

```python
import functools

import jax
import jax.numpy as jnp
from jax import lax
from jax.experimental import pallas as pl
from jax.experimental.pallas import tpu as pltpu
from jax.sharding import PartitionSpec as P

HEAD_SIZE = 128
ROPE_BASE = 500000.0
NORM_EPS = 1e-05
LOG2E = 1.4426950408889634
VMEM_LIMIT = 24 * 1024 * 1024
PIECES = 2
F32 = jnp.float32
BF16 = jnp.bfloat16
I32 = jnp.int32
COST = 400_000_000
PART_COST = 400_000_000
OWN_COST = 1_500_000_000
GATE_COST = 1_000_000
FAR_COST = 3_000_000_000
BESIDE_COST = 1_000_000
KV_COST = 1_000_000
Q_COST = 1_000_000
QA_COST = 1_000_000
ATTEND_COST = 400_000_000


VMEM = pl.BlockSpec(memory_space=pltpu.VMEM)
HBM = pl.BlockSpec(memory_space=pltpu.HBM)


def arr(shape, dtype):
    return jax.ShapeDtypeStruct(shape, dtype)


def call(kernel, name, operands, out_shape, scratch=(), rides=None, hbm=(), out_hbm=False, flops=COST):
    operands = [(o, any(o is h for h in hbm)) for o in operands]
    return pl.pallas_call(
        kernel,
        out_shape=out_shape,
        in_specs=[HBM if far else VMEM for _, far in operands],
        out_specs=[HBM if out_hbm else VMEM] * len(out_shape),
        scratch_shapes=list(scratch),
        input_output_aliases=rides or {},
        compiler_params=pltpu.CompilerParams(vmem_limit_bytes=VMEM_LIMIT),
        cost_estimate=pl.CostEstimate(flops=flops, bytes_accessed=1, transcendentals=0),
        name=name,
    )(*(pltpu.with_memory_space_constraint(o, pltpu.HBM) if far else o for o, far in operands))


def fetch(pairs, sems, base=0):
    copies = [pltpu.make_async_copy(src, dst, sems.at[base + i]) for i, (src, dst) in enumerate(pairs)]
    for copy in copies:
        copy.start()
    return copies


def place():
    d = lax.axis_index("heads")
    return d // 2, lax.rem(d, 2)


def live_row(pos_ref, cnt_ref, shard, dead):
    pos = pos_ref[pl.ds(shard, 1), :]
    slot = lax.broadcasted_iota(I32, pos.shape, 1)
    return jnp.where(slot < cnt_ref[shard], pos, dead)


def column(row):
    return jnp.transpose(jnp.broadcast_to(row, (128, row.shape[1])))


def pick_kernel(pos_hbm, hid_hbm, x_ref, xa_ref, xb_ref, rowpos_ref, pos_ref, hid_ref, sems):
    own, shards = lax.axis_index("ctx"), lax.axis_size("ctx")
    tok, cap = hid_ref.shape[0], x_ref.shape[0]
    pieces = [slice(at, at + 256) for at in range(0, tok, 256)]
    copies = fetch([(pos_hbm, pos_ref), *((hid_hbm.at[p, :], hid_ref.at[p, :]) for p in pieces)], sems)
    copies[0].wait()
    pos = column(pos_ref[pl.ds(own, 1), :])
    rowpos_ref[...] = jnp.where(pos < 0, shards * tok, pos)
    local = pos[:, :1] - own * tok
    total = None
    for piece, copy in zip(pieces, copies[1:]):
        at = lax.broadcasted_iota(I32, (cap, 256), 1) + piece.start
        hot = jnp.where(at == local, 1.0, 0.0).astype(BF16)
        copy.wait()
        total = add(total, jnp.dot(hot, hid_ref[piece, :], preferred_element_type=F32))
    x = total.astype(BF16)
    x_ref[...] = x
    xa_ref[...] = x[: cap // 2]
    xb_ref[...] = x[cap // 2 :]


def pick(positions, hidden):
    cap, width = positions.shape[1], hidden.shape[1]
    return call(
        pick_kernel,
        "pick",
        (positions, hidden),
        [arr((cap, width), BF16), arr((cap // 2, width), BF16), arr((cap // 2, width), BF16), arr((cap, 128), I32)],
        scratch=[
            pltpu.VMEM(positions.shape, I32),
            pltpu.VMEM(hidden.shape, BF16),
            pltpu.SemaphoreType.DMA((1 + hidden.shape[0] // 256,)),
        ],
        hbm=(positions, hidden),
    )


def sender(perm):
    return functools.partial(lax.ppermute, axis_name="heads", perm=perm)


def chip_sender(size, f):
    return sender([(2 * z + c, 2 * f(z) + c) for z in range(size // 2) for c in range(2)])


def gate(*rides):
    shapes = [arr(r.shape, r.dtype) for r in rides]
    return call(lambda *_: None, "gate", rides, shapes, rides={i: i for i in range(len(rides))}, flops=GATE_COST)


def spread(size, full, first, second, use_own, use_far, use_beside):
    cross = chip_sender(size, lambda z: z ^ 2)
    near = chip_sender(size, lambda z: z ^ 1)
    twin = sender([(d, d ^ 1) for d in range(size)])
    far = cross(full)
    mates = twin(first), twin(second)
    beside = near(first), near(second)
    half = first.shape[0]
    last = near(far[:half]), near(far[half:])
    beside = use_own((full,), mates, beside)
    beside = use_far((far,), (twin(far),), beside)
    use_beside(beside, (twin(beside[0]), twin(beside[1])), last, twin(last[0]))
    return twin(last[1])


def spread_halves(size, full, first, second, use_own, use_far, use_beside):
    cross = chip_sender(size, lambda z: z ^ 2)
    near = chip_sender(size, lambda z: z ^ 1)
    twin = sender([(d, d ^ 1) for d in range(size)])
    far = cross(first), cross(second)
    beside = near(use_own((full,), (twin(full),)))
    last_a, last_b = near(far[0]), near(far[1])
    last_a = use_far(far, (twin(far[0]), twin(far[1])), last_a)
    use_beside((beside,), (twin(beside),))
    return (last_a, tuple(twin(x) for x in last_a)), last_b, twin


def joined(refs):
    parts = [ref[...] for ref in refs]
    return parts[0] if len(parts) == 1 else jnp.concatenate(parts, axis=0)


def lanes_sum(x):
    total = x[:, :128]
    for at in range(128, x.shape[1], 128):
        total = total + x[:, at : at + 128]
    return total


def halves(mine, twin, zz, core):
    width = mine.shape[1]
    rows = [pl.ds(pl.multiple_of((2 * zz + at) * width, width), width) for at in (core, 1 - core)]
    return zip((mine, twin), rows)


def add(a, b):
    return b if a is None else a + b


def project(mine, twin, zz, core, gain_ref, router_ref, w_ref, columns, stats=True):
    product = squares = routed = None
    for x, rows in halves(mine, twin, zz, core):
        xf = x.astype(F32)
        gained = (xf * gain_ref[:, rows]).astype(BF16)
        product = add(product, jnp.dot(gained, w_ref[rows, columns], preferred_element_type=F32))
        if stats:
            squares = add(squares, lanes_sum(xf * xf))
            routed = add(routed, lanes_sum(xf * router_ref[:, rows]))
    return product, squares, routed


def settle(copies):
    for copy in copies:
        copy.wait()


def own_kernel(x_ref, twin_ref, gain, router, wq, wk, wv, cnt, pos, flag, *refs):
    _, sums_ref, gain_ref, router_ref, w_ref, bias_ref, hot_ref, sems = refs[:8]
    z, core = place()
    nq, nk, depth = wq.shape[1], wk.shape[1], wq.shape[0]
    lanes = ((wq, slice(0, nq)), (wk, slice(nq, nq + nk)), (wv, slice(nq + nk, nq + 2 * nk)))
    block = 2 * x_ref.shape[1]
    blocks = depth // block
    vectors = fetch([(gain, gain_ref), (router, router_ref)], sems, 3 * blocks)
    copies = []
    for i in range(blocks):
        rows = pl.ds(pl.multiple_of((z ^ i) * block, block), block)
        copies.append(fetch([(w.at[rows, :], w_ref.at[rows, at]) for w, at in lanes], sems, 3 * i))
    settle(vectors)
    settle(copies[0])
    product, squares, routed = project(x_ref[...], twin_ref[...], z, core, gain_ref, router_ref, w_ref, slice(None))
    n = product.shape[1]
    sums_ref[:, 0:n] = product
    sums_ref[:, n : n + 128] = squares
    sums_ref[:, n + 128 : n + 256] = routed
    masks_kernel(cnt, pos, flag, bias_ref, hot_ref, *refs[8:])
    for later in copies[1:]:
        settle(later)


def own_part(full, twin, weights, counts, positions, flags, tok):
    cap, width = full.shape
    depth = weights[2].shape[0]
    columns = sum(w.shape[1] for w in weights[2:])
    shards = positions.shape[0]
    return call(
        own_kernel,
        "own_part",
        (full, twin, *weights, counts, positions, flags),
        [
            arr(full.shape, BF16),
            arr((cap, columns + 256), F32),
            arr((1, depth), F32),
            arr((1, depth), F32),
            arr((depth, columns), BF16),
            arr((shards, cap, cap), F32),
            arr((tok, cap), BF16),
        ],
        scratch=[
            pltpu.SemaphoreType.DMA((3 * depth // (2 * width) + 2,)),
            pltpu.SMEM(counts.shape, I32),
            pltpu.VMEM(positions.shape, I32),
            pltpu.VMEM(flags.shape, I32),
            pltpu.SemaphoreType.DMA((3,)),
        ],
        rides={0: 0},
        hbm=(*weights, counts, positions, flags),
        flops=OWN_COST,
    )


def masks_kernel(cnt_hbm, pos_hbm, flag_hbm, bias_ref, hot_ref, cnt_ref, pos_ref, flag_ref, sems):
    settle(fetch([(cnt_hbm, cnt_ref), (pos_hbm, pos_ref), (flag_hbm, flag_ref)], sems))
    own, shards = lax.axis_index("ctx"), lax.axis_size("ctx")
    tok = hot_ref.shape[0]
    seq = shards * tok
    row = live_row(pos_ref, cnt_ref, own, seq)
    for step in range(shards):
        source = lax.rem(own + shards - step, shards)
        keys = column(live_row(pos_ref, cnt_ref, source, seq + 1))[:, :1]
        bias_ref[step] = jnp.where(keys <= row, 0.0, -jnp.inf).astype(F32)
    flags = jnp.transpose(flag_ref[...].astype(F32))
    local = row - own * tok
    for r in range(tok // 128):
        at = lax.broadcasted_iota(I32, (128, row.shape[1]), 0) + r * 128
        hot = jnp.where(at == local, flags[:, r : r + 1], 0.0)
        hot_ref[r * 128 : (r + 1) * 128, :] = hot.astype(BF16)


def more_kernel(n_mine, n_twin, n_ride, flip, split, *refs):
    mine, twin, refs = refs[:n_mine], refs[n_mine : n_mine + n_twin], refs[n_mine + n_twin :]
    gain_ref, router_ref, w_ref, sums_in = refs[:4]
    refs = refs[4 + n_ride :]
    if split:
        whole_ref, refs = refs[0], refs[1:]
        pieces = refs[1 + n_ride :]
        for i, piece in enumerate(pieces):
            piece[...] = whole_ref[i * piece.shape[0] : (i + 1) * piece.shape[0], :]
    sums_out = refs[0]
    z, core = place()
    product, squares, routed = project(
        joined(mine), joined(twin), flip(z), core, gain_ref, router_ref, w_ref, slice(None)
    )
    n = product.shape[1]
    sums_out[:, 0:n] = sums_in[:, 0:n] + product
    sums_out[:, n : n + 128] = sums_in[:, n : n + 128] + squares
    sums_out[:, n + 128 : n + 256] = sums_in[:, n + 128 : n + 256] + routed


def more_part(mine, twin, staged, sums, rides, flip, flops, split=()):
    at = len(mine) + len(twin) + 3
    shapes = [arr((x.shape[0] // PIECES, x.shape[1]), x.dtype) for x in split for _ in range(PIECES)]
    return call(
        functools.partial(more_kernel, len(mine), len(twin), len(rides), flip, bool(split)),
        "more_part",
        (*mine, *twin, *staged, sums, *rides, *split),
        [arr(sums.shape, F32), *(arr(r.shape, r.dtype) for r in rides), *shapes],
        rides={at + i: i for i in range(1 + len(rides))},
        flops=flops,
    )


def turn(x, cos, sin):
    return x * cos + pltpu.roll(x, HEAD_SIZE // 2, 1) * sin


def kv_last_kernel(nq, at, n_mine, *refs):
    mine, twin, refs = joined(refs[:n_mine]), joined(refs[n_mine : 2 * n_mine]), refs[2 * n_mine :]
    gain_ref, router_ref, w_ref, sums, cos_ref, sin_ref, kv_out, stat_out = refs
    z, core = place()
    n, features = w_ref.shape[1], w_ref.shape[0]
    rows = slice(at, at + mine.shape[0])
    product, squares, routed = project(mine, twin, 3 - z, core, gain_ref, router_ref, w_ref, slice(nq, n))
    squares = jnp.sum(sums[rows, n : n + 128] + squares, axis=1, keepdims=True)
    routed = jnp.sum(sums[rows, n + 128 : n + 256] + routed, axis=1, keepdims=True)
    inverse = lax.rsqrt(squares * (1.0 / features) + NORM_EPS)
    kv = (sums[rows, nq:n] + product) * inverse
    kv_out[:, 0:128] = turn(kv[:, 0:128], cos_ref[rows, :], sin_ref[rows, :]).astype(BF16)
    kv_out[:, 128:256] = kv[:, 128:256].astype(BF16)
    stat_out[:, 0:128] = jnp.broadcast_to(inverse, (inverse.shape[0], 128))
    gate_value = 1.0 / (1.0 + jnp.exp(-routed))
    stat_out[:, 128:256] = jnp.broadcast_to(gate_value, (gate_value.shape[0], 128))


def kv_last(at, pair, staged, sums, cos, sin, nq, flops):
    mine, twin = pair
    cap = sum(x.shape[0] for x in mine)
    return call(
        functools.partial(kv_last_kernel, nq, at, len(mine)),
        "kv_last",
        (*mine, *twin, *staged, sums, cos, sin),
        [arr((cap, 256), BF16), arr((cap, 256), F32)],
        flops=flops,
    )


def attend(q, kv, bias, carry):
    k, v = kv[:, 0:128], kv[:, 128:256]
    scale = LOG2E / HEAD_SIZE**0.5
    s = lax.dot_general(k, q, (((1,), (1,)), ((), ())), preferred_element_type=F32) * scale + bias
    top = jnp.max(s, axis=0, keepdims=True)
    if carry is not None:
        top = jnp.maximum(top, carry[0])
    e = jnp.exp2(s - top)
    total = jnp.sum(e, axis=0, keepdims=True)
    mix = lax.dot_general(v, e.astype(BF16), (((0,), (0,)), ((), ())), preferred_element_type=F32)
    if carry is not None:
        fade = jnp.exp2(carry[0] - top)
        total = total + carry[1] * fade
        mix = mix + carry[2] * fade
    return top, total, mix


def q_kernel(i, n_mine, n_kv, *refs):
    mine, twin, refs = joined(refs[:n_mine]), joined(refs[n_mine : 2 * n_mine]), refs[2 * n_mine :]
    gain_ref, w_ref, sums, stat_ref, cos_ref, sin_ref, bias_ref, *refs = refs
    kv_refs, (q_out, top_ref, total_ref, mix_ref) = refs[:n_kv], refs[n_kv:]
    z, core = place()
    half, nq = q_out.shape
    rows, keys = slice(i * half, (i + 1) * half), slice(0, (i + 1) * half)
    product, _, _ = project(
        mine, twin, 3 - z, core, gain_ref, None, w_ref, slice(0, nq), stats=False
    )
    q = (sums[rows, 0:nq] + product) * stat_ref[:, 0:1]
    cos, sin, kv = cos_ref[rows, :], sin_ref[rows, :], joined(kv_refs)
    for h in range(nq // HEAD_SIZE):
        lanes = slice(h * HEAD_SIZE, (h + 1) * HEAD_SIZE)
        turned = turn(q[:, lanes], cos, sin).astype(BF16)
        q_out[:, lanes] = turned
        top, total, mix = attend(turned, kv, bias_ref[0, keys, rows], None)
        at = slice(h * half, (h + 1) * half)
        top_ref[:, at], total_ref[:, at], mix_ref[:, at] = top, total, mix


def carry_shapes(cap, nq):
    heads = nq // HEAD_SIZE
    return [arr((1, heads * cap), F32), arr((1, heads * cap), F32), arr((HEAD_SIZE, heads * cap), F32)]


def q_part(i, pair, staged, sums, stat, cos, sin, kvs, bias, nq, flops):
    mine, twin = pair
    half = stat.shape[0]
    return call(
        functools.partial(q_kernel, i, len(mine), len(kvs)),
        "q_part",
        (*mine, *twin, staged[0], staged[2], sums, stat, cos, sin, bias, *kvs),
        [arr((half, nq), BF16), *carry_shapes(half, nq)],
        flops=flops,
    )


def attend_kernel(step, first_key, n_carry, last, qa_ref, qb_ref, kv_ref, bias_ref, *refs):
    carries, outs = refs[: 3 * n_carry], refs[3 * n_carry :]
    half, nq = qa_ref.shape
    cap = 2 * half
    keys = slice(first_key, first_key + kv_ref.shape[0])
    for h in range(nq // HEAD_SIZE):
        lanes = slice(h * HEAD_SIZE, (h + 1) * HEAD_SIZE)
        at = slice(h * cap, (h + 1) * cap)
        part = slice(h * cap // n_carry, (h + 1) * cap // n_carry)
        carry = [
            jnp.concatenate([carries[j][:, part] for j in range(k, 3 * n_carry, 3)], axis=1) for k in range(3)
        ]
        q = jnp.concatenate([qa_ref[:, lanes], qb_ref[:, lanes]], axis=0)
        top, total, mix = attend(q, kv_ref[...], bias_ref[step, keys, :], carry)
        if not last:
            outs[0][:, at], outs[1][:, at], outs[2][:, at] = top, total, mix
            continue
        full, first, second = outs
        attn = jnp.transpose(mix * (1.0 / total)).astype(BF16)
        full[:, lanes] = attn
        first[:, lanes] = attn[:half]
        second[:, lanes] = attn[half:]


def attend_more(step, first_key, last, qs, kv, bias, carry, flops):
    half, nq = qs[0].shape
    cap = 2 * half
    shapes = [arr((cap, nq), BF16), arr((half, nq), BF16), arr((half, nq), BF16)]
    return call(
        functools.partial(attend_kernel, step, first_key, len(carry) // 3, last),
        "attend_more",
        (*qs, kv, bias, *carry),
        shapes if last else carry_shapes(cap, nq),
        flops=flops,
    )


def out_term(mine, twin, zz, core, w_ref):
    out = None
    for x, rows in halves(mine, twin, zz, core):
        out = add(out, jnp.dot(x, w_ref[rows, :], preferred_element_type=F32))
    return out


def out_own_kernel(n_mine, n_twin, *refs):
    mine, twin, refs = refs[:n_mine], refs[n_mine : n_mine + n_twin], refs[n_mine + n_twin :]
    n_ride = (len(refs) - 6) // 2
    w, hidden = refs[n_ride : n_ride + 2]
    total_ref, w_ref, hid_ref, sems = refs[-4:]
    z, core = place()
    copies = fetch([(w, w_ref), (hidden, hid_ref)], sems)
    copies[0].wait()
    total_ref[...] = out_term(joined(mine), joined(twin), z, core, w_ref)
    copies[1].wait()


def out_own(mine, twin, rides, w_out, hidden):
    cap = sum(x.shape[0] for x in mine)
    at = len(mine) + len(twin)
    return call(
        functools.partial(out_own_kernel, len(mine), len(twin)),
        "out_own",
        (*mine, *twin, *rides, w_out, hidden),
        [
            *(arr(r.shape, r.dtype) for r in rides),
            arr((cap, w_out.shape[1]), F32),
            arr(w_out.shape, BF16),
            arr(hidden.shape, BF16),
        ],
        scratch=[pltpu.SemaphoreType.DMA((2,))],
        rides={at + i: i for i in range(len(rides))},
        hbm=(w_out, hidden),
        flops=PART_COST,
    )


def out_more_kernel(n_mine, n_twin, flip, *refs):
    mine, twin, refs = refs[:n_mine], refs[n_mine : n_mine + n_twin], refs[n_mine + n_twin :]
    w_ref, total_in = refs[:2]
    total_out = refs[2 + (len(refs) - 3) // 2]
    z, core = place()
    total_out[...] = total_in[...] + out_term(joined(mine), joined(twin), flip(z), core, w_ref)


def out_more(mine, twin, w, total, rides, flip, flops):
    at = len(mine) + len(twin) + 1
    return call(
        functools.partial(out_more_kernel, len(mine), len(twin), flip),
        "out_more",
        (*mine, *twin, w, total, *rides),
        [arr(total.shape, F32), *(arr(r.shape, r.dtype) for r in rides)],
        rides={at + i: i for i in range(1 + len(rides))},
        flops=flops,
    )


def out_beside_kernel(a, b, c, d, last_a, last_b, last_twin, w_ref, total_in, total_out):
    z, core = place()
    half = last_a.shape[0]
    last, twin = (rows for _, rows in halves(last_a, last_b, 3 - z, core))
    total = total_in[...] + out_term(joined((a, b)), joined((c, d)), z ^ 1, core, w_ref)
    total = total + jnp.dot(joined((last_a, last_b)), w_ref[last, :], preferred_element_type=F32)
    total_out[:half] = total[:half] + jnp.dot(last_twin[...], w_ref[twin, :], preferred_element_type=F32)
    total_out[half:] = total[half:]


def out_beside(mine, twin, last, last_twin, w, total, flops):
    return call(
        out_beside_kernel,
        "out_beside",
        (*mine, *twin, *last, last_twin, w, total),
        [arr(total.shape, F32)],
        rides={8: 0},
        flops=flops,
    )[0]


def out_last_kernel(twin_ref, w_ref, total_ref, sa_ref, sb_ref, hot_ref, hid_ref, out, out_ref, sems):
    z, core = place()
    half, width = twin_ref.shape
    rows = pl.ds(pl.multiple_of((2 * (3 - z) + 1 - core) * width, width), width)
    top = sa_ref[:, 128:129] * total_ref[:half]
    rest = total_ref[half:] + jnp.dot(twin_ref[...], w_ref[rows, :], preferred_element_type=F32)
    update = jnp.concatenate([top.astype(BF16), (sb_ref[:, 128:129] * rest).astype(BF16)], axis=0)
    block = 256
    copies = []
    for i in range(hid_ref.shape[0] // block):
        rows = slice(i * block, (i + 1) * block)
        placed = jnp.dot(hot_ref[rows, :], update, preferred_element_type=F32)
        out_ref[rows, :] = (hid_ref[rows, :].astype(F32) + placed).astype(BF16)
        copies += fetch([(out_ref.at[rows, :], out.at[rows, :])], sems, i)
    settle(copies)


def out_last(twin, w, total, stats, hot, hidden):
    return call(
        out_last_kernel,
        "out_last",
        (twin, w, total, *stats, hot, hidden),
        [arr(hidden.shape, BF16)],
        scratch=[pltpu.VMEM(hidden.shape, BF16), pltpu.SemaphoreType.DMA((hidden.shape[0] // 256,))],
        out_hbm=True,
    )[0]


def angles(row_pos):
    half = HEAD_SIZE // 2
    frequency = ROPE_BASE ** (-(jnp.arange(half, dtype=F32) * 2.0 / HEAD_SIZE))
    turned = row_pos.astype(F32) * jnp.concatenate([frequency, frequency])[None, :]
    sign = jnp.concatenate([-jnp.ones((half,), F32), jnp.ones((half,), F32)])
    return jnp.cos(turned), jnp.sin(turned) * sign[None, :]


def body(
    size,
    hidden_in,
    norm_gain,
    router_weight,
    w_query,
    w_key,
    value_weight,
    w_out,
    keep_flags,
    keep_counts,
    keep_positions,
):
    shards = lax.axis_size("ctx")
    tok = hidden_in.shape[0]
    nq = w_query.shape[1]
    flags = keep_flags.reshape(-1, 128)
    weights = (norm_gain.reshape(1, -1), router_weight.reshape(1, -1), w_query, w_key, value_weight)

    full, first, second, rowpos = pick(keep_positions, hidden_in)
    held = {}

    def own(mine, mate):
        ride, held["sums"], *held["staged"], held["bias"], held["hot"] = own_part(
            *mine, *mate, weights, keep_counts, keep_positions, flags, tok
        )
        return ride

    def far(mine, twin, last):
        held["sums"], held["cos"], held["sin"], *pieces = more_part(
            mine, twin, held["staged"], held["sums"], angles(rowpos), lambda z: z ^ 2, FAR_COST, (last,)
        )
        return tuple(pieces)

    def beside(mine, twin):
        (held["sums"],) = more_part(mine, twin, held["staged"], held["sums"], (), lambda z: z ^ 1, BESIDE_COST)

    pair, last_b, twin = spread_halves(size, full, first, second, own, far, beside)
    sums, staged, bias = held["sums"], held["staged"], held["bias"]
    cos, sin = held["cos"], held["sin"]
    half = first.shape[0]
    ring = [(s, (s + 1) % shards) for s in range(shards)]
    kvs, stats, pairs, qs, carry = [], [], [], [], []
    for i in range(2):
        if i == 1:
            kvs[0], last_b = gate(kvs[0], last_b)
            pair = (last_b,), (twin(last_b),)
        kv, stat = kv_last(i * half, pair, staged, sums, cos, sin, nq, KV_COST)
        kvs.append(kv)
        stats.append(stat)
        pairs.append(pair)
    moved = [lax.ppermute(kv, "ctx", ring) for kv in kvs]
    for i in range(2):
        q, *terms = q_part(
            i, pairs[i], staged, sums, stats[i], cos, sin, kvs[: i + 1], bias, nq, Q_COST if i else QA_COST
        )
        qs.append(q)
        carry += terms
    for step in range(1, shards):
        for i in range(2):
            last = step == shards - 1 and i == 1
            carry = attend_more(step, i * half, last, qs, moved[i], bias, carry, ATTEND_COST)
        if step < shards - 1:
            moved = [lax.ppermute(kv, "ctx", ring) for kv in moved]

    def own_out(mine, twin, rides):
        *rides, held["total"], held["w"], held["hidden"] = out_own(mine, twin, rides, w_out, hidden_in)
        return rides

    def far_out(mine, twin, rides):
        held["total"], *rides = out_more(mine, twin, held["w"], held["total"], rides, lambda z: z ^ 2, PART_COST)
        return rides

    def beside_out(mine, twin, last, last_twin):
        held["total"] = out_beside(mine, twin, last, last_twin, held["w"], held["total"], PART_COST)

    twin = spread(size, *carry, own_out, far_out, beside_out)
    return out_last(twin, held["w"], held["total"], stats, held["hot"], held["hidden"])


def solution(mesh):
    in_specs = (
        P(("groups", "ctx"), "heads"),
        P(),
        P(),
        P(None, "heads"),
        P(None, "heads"),
        P(None, "heads"),
        P(None, "heads"),
        P(("groups", "ctx")),
        P("groups"),
        P("groups", None),
    )
    out_specs = P(("groups", "ctx"), "heads")
    return jax.shard_map(
        functools.partial(body, mesh.shape["heads"]),
        mesh=mesh,
        in_specs=in_specs,
        out_specs=out_specs,
        check_vma=False,
    )
```

```python
import functools

import jax
import jax.numpy as jnp
from jax import lax
from jax.experimental import pallas as pl
from jax.experimental.pallas import tpu as pltpu
from jax.sharding import PartitionSpec as P

HEAD_SIZE = 128
ROPE_BASE = 500000.0
NORM_EPS = 1e-05
LOG2E = 1.4426950408889634
VMEM_LIMIT = 24 * 1024 * 1024
PIECES = 2
F32 = jnp.float32
BF16 = jnp.bfloat16
I32 = jnp.int32
COST = 400_000_000
PART_COST = 400_000_000
OWN_COST = 1_500_000_000
GATE_COST = 1_000_000
FAR_COST = 3_000_000_000
BESIDE_COST = 1_000_000
KV_COST = 1_000_000
Q_COST = 1_000_000
QA_COST = 1_000_000
ATTEND_COST = 400_000_000


VMEM = pl.BlockSpec(memory_space=pltpu.VMEM)
HBM = pl.BlockSpec(memory_space=pltpu.HBM)


def arr(shape, dtype):
    return jax.ShapeDtypeStruct(shape, dtype)


def call(kernel, name, operands, out_shape, scratch=(), rides=None, hbm=(), out_hbm=False, flops=COST):
    operands = [(o, any(o is h for h in hbm)) for o in operands]
    return pl.pallas_call(
        kernel,
        out_shape=out_shape,
        in_specs=[HBM if far else VMEM for _, far in operands],
        out_specs=[HBM if out_hbm else VMEM] * len(out_shape),
        scratch_shapes=list(scratch),
        input_output_aliases=rides or {},
        compiler_params=pltpu.CompilerParams(vmem_limit_bytes=VMEM_LIMIT),
        cost_estimate=pl.CostEstimate(flops=flops, bytes_accessed=1, transcendentals=0),
        name=name,
    )(*(pltpu.with_memory_space_constraint(o, pltpu.HBM) if far else o for o, far in operands))


def fetch(pairs, sems, base=0):
    copies = [pltpu.make_async_copy(src, dst, sems.at[base + i]) for i, (src, dst) in enumerate(pairs)]
    for copy in copies:
        copy.start()
    return copies


def place():
    d = lax.axis_index("heads")
    return d // 2, lax.rem(d, 2)


def live_row(pos_ref, cnt_ref, shard, dead):
    pos = pos_ref[pl.ds(shard, 1), :]
    slot = lax.broadcasted_iota(I32, pos.shape, 1)
    return jnp.where(slot < cnt_ref[shard], pos, dead)


def column(row):
    return jnp.transpose(jnp.broadcast_to(row, (128, row.shape[1])))


def pick_kernel(pos_hbm, hid_hbm, x_ref, xa_ref, xb_ref, rowpos_ref, pos_ref, hid_ref, sems):
    own, shards = lax.axis_index("ctx"), lax.axis_size("ctx")
    tok, cap = hid_ref.shape[0], x_ref.shape[0]
    pieces = [slice(at, at + 256) for at in range(0, tok, 256)]
    copies = fetch([(pos_hbm, pos_ref), *((hid_hbm.at[p, :], hid_ref.at[p, :]) for p in pieces)], sems)
    copies[0].wait()
    pos = column(pos_ref[pl.ds(own, 1), :])
    rowpos_ref[...] = jnp.where(pos < 0, shards * tok, pos)
    local = pos[:, :1] - own * tok
    total = None
    for piece, copy in zip(pieces, copies[1:]):
        at = lax.broadcasted_iota(I32, (cap, 256), 1) + piece.start
        hot = jnp.where(at == local, 1.0, 0.0).astype(BF16)
        copy.wait()
        total = add(total, jnp.dot(hot, hid_ref[piece, :], preferred_element_type=F32))
    x = total.astype(BF16)
    x_ref[...] = x
    xa_ref[...] = x[: cap // 2]
    xb_ref[...] = x[cap // 2 :]


def pick(positions, hidden):
    cap, width = positions.shape[1], hidden.shape[1]
    return call(
        pick_kernel,
        "pick",
        (positions, hidden),
        [arr((cap, width), BF16), arr((cap // 2, width), BF16), arr((cap // 2, width), BF16), arr((cap, 128), I32)],
        scratch=[
            pltpu.VMEM(positions.shape, I32),
            pltpu.VMEM(hidden.shape, BF16),
            pltpu.SemaphoreType.DMA((1 + hidden.shape[0] // 256,)),
        ],
        hbm=(positions, hidden),
    )


def sender(perm):
    return functools.partial(lax.ppermute, axis_name="heads", perm=perm)


def chip_sender(size, f):
    return sender([(2 * z + c, 2 * f(z) + c) for z in range(size // 2) for c in range(2)])


def gate(*rides):
    shapes = [arr(r.shape, r.dtype) for r in rides]
    return call(lambda *_: None, "gate", rides, shapes, rides={i: i for i in range(len(rides))}, flops=GATE_COST)


def spread(size, full, first, second, use_own, use_far, use_beside):
    cross = chip_sender(size, lambda z: 3 - z)
    near = chip_sender(size, lambda z: z ^ 1)
    twin = sender([(d, d ^ 1) for d in range(size)])
    far = cross(full)
    mates = twin(first), twin(second)
    beside = near(first), near(second)
    half = first.shape[0]
    last = near(far[:half]), near(far[half:])
    beside = use_own((full,), mates, beside)
    beside = use_far((far,), (twin(far),), beside)
    use_beside(beside, (twin(beside[0]), twin(beside[1])), last, twin(last[0]))
    return twin(last[1])


def spread_halves(size, full, first, second, use_own, use_far, use_beside):
    cross = chip_sender(size, lambda z: 3 - z)
    near = chip_sender(size, lambda z: z ^ 1)
    twin = sender([(d, d ^ 1) for d in range(size)])
    far = cross(first), cross(second)
    beside = near(use_own((full,), (twin(full),)))
    last_a, last_b = near(far[0]), near(far[1])
    last_a = use_far(far, (twin(far[0]), twin(far[1])), last_a)
    use_beside((beside,), (twin(beside),))
    return (last_a, tuple(twin(x) for x in last_a)), last_b, twin


def joined(refs):
    parts = [ref[...] for ref in refs]
    return parts[0] if len(parts) == 1 else jnp.concatenate(parts, axis=0)


def lanes_sum(x):
    total = x[:, :128]
    for at in range(128, x.shape[1], 128):
        total = total + x[:, at : at + 128]
    return total


def halves(mine, twin, zz, core):
    width = mine.shape[1]
    rows = [pl.ds(pl.multiple_of((2 * zz + at) * width, width), width) for at in (core, 1 - core)]
    return zip((mine, twin), rows)


def add(a, b):
    return b if a is None else a + b


def project(mine, twin, zz, core, gain_ref, router_ref, w_ref, columns, stats=True):
    product = squares = routed = None
    for x, rows in halves(mine, twin, zz, core):
        xf = x.astype(F32)
        gained = (xf * gain_ref[:, rows]).astype(BF16)
        product = add(product, jnp.dot(gained, w_ref[rows, columns], preferred_element_type=F32))
        if stats:
            squares = add(squares, lanes_sum(xf * xf))
            routed = add(routed, lanes_sum(xf * router_ref[:, rows]))
    return product, squares, routed


def settle(copies):
    for copy in copies:
        copy.wait()


def own_kernel(x_ref, twin_ref, gain, router, wq, wk, wv, cnt, pos, flag, *refs):
    _, sums_ref, gain_ref, router_ref, w_ref, bias_ref, hot_ref, sems = refs[:8]
    z, core = place()
    nq, nk, depth = wq.shape[1], wk.shape[1], wq.shape[0]
    lanes = ((wq, slice(0, nq)), (wk, slice(nq, nq + nk)), (wv, slice(nq + nk, nq + 2 * nk)))
    block = 2 * x_ref.shape[1]
    blocks = depth // block
    vectors = fetch([(gain, gain_ref), (router, router_ref)], sems, 3 * blocks)
    copies = []
    for i in range(blocks):
        rows = pl.ds(pl.multiple_of((z ^ i) * block, block), block)
        copies.append(fetch([(w.at[rows, :], w_ref.at[rows, at]) for w, at in lanes], sems, 3 * i))
    settle(vectors)
    settle(copies[0])
    product, squares, routed = project(x_ref[...], twin_ref[...], z, core, gain_ref, router_ref, w_ref, slice(None))
    n = product.shape[1]
    sums_ref[:, 0:n] = product
    sums_ref[:, n : n + 128] = squares
    sums_ref[:, n + 128 : n + 256] = routed
    masks_kernel(cnt, pos, flag, bias_ref, hot_ref, *refs[8:])
    for later in copies[1:]:
        settle(later)


def own_part(full, twin, weights, counts, positions, flags, tok):
    cap, width = full.shape
    depth = weights[2].shape[0]
    columns = sum(w.shape[1] for w in weights[2:])
    shards = positions.shape[0]
    return call(
        own_kernel,
        "own_part",
        (full, twin, *weights, counts, positions, flags),
        [
            arr(full.shape, BF16),
            arr((cap, columns + 256), F32),
            arr((1, depth), F32),
            arr((1, depth), F32),
            arr((depth, columns), BF16),
            arr((shards, cap, cap), F32),
            arr((tok, cap), BF16),
        ],
        scratch=[
            pltpu.SemaphoreType.DMA((3 * depth // (2 * width) + 2,)),
            pltpu.SMEM(counts.shape, I32),
            pltpu.VMEM(positions.shape, I32),
            pltpu.VMEM(flags.shape, I32),
            pltpu.SemaphoreType.DMA((3,)),
        ],
        rides={0: 0},
        hbm=(*weights, counts, positions, flags),
        flops=OWN_COST,
    )


def masks_kernel(cnt_hbm, pos_hbm, flag_hbm, bias_ref, hot_ref, cnt_ref, pos_ref, flag_ref, sems):
    settle(fetch([(cnt_hbm, cnt_ref), (pos_hbm, pos_ref), (flag_hbm, flag_ref)], sems))
    own, shards = lax.axis_index("ctx"), lax.axis_size("ctx")
    tok = hot_ref.shape[0]
    seq = shards * tok
    row = live_row(pos_ref, cnt_ref, own, seq)
    for step in range(shards):
        source = lax.rem(own + shards - step, shards)
        keys = column(live_row(pos_ref, cnt_ref, source, seq + 1))[:, :1]
        bias_ref[step] = jnp.where(keys <= row, 0.0, -jnp.inf).astype(F32)
    flags = jnp.transpose(flag_ref[...].astype(F32))
    local = row - own * tok
    for r in range(tok // 128):
        at = lax.broadcasted_iota(I32, (128, row.shape[1]), 0) + r * 128
        hot = jnp.where(at == local, flags[:, r : r + 1], 0.0)
        hot_ref[r * 128 : (r + 1) * 128, :] = hot.astype(BF16)


def more_kernel(n_mine, n_twin, n_ride, flip, split, *refs):
    mine, twin, refs = refs[:n_mine], refs[n_mine : n_mine + n_twin], refs[n_mine + n_twin :]
    gain_ref, router_ref, w_ref, sums_in = refs[:4]
    refs = refs[4 + n_ride :]
    if split:
        whole_ref, refs = refs[0], refs[1:]
        pieces = refs[1 + n_ride :]
        for i, piece in enumerate(pieces):
            piece[...] = whole_ref[i * piece.shape[0] : (i + 1) * piece.shape[0], :]
    sums_out = refs[0]
    z, core = place()
    product, squares, routed = project(
        joined(mine), joined(twin), flip(z), core, gain_ref, router_ref, w_ref, slice(None)
    )
    n = product.shape[1]
    sums_out[:, 0:n] = sums_in[:, 0:n] + product
    sums_out[:, n : n + 128] = sums_in[:, n : n + 128] + squares
    sums_out[:, n + 128 : n + 256] = sums_in[:, n + 128 : n + 256] + routed


def more_part(mine, twin, staged, sums, rides, flip, flops, split=()):
    at = len(mine) + len(twin) + 3
    shapes = [arr((x.shape[0] // PIECES, x.shape[1]), x.dtype) for x in split for _ in range(PIECES)]
    return call(
        functools.partial(more_kernel, len(mine), len(twin), len(rides), flip, bool(split)),
        "more_part",
        (*mine, *twin, *staged, sums, *rides, *split),
        [arr(sums.shape, F32), *(arr(r.shape, r.dtype) for r in rides), *shapes],
        rides={at + i: i for i in range(1 + len(rides))},
        flops=flops,
    )


def turn(x, cos, sin):
    return x * cos + pltpu.roll(x, HEAD_SIZE // 2, 1) * sin


def kv_last_kernel(nq, at, n_mine, *refs):
    mine, twin, refs = joined(refs[:n_mine]), joined(refs[n_mine : 2 * n_mine]), refs[2 * n_mine :]
    gain_ref, router_ref, w_ref, sums, cos_ref, sin_ref, kv_out, stat_out = refs
    z, core = place()
    n, features = w_ref.shape[1], w_ref.shape[0]
    rows = slice(at, at + mine.shape[0])
    product, squares, routed = project(mine, twin, z ^ 2, core, gain_ref, router_ref, w_ref, slice(nq, n))
    squares = jnp.sum(sums[rows, n : n + 128] + squares, axis=1, keepdims=True)
    routed = jnp.sum(sums[rows, n + 128 : n + 256] + routed, axis=1, keepdims=True)
    inverse = lax.rsqrt(squares * (1.0 / features) + NORM_EPS)
    kv = (sums[rows, nq:n] + product) * inverse
    kv_out[:, 0:128] = turn(kv[:, 0:128], cos_ref[rows, :], sin_ref[rows, :]).astype(BF16)
    kv_out[:, 128:256] = kv[:, 128:256].astype(BF16)
    stat_out[:, 0:128] = jnp.broadcast_to(inverse, (inverse.shape[0], 128))
    gate_value = 1.0 / (1.0 + jnp.exp(-routed))
    stat_out[:, 128:256] = jnp.broadcast_to(gate_value, (gate_value.shape[0], 128))


def kv_last(at, pair, staged, sums, cos, sin, nq, flops):
    mine, twin = pair
    cap = sum(x.shape[0] for x in mine)
    return call(
        functools.partial(kv_last_kernel, nq, at, len(mine)),
        "kv_last",
        (*mine, *twin, *staged, sums, cos, sin),
        [arr((cap, 256), BF16), arr((cap, 256), F32)],
        flops=flops,
    )


def attend(q, kv, bias, carry):
    k, v = kv[:, 0:128], kv[:, 128:256]
    scale = LOG2E / HEAD_SIZE**0.5
    s = lax.dot_general(k, q, (((1,), (1,)), ((), ())), preferred_element_type=F32) * scale + bias
    top = jnp.max(s, axis=0, keepdims=True)
    if carry is not None:
        top = jnp.maximum(top, carry[0])
    e = jnp.exp2(s - top)
    total = jnp.sum(e, axis=0, keepdims=True)
    mix = lax.dot_general(v, e.astype(BF16), (((0,), (0,)), ((), ())), preferred_element_type=F32)
    if carry is not None:
        fade = jnp.exp2(carry[0] - top)
        total = total + carry[1] * fade
        mix = mix + carry[2] * fade
    return top, total, mix


def q_kernel(i, n_mine, n_kv, *refs):
    mine, twin, refs = joined(refs[:n_mine]), joined(refs[n_mine : 2 * n_mine]), refs[2 * n_mine :]
    gain_ref, w_ref, sums, stat_ref, cos_ref, sin_ref, bias_ref, *refs = refs
    kv_refs, (q_out, top_ref, total_ref, mix_ref) = refs[:n_kv], refs[n_kv:]
    z, core = place()
    half, nq = q_out.shape
    rows, keys = slice(i * half, (i + 1) * half), slice(0, (i + 1) * half)
    product, _, _ = project(
        mine, twin, z ^ 2, core, gain_ref, None, w_ref, slice(0, nq), stats=False
    )
    q = (sums[rows, 0:nq] + product) * stat_ref[:, 0:1]
    cos, sin, kv = cos_ref[rows, :], sin_ref[rows, :], joined(kv_refs)
    for h in range(nq // HEAD_SIZE):
        lanes = slice(h * HEAD_SIZE, (h + 1) * HEAD_SIZE)
        turned = turn(q[:, lanes], cos, sin).astype(BF16)
        q_out[:, lanes] = turned
        top, total, mix = attend(turned, kv, bias_ref[0, keys, rows], None)
        at = slice(h * half, (h + 1) * half)
        top_ref[:, at], total_ref[:, at], mix_ref[:, at] = top, total, mix


def carry_shapes(cap, nq):
    heads = nq // HEAD_SIZE
    return [arr((1, heads * cap), F32), arr((1, heads * cap), F32), arr((HEAD_SIZE, heads * cap), F32)]


def q_part(i, pair, staged, sums, stat, cos, sin, kvs, bias, nq, flops):
    mine, twin = pair
    half = stat.shape[0]
    return call(
        functools.partial(q_kernel, i, len(mine), len(kvs)),
        "q_part",
        (*mine, *twin, staged[0], staged[2], sums, stat, cos, sin, bias, *kvs),
        [arr((half, nq), BF16), *carry_shapes(half, nq)],
        flops=flops,
    )


def attend_kernel(step, first_key, n_carry, last, qa_ref, qb_ref, kv_ref, bias_ref, *refs):
    carries, outs = refs[: 3 * n_carry], refs[3 * n_carry :]
    half, nq = qa_ref.shape
    cap = 2 * half
    keys = slice(first_key, first_key + kv_ref.shape[0])
    for h in range(nq // HEAD_SIZE):
        lanes = slice(h * HEAD_SIZE, (h + 1) * HEAD_SIZE)
        at = slice(h * cap, (h + 1) * cap)
        part = slice(h * cap // n_carry, (h + 1) * cap // n_carry)
        carry = [
            jnp.concatenate([carries[j][:, part] for j in range(k, 3 * n_carry, 3)], axis=1) for k in range(3)
        ]
        q = jnp.concatenate([qa_ref[:, lanes], qb_ref[:, lanes]], axis=0)
        top, total, mix = attend(q, kv_ref[...], bias_ref[step, keys, :], carry)
        if not last:
            outs[0][:, at], outs[1][:, at], outs[2][:, at] = top, total, mix
            continue
        full, first, second = outs
        attn = jnp.transpose((mix * (1.0 / total)).astype(BF16))
        full[:, lanes] = attn
        first[:, lanes] = attn[:half]
        second[:, lanes] = attn[half:]


def attend_more(step, first_key, last, qs, kv, bias, carry, flops):
    half, nq = qs[0].shape
    cap = 2 * half
    shapes = [arr((cap, nq), BF16), arr((half, nq), BF16), arr((half, nq), BF16)]
    return call(
        functools.partial(attend_kernel, step, first_key, len(carry) // 3, last),
        "attend_more",
        (*qs, kv, bias, *carry),
        shapes if last else carry_shapes(cap, nq),
        flops=flops,
    )


def out_term(mine, twin, zz, core, w_ref):
    out = None
    for x, rows in halves(mine, twin, zz, core):
        out = add(out, jnp.dot(x, w_ref[rows, :], preferred_element_type=F32))
    return out


def out_own_kernel(n_mine, n_twin, *refs):
    mine, twin, refs = refs[:n_mine], refs[n_mine : n_mine + n_twin], refs[n_mine + n_twin :]
    n_ride = (len(refs) - 6) // 2
    w, hidden = refs[n_ride : n_ride + 2]
    total_ref, w_ref, hid_ref, sems = refs[-4:]
    z, core = place()
    copies = fetch([(w, w_ref), (hidden, hid_ref)], sems)
    copies[0].wait()
    total_ref[...] = out_term(joined(mine), joined(twin), z, core, w_ref)
    copies[1].wait()


def out_own(mine, twin, rides, w_out, hidden):
    cap = sum(x.shape[0] for x in mine)
    at = len(mine) + len(twin)
    return call(
        functools.partial(out_own_kernel, len(mine), len(twin)),
        "out_own",
        (*mine, *twin, *rides, w_out, hidden),
        [
            *(arr(r.shape, r.dtype) for r in rides),
            arr((cap, w_out.shape[1]), F32),
            arr(w_out.shape, BF16),
            arr(hidden.shape, BF16),
        ],
        scratch=[pltpu.SemaphoreType.DMA((2,))],
        rides={at + i: i for i in range(len(rides))},
        hbm=(w_out, hidden),
        flops=PART_COST,
    )


def out_more_kernel(n_mine, n_twin, flip, *refs):
    mine, twin, refs = refs[:n_mine], refs[n_mine : n_mine + n_twin], refs[n_mine + n_twin :]
    w_ref, total_in = refs[:2]
    total_out = refs[2 + (len(refs) - 3) // 2]
    z, core = place()
    total_out[...] = total_in[...] + out_term(joined(mine), joined(twin), flip(z), core, w_ref)


def out_more(mine, twin, w, total, rides, flip, flops):
    at = len(mine) + len(twin) + 1
    return call(
        functools.partial(out_more_kernel, len(mine), len(twin), flip),
        "out_more",
        (*mine, *twin, w, total, *rides),
        [arr(total.shape, F32), *(arr(r.shape, r.dtype) for r in rides)],
        rides={at + i: i for i in range(1 + len(rides))},
        flops=flops,
    )


def out_beside_kernel(a, b, c, d, last_a, last_b, last_twin, w_ref, total_in, total_out):
    z, core = place()
    half = last_a.shape[0]
    last, twin = (rows for _, rows in halves(last_a, last_b, z ^ 2, core))
    total = total_in[...] + out_term(joined((a, b)), joined((c, d)), z ^ 1, core, w_ref)
    total = total + jnp.dot(joined((last_a, last_b)), w_ref[last, :], preferred_element_type=F32)
    total_out[:half] = total[:half] + jnp.dot(last_twin[...], w_ref[twin, :], preferred_element_type=F32)
    total_out[half:] = total[half:]


def out_beside(mine, twin, last, last_twin, w, total, flops):
    return call(
        out_beside_kernel,
        "out_beside",
        (*mine, *twin, *last, last_twin, w, total),
        [arr(total.shape, F32)],
        rides={8: 0},
        flops=flops,
    )[0]


def out_last_kernel(twin_ref, w_ref, total_ref, sa_ref, sb_ref, hot_ref, hid_ref, out, out_ref, sems):
    z, core = place()
    half, width = twin_ref.shape
    rows = pl.ds(pl.multiple_of((2 * (z ^ 2) + 1 - core) * width, width), width)
    top = sa_ref[:, 128:129] * total_ref[:half]
    rest = total_ref[half:] + jnp.dot(twin_ref[...], w_ref[rows, :], preferred_element_type=F32)
    update = jnp.concatenate([top.astype(BF16), (sb_ref[:, 128:129] * rest).astype(BF16)], axis=0)
    block = 256
    copies = []
    for i in range(hid_ref.shape[0] // block):
        rows = slice(i * block, (i + 1) * block)
        placed = jnp.dot(hot_ref[rows, :], update, preferred_element_type=F32)
        out_ref[rows, :] = (hid_ref[rows, :].astype(F32) + placed).astype(BF16)
        copies += fetch([(out_ref.at[rows, :], out.at[rows, :])], sems, i)
    settle(copies)


def out_last(twin, w, total, stats, hot, hidden):
    return call(
        out_last_kernel,
        "out_last",
        (twin, w, total, *stats, hot, hidden),
        [arr(hidden.shape, BF16)],
        scratch=[pltpu.VMEM(hidden.shape, BF16), pltpu.SemaphoreType.DMA((hidden.shape[0] // 256,))],
        out_hbm=True,
    )[0]


def angles(row_pos):
    half = HEAD_SIZE // 2
    frequency = ROPE_BASE ** (-(jnp.arange(half, dtype=F32) * 2.0 / HEAD_SIZE))
    turned = row_pos.astype(F32) * jnp.concatenate([frequency, frequency])[None, :]
    sign = jnp.concatenate([-jnp.ones((half,), F32), jnp.ones((half,), F32)])
    return jnp.cos(turned), jnp.sin(turned) * sign[None, :]


def body(
    size,
    hidden_in,
    norm_gain,
    router_weight,
    w_query,
    w_key,
    value_weight,
    w_out,
    keep_flags,
    keep_counts,
    keep_positions,
):
    shards = lax.axis_size("ctx")
    tok = hidden_in.shape[0]
    nq = w_query.shape[1]
    flags = keep_flags.reshape(-1, 128)
    weights = (norm_gain.reshape(1, -1), router_weight.reshape(1, -1), w_query, w_key, value_weight)

    full, first, second, rowpos = pick(keep_positions, hidden_in)
    held = {}

    def own(mine, mate):
        ride, held["sums"], *held["staged"], held["bias"], held["hot"] = own_part(
            *mine, *mate, weights, keep_counts, keep_positions, flags, tok
        )
        return ride

    def far(mine, twin, last):
        held["sums"], held["cos"], held["sin"], *pieces = more_part(
            mine, twin, held["staged"], held["sums"], angles(rowpos), lambda z: 3 - z, FAR_COST, (last,)
        )
        return tuple(pieces)

    def beside(mine, twin):
        (held["sums"],) = more_part(mine, twin, held["staged"], held["sums"], (), lambda z: z ^ 1, BESIDE_COST)

    pair, last_b, twin = spread_halves(size, full, first, second, own, far, beside)
    sums, staged, bias = held["sums"], held["staged"], held["bias"]
    cos, sin = held["cos"], held["sin"]
    half = first.shape[0]
    ring = [(s, (s + 1) % shards) for s in range(shards)]
    kvs, stats, pairs, qs, carry = [], [], [], [], []
    for i in range(2):
        if i == 1:
            kvs[0], last_b = gate(kvs[0], last_b)
            pair = (last_b,), (twin(last_b),)
        kv, stat = kv_last(i * half, pair, staged, sums, cos, sin, nq, KV_COST)
        kvs.append(kv)
        stats.append(stat)
        pairs.append(pair)
    moved = [lax.ppermute(kv, "ctx", ring) for kv in kvs]
    for i in range(2):
        q, *terms = q_part(
            i, pairs[i], staged, sums, stats[i], cos, sin, kvs[: i + 1], bias, nq, Q_COST if i else QA_COST
        )
        qs.append(q)
        carry += terms
    for step in range(1, shards):
        for i in range(2):
            last = step == shards - 1 and i == 1
            carry = attend_more(step, i * half, last, qs, moved[i], bias, carry, ATTEND_COST)
        if step < shards - 1:
            moved = [lax.ppermute(kv, "ctx", ring) for kv in moved]

    def own_out(mine, twin, rides):
        *rides, held["total"], held["w"], held["hidden"] = out_own(mine, twin, rides, w_out, hidden_in)
        return rides

    def far_out(mine, twin, rides):
        held["total"], *rides = out_more(mine, twin, held["w"], held["total"], rides, lambda z: 3 - z, PART_COST)
        return rides

    def beside_out(mine, twin, last, last_twin):
        held["total"] = out_beside(mine, twin, last, last_twin, held["w"], held["total"], PART_COST)

    twin = spread(size, *carry, own_out, far_out, beside_out)
    return out_last(twin, held["w"], held["total"], stats, held["hot"], held["hidden"])


def solution(mesh):
    in_specs = (
        P(("groups", "ctx"), "heads"),
        P(),
        P(),
        P(None, "heads"),
        P(None, "heads"),
        P(None, "heads"),
        P(None, "heads"),
        P(("groups", "ctx")),
        P("groups"),
        P("groups", None),
    )
    out_specs = P(("groups", "ctx"), "heads")
    return jax.shard_map(
        functools.partial(body, mesh.shape["heads"]),
        mesh=mesh,
        in_specs=in_specs,
        out_specs=out_specs,
        check_vma=False,
    )
```

```python
import functools

import jax
import jax.numpy as jnp
from jax import lax
from jax.experimental import pallas as pl
from jax.experimental.pallas import tpu as pltpu
from jax.sharding import PartitionSpec as P

HEAD_SIZE = 128
ROPE_BASE = 500000.0
NORM_EPS = 1e-05
LOG2E = 1.4426950408889634
VMEM_LIMIT = 24 * 1024 * 1024
PIECES = 2
F32 = jnp.float32
BF16 = jnp.bfloat16
I32 = jnp.int32
COST = 400_000_000
PART_COST = 400_000_000
OWN_COST = 1_500_000_000
GATE_COST = 1_000_000
FAR_COST = 3_000_000_000
BESIDE_COST = 1_000_000
KV_COST = 1_000_000
Q_COST = 1_000_000
QA_COST = 1_000_000
ATTEND_COST = 400_000_000


VMEM = pl.BlockSpec(memory_space=pltpu.VMEM)
HBM = pl.BlockSpec(memory_space=pltpu.HBM)


def arr(shape, dtype):
    return jax.ShapeDtypeStruct(shape, dtype)


def call(kernel, name, operands, out_shape, scratch=(), rides=None, hbm=(), out_hbm=False, flops=COST):
    operands = [(o, any(o is h for h in hbm)) for o in operands]
    return pl.pallas_call(
        kernel,
        out_shape=out_shape,
        in_specs=[HBM if far else VMEM for _, far in operands],
        out_specs=[HBM if out_hbm else VMEM] * len(out_shape),
        scratch_shapes=list(scratch),
        input_output_aliases=rides or {},
        compiler_params=pltpu.CompilerParams(vmem_limit_bytes=VMEM_LIMIT),
        cost_estimate=pl.CostEstimate(flops=flops, bytes_accessed=1, transcendentals=0),
        name=name,
    )(*(pltpu.with_memory_space_constraint(o, pltpu.HBM) if far else o for o, far in operands))


def fetch(pairs, sems, base=0):
    copies = [pltpu.make_async_copy(src, dst, sems.at[base + i]) for i, (src, dst) in enumerate(pairs)]
    for copy in copies:
        copy.start()
    return copies


def place():
    d = lax.axis_index("heads")
    return d // 2, lax.rem(d, 2)


def live_row(pos_ref, cnt_ref, shard, dead):
    pos = pos_ref[pl.ds(shard, 1), :]
    slot = lax.broadcasted_iota(I32, pos.shape, 1)
    return jnp.where(slot < cnt_ref[shard], pos, dead)


def column(row):
    return jnp.transpose(jnp.broadcast_to(row, (128, row.shape[1])))


def pick_kernel(pos_hbm, hid_hbm, x_ref, xa_ref, xb_ref, rowpos_ref, pos_ref, hid_ref, sems):
    own, shards = lax.axis_index("ctx"), lax.axis_size("ctx")
    tok, cap = hid_ref.shape[0], x_ref.shape[0]
    pieces = [slice(at, at + 256) for at in range(0, tok, 256)]
    copies = fetch([*((hid_hbm.at[p, :], hid_ref.at[p, :]) for p in pieces), (pos_hbm, pos_ref)], sems)
    copies[-1].wait()
    pos = column(pos_ref[pl.ds(own, 1), :])
    rowpos_ref[...] = jnp.where(pos < 0, shards * tok, pos)
    local = pos[:, :1] - own * tok
    total = None
    for piece, copy in zip(pieces, copies):
        at = lax.broadcasted_iota(I32, (cap, 256), 1) + piece.start
        hot = jnp.where(at == local, 1.0, 0.0).astype(BF16)
        copy.wait()
        total = add(total, jnp.dot(hot, hid_ref[piece, :], preferred_element_type=F32))
    x = total.astype(BF16)
    x_ref[...] = x
    xa_ref[...] = x[: cap // 2]
    xb_ref[...] = x[cap // 2 :]


def pick(positions, hidden):
    cap, width = positions.shape[1], hidden.shape[1]
    return call(
        pick_kernel,
        "pick",
        (positions, hidden),
        [arr((cap, width), BF16), arr((cap // 2, width), BF16), arr((cap // 2, width), BF16), arr((cap, 128), I32)],
        scratch=[
            pltpu.VMEM(positions.shape, I32),
            pltpu.VMEM(hidden.shape, BF16),
            pltpu.SemaphoreType.DMA((1 + hidden.shape[0] // 256,)),
        ],
        hbm=(positions, hidden),
    )


def sender(perm):
    return functools.partial(lax.ppermute, axis_name="heads", perm=perm)


def chip_sender(size, f):
    return sender([(2 * z + c, 2 * f(z) + c) for z in range(size // 2) for c in range(2)])


def gate(*rides):
    shapes = [arr(r.shape, r.dtype) for r in rides]
    return call(lambda *_: None, "gate", rides, shapes, rides={i: i for i in range(len(rides))}, flops=GATE_COST)


def spread(size, full, first, second, use_own, use_far, use_beside):
    cross = chip_sender(size, lambda z: 3 - z)
    near = chip_sender(size, lambda z: z ^ 1)
    twin = sender([(d, d ^ 1) for d in range(size)])
    far = cross(full)
    mates = twin(first), twin(second)
    beside = near(first), near(second)
    half = first.shape[0]
    last = near(far[:half]), near(far[half:])
    beside = use_own((full,), mates, beside)
    beside = use_far((far,), (twin(far),), beside)
    use_beside(beside, (twin(beside[0]), twin(beside[1])), last, twin(last[0]))
    return twin(last[1])


def spread_halves(size, full, first, second, use_own, use_far, use_beside):
    cross = chip_sender(size, lambda z: 3 - z)
    near = chip_sender(size, lambda z: z ^ 1)
    twin = sender([(d, d ^ 1) for d in range(size)])
    far = cross(first), cross(second)
    beside = near(use_own((full,), (twin(full),)))
    last_a, last_b = near(far[0]), near(far[1])
    last_a = use_far(far, (twin(far[0]), twin(far[1])), last_a)
    use_beside((beside,), (twin(beside),))
    return (last_a, tuple(twin(x) for x in last_a)), last_b, twin


def joined(refs):
    parts = [ref[...] for ref in refs]
    return parts[0] if len(parts) == 1 else jnp.concatenate(parts, axis=0)


def lanes_sum(x):
    total = x[:, :128]
    for at in range(128, x.shape[1], 128):
        total = total + x[:, at : at + 128]
    return total


def halves(mine, twin, zz, core):
    width = mine.shape[1]
    rows = [pl.ds(pl.multiple_of((2 * zz + at) * width, width), width) for at in (core, 1 - core)]
    return zip((mine, twin), rows)


def add(a, b):
    return b if a is None else a + b


def project(mine, twin, zz, core, gain_ref, router_ref, w_ref, columns, stats=True):
    product = squares = routed = None
    for x, rows in halves(mine, twin, zz, core):
        xf = x.astype(F32)
        gained = (xf * gain_ref[:, rows]).astype(BF16)
        product = add(product, jnp.dot(gained, w_ref[rows, columns], preferred_element_type=F32))
        if stats:
            squares = add(squares, lanes_sum(xf * xf))
            routed = add(routed, lanes_sum(xf * router_ref[:, rows]))
    return product, squares, routed


def settle(copies):
    for copy in copies:
        copy.wait()


def own_kernel(x_ref, twin_ref, gain, router, wq, wk, wv, cnt, pos, flag, *refs):
    _, sums_ref, gain_ref, router_ref, w_ref, bias_ref, hot_ref, sems = refs[:8]
    z, core = place()
    nq, nk, depth = wq.shape[1], wk.shape[1], wq.shape[0]
    lanes = ((wq, slice(0, nq)), (wk, slice(nq, nq + nk)), (wv, slice(nq + nk, nq + 2 * nk)))
    block = 2 * x_ref.shape[1]
    blocks = depth // block
    vectors = fetch([(gain, gain_ref), (router, router_ref)], sems, 3 * blocks)
    copies = []
    for i in range(blocks):
        rows = pl.ds(pl.multiple_of((z ^ i) * block, block), block)
        copies.append(fetch([(w.at[rows, :], w_ref.at[rows, at]) for w, at in lanes], sems, 3 * i))
    settle(vectors)
    settle(copies[0])
    product, squares, routed = project(x_ref[...], twin_ref[...], z, core, gain_ref, router_ref, w_ref, slice(None))
    n = product.shape[1]
    sums_ref[:, 0:n] = product
    sums_ref[:, n : n + 128] = squares
    sums_ref[:, n + 128 : n + 256] = routed
    masks_kernel(cnt, pos, flag, bias_ref, hot_ref, *refs[8:])
    for later in copies[1:]:
        settle(later)


def own_part(full, twin, weights, counts, positions, flags, tok):
    cap, width = full.shape
    depth = weights[2].shape[0]
    columns = sum(w.shape[1] for w in weights[2:])
    shards = positions.shape[0]
    return call(
        own_kernel,
        "own_part",
        (full, twin, *weights, counts, positions, flags),
        [
            arr(full.shape, BF16),
            arr((cap, columns + 256), F32),
            arr((1, depth), F32),
            arr((1, depth), F32),
            arr((depth, columns), BF16),
            arr((shards, cap, cap), F32),
            arr((tok, cap), BF16),
        ],
        scratch=[
            pltpu.SemaphoreType.DMA((3 * depth // (2 * width) + 2,)),
            pltpu.SMEM(counts.shape, I32),
            pltpu.VMEM(positions.shape, I32),
            pltpu.VMEM(flags.shape, I32),
            pltpu.SemaphoreType.DMA((3,)),
        ],
        rides={0: 0},
        hbm=(*weights, counts, positions, flags),
        flops=OWN_COST,
    )


def masks_kernel(cnt_hbm, pos_hbm, flag_hbm, bias_ref, hot_ref, cnt_ref, pos_ref, flag_ref, sems):
    settle(fetch([(cnt_hbm, cnt_ref), (pos_hbm, pos_ref), (flag_hbm, flag_ref)], sems))
    own, shards = lax.axis_index("ctx"), lax.axis_size("ctx")
    tok = hot_ref.shape[0]
    seq = shards * tok
    row = live_row(pos_ref, cnt_ref, own, seq)
    for step in range(shards):
        source = lax.rem(own + shards - step, shards)
        keys = column(live_row(pos_ref, cnt_ref, source, seq + 1))[:, :1]
        bias_ref[step] = jnp.where(keys <= row, 0.0, -jnp.inf).astype(F32)
    flags = jnp.transpose(flag_ref[...].astype(F32))
    local = row - own * tok
    for r in range(tok // 128):
        at = lax.broadcasted_iota(I32, (128, row.shape[1]), 0) + r * 128
        hot = jnp.where(at == local, flags[:, r : r + 1], 0.0)
        hot_ref[r * 128 : (r + 1) * 128, :] = hot.astype(BF16)


def more_kernel(n_mine, n_twin, n_ride, flip, split, *refs):
    mine, twin, refs = refs[:n_mine], refs[n_mine : n_mine + n_twin], refs[n_mine + n_twin :]
    gain_ref, router_ref, w_ref, sums_in = refs[:4]
    refs = refs[4 + n_ride :]
    if split:
        whole_ref, refs = refs[0], refs[1:]
        pieces = refs[1 + n_ride :]
        for i, piece in enumerate(pieces):
            piece[...] = whole_ref[i * piece.shape[0] : (i + 1) * piece.shape[0], :]
    sums_out = refs[0]
    z, core = place()
    product, squares, routed = project(
        joined(mine), joined(twin), flip(z), core, gain_ref, router_ref, w_ref, slice(None)
    )
    n = product.shape[1]
    sums_out[:, 0:n] = sums_in[:, 0:n] + product
    sums_out[:, n : n + 128] = sums_in[:, n : n + 128] + squares
    sums_out[:, n + 128 : n + 256] = sums_in[:, n + 128 : n + 256] + routed


def more_part(mine, twin, staged, sums, rides, flip, flops, split=()):
    at = len(mine) + len(twin) + 3
    shapes = [arr((x.shape[0] // PIECES, x.shape[1]), x.dtype) for x in split for _ in range(PIECES)]
    return call(
        functools.partial(more_kernel, len(mine), len(twin), len(rides), flip, bool(split)),
        "more_part",
        (*mine, *twin, *staged, sums, *rides, *split),
        [arr(sums.shape, F32), *(arr(r.shape, r.dtype) for r in rides), *shapes],
        rides={at + i: i for i in range(1 + len(rides))},
        flops=flops,
    )


def turn(x, cos, sin):
    return x * cos + pltpu.roll(x, HEAD_SIZE // 2, 1) * sin


def kv_last_kernel(nq, at, n_mine, *refs):
    mine, twin, refs = joined(refs[:n_mine]), joined(refs[n_mine : 2 * n_mine]), refs[2 * n_mine :]
    gain_ref, router_ref, w_ref, sums, cos_ref, sin_ref, kv_out, stat_out = refs
    z, core = place()
    n, features = w_ref.shape[1], w_ref.shape[0]
    rows = slice(at, at + mine.shape[0])
    product, squares, routed = project(mine, twin, z ^ 2, core, gain_ref, router_ref, w_ref, slice(nq, n))
    squares = jnp.sum(sums[rows, n : n + 128] + squares, axis=1, keepdims=True)
    routed = jnp.sum(sums[rows, n + 128 : n + 256] + routed, axis=1, keepdims=True)
    inverse = lax.rsqrt(squares * (1.0 / features) + NORM_EPS)
    kv = (sums[rows, nq:n] + product) * inverse
    kv_out[:, 0:128] = turn(kv[:, 0:128], cos_ref[rows, :], sin_ref[rows, :]).astype(BF16)
    kv_out[:, 128:256] = kv[:, 128:256].astype(BF16)
    stat_out[:, 0:128] = jnp.broadcast_to(inverse, (inverse.shape[0], 128))
    gate_value = 1.0 / (1.0 + jnp.exp(-routed))
    stat_out[:, 128:256] = jnp.broadcast_to(gate_value, (gate_value.shape[0], 128))


def kv_last(at, pair, staged, sums, cos, sin, nq, flops):
    mine, twin = pair
    cap = sum(x.shape[0] for x in mine)
    return call(
        functools.partial(kv_last_kernel, nq, at, len(mine)),
        "kv_last",
        (*mine, *twin, *staged, sums, cos, sin),
        [arr((cap, 256), BF16), arr((cap, 256), F32)],
        flops=flops,
    )


def attend(q, kv, bias, carry):
    k, v = kv[:, 0:128], kv[:, 128:256]
    scale = LOG2E / HEAD_SIZE**0.5
    s = lax.dot_general(k, q, (((1,), (1,)), ((), ())), preferred_element_type=F32) * scale + bias
    top = jnp.max(s, axis=0, keepdims=True)
    if carry is not None:
        top = jnp.maximum(top, carry[0])
    e = jnp.exp2(s - top)
    total = jnp.sum(e, axis=0, keepdims=True)
    mix = lax.dot_general(v, e.astype(BF16), (((0,), (0,)), ((), ())), preferred_element_type=F32)
    if carry is not None:
        fade = jnp.exp2(carry[0] - top)
        total = total + carry[1] * fade
        mix = mix + carry[2] * fade
    return top, total, mix


def q_kernel(i, n_mine, n_kv, *refs):
    mine, twin, refs = joined(refs[:n_mine]), joined(refs[n_mine : 2 * n_mine]), refs[2 * n_mine :]
    gain_ref, w_ref, sums, stat_ref, cos_ref, sin_ref, bias_ref, *refs = refs
    kv_refs, (q_out, top_ref, total_ref, mix_ref) = refs[:n_kv], refs[n_kv:]
    z, core = place()
    half, nq = q_out.shape
    rows, keys = slice(i * half, (i + 1) * half), slice(0, (i + 1) * half)
    product, _, _ = project(
        mine, twin, z ^ 2, core, gain_ref, None, w_ref, slice(0, nq), stats=False
    )
    q = (sums[rows, 0:nq] + product) * stat_ref[:, 0:1]
    cos, sin, kv = cos_ref[rows, :], sin_ref[rows, :], joined(kv_refs)
    for h in range(nq // HEAD_SIZE):
        lanes = slice(h * HEAD_SIZE, (h + 1) * HEAD_SIZE)
        turned = turn(q[:, lanes], cos, sin).astype(BF16)
        q_out[:, lanes] = turned
        top, total, mix = attend(turned, kv, bias_ref[0, keys, rows], None)
        at = slice(h * half, (h + 1) * half)
        top_ref[:, at], total_ref[:, at], mix_ref[:, at] = top, total, mix


def carry_shapes(cap, nq):
    heads = nq // HEAD_SIZE
    return [arr((1, heads * cap), F32), arr((1, heads * cap), F32), arr((HEAD_SIZE, heads * cap), F32)]


def q_part(i, pair, staged, sums, stat, cos, sin, kvs, bias, nq, flops):
    mine, twin = pair
    half = stat.shape[0]
    return call(
        functools.partial(q_kernel, i, len(mine), len(kvs)),
        "q_part",
        (*mine, *twin, staged[0], staged[2], sums, stat, cos, sin, bias, *kvs),
        [arr((half, nq), BF16), *carry_shapes(half, nq)],
        flops=flops,
    )


def attend_kernel(step, first_key, n_carry, last, qa_ref, qb_ref, kv_ref, bias_ref, *refs):
    carries, outs = refs[: 3 * n_carry], refs[3 * n_carry :]
    half, nq = qa_ref.shape
    cap = 2 * half
    keys = slice(first_key, first_key + kv_ref.shape[0])
    for h in range(nq // HEAD_SIZE):
        lanes = slice(h * HEAD_SIZE, (h + 1) * HEAD_SIZE)
        at = slice(h * cap, (h + 1) * cap)
        part = slice(h * cap // n_carry, (h + 1) * cap // n_carry)
        carry = [
            jnp.concatenate([carries[j][:, part] for j in range(k, 3 * n_carry, 3)], axis=1) for k in range(3)
        ]
        q = jnp.concatenate([qa_ref[:, lanes], qb_ref[:, lanes]], axis=0)
        top, total, mix = attend(q, kv_ref[...], bias_ref[step, keys, :], carry)
        if not last:
            outs[0][:, at], outs[1][:, at], outs[2][:, at] = top, total, mix
            continue
        full, first, second = outs
        attn = jnp.transpose(mix * (1.0 / total)).astype(BF16)
        full[:, lanes] = attn
        first[:, lanes] = attn[:half]
        second[:, lanes] = attn[half:]


def attend_more(step, first_key, last, qs, kv, bias, carry, flops):
    half, nq = qs[0].shape
    cap = 2 * half
    shapes = [arr((cap, nq), BF16), arr((half, nq), BF16), arr((half, nq), BF16)]
    return call(
        functools.partial(attend_kernel, step, first_key, len(carry) // 3, last),
        "attend_more",
        (*qs, kv, bias, *carry),
        shapes if last else carry_shapes(cap, nq),
        flops=flops,
    )


def out_term(mine, twin, zz, core, w_ref):
    out = None
    for x, rows in halves(mine, twin, zz, core):
        out = add(out, jnp.dot(x, w_ref[rows, :], preferred_element_type=F32))
    return out


def out_own_kernel(n_mine, n_twin, *refs):
    mine, twin, refs = refs[:n_mine], refs[n_mine : n_mine + n_twin], refs[n_mine + n_twin :]
    n_ride = (len(refs) - 6) // 2
    w, hidden = refs[n_ride : n_ride + 2]
    total_ref, w_ref, hid_ref, sems = refs[-4:]
    z, core = place()
    copies = fetch([(w, w_ref), (hidden, hid_ref)], sems)
    copies[0].wait()
    total_ref[...] = out_term(joined(mine), joined(twin), z, core, w_ref)
    copies[1].wait()


def out_own(mine, twin, rides, w_out, hidden):
    cap = sum(x.shape[0] for x in mine)
    at = len(mine) + len(twin)
    return call(
        functools.partial(out_own_kernel, len(mine), len(twin)),
        "out_own",
        (*mine, *twin, *rides, w_out, hidden),
        [
            *(arr(r.shape, r.dtype) for r in rides),
            arr((cap, w_out.shape[1]), F32),
            arr(w_out.shape, BF16),
            arr(hidden.shape, BF16),
        ],
        scratch=[pltpu.SemaphoreType.DMA((2,))],
        rides={at + i: i for i in range(len(rides))},
        hbm=(w_out, hidden),
        flops=PART_COST,
    )


def out_more_kernel(n_mine, n_twin, flip, *refs):
    mine, twin, refs = refs[:n_mine], refs[n_mine : n_mine + n_twin], refs[n_mine + n_twin :]
    w_ref, total_in = refs[:2]
    total_out = refs[2 + (len(refs) - 3) // 2]
    z, core = place()
    total_out[...] = total_in[...] + out_term(joined(mine), joined(twin), flip(z), core, w_ref)


def out_more(mine, twin, w, total, rides, flip, flops):
    at = len(mine) + len(twin) + 1
    return call(
        functools.partial(out_more_kernel, len(mine), len(twin), flip),
        "out_more",
        (*mine, *twin, w, total, *rides),
        [arr(total.shape, F32), *(arr(r.shape, r.dtype) for r in rides)],
        rides={at + i: i for i in range(1 + len(rides))},
        flops=flops,
    )


def out_beside_kernel(a, b, c, d, last_a, last_b, last_twin, w_ref, total_in, total_out):
    z, core = place()
    half = last_a.shape[0]
    last, twin = (rows for _, rows in halves(last_a, last_b, z ^ 2, core))
    total = total_in[...] + out_term(joined((a, b)), joined((c, d)), z ^ 1, core, w_ref)
    total = total + jnp.dot(joined((last_a, last_b)), w_ref[last, :], preferred_element_type=F32)
    total_out[:half] = total[:half] + jnp.dot(last_twin[...], w_ref[twin, :], preferred_element_type=F32)
    total_out[half:] = total[half:]


def out_beside(mine, twin, last, last_twin, w, total, flops):
    return call(
        out_beside_kernel,
        "out_beside",
        (*mine, *twin, *last, last_twin, w, total),
        [arr(total.shape, F32)],
        rides={8: 0},
        flops=flops,
    )[0]


def out_last_kernel(twin_ref, w_ref, total_ref, sa_ref, sb_ref, hot_ref, hid_ref, out, out_ref, sems):
    z, core = place()
    half, width = twin_ref.shape
    rows = pl.ds(pl.multiple_of((2 * (z ^ 2) + 1 - core) * width, width), width)
    top = sa_ref[:, 128:129] * total_ref[:half]
    rest = total_ref[half:] + jnp.dot(twin_ref[...], w_ref[rows, :], preferred_element_type=F32)
    update = jnp.concatenate([top.astype(BF16), (sb_ref[:, 128:129] * rest).astype(BF16)], axis=0)
    block = 256
    copies = []
    for i in range(hid_ref.shape[0] // block):
        rows = slice(i * block, (i + 1) * block)
        placed = jnp.dot(hot_ref[rows, :], update, preferred_element_type=F32)
        out_ref[rows, :] = (hid_ref[rows, :].astype(F32) + placed).astype(BF16)
        copies += fetch([(out_ref.at[rows, :], out.at[rows, :])], sems, i)
    settle(copies)


def out_last(twin, w, total, stats, hot, hidden):
    return call(
        out_last_kernel,
        "out_last",
        (twin, w, total, *stats, hot, hidden),
        [arr(hidden.shape, BF16)],
        scratch=[pltpu.VMEM(hidden.shape, BF16), pltpu.SemaphoreType.DMA((hidden.shape[0] // 256,))],
        out_hbm=True,
    )[0]


def angles(row_pos):
    half = HEAD_SIZE // 2
    frequency = ROPE_BASE ** (-(jnp.arange(half, dtype=F32) * 2.0 / HEAD_SIZE))
    turned = row_pos.astype(F32) * jnp.concatenate([frequency, frequency])[None, :]
    sign = jnp.concatenate([-jnp.ones((half,), F32), jnp.ones((half,), F32)])
    return jnp.cos(turned), jnp.sin(turned) * sign[None, :]


def body(
    size,
    hidden_in,
    norm_gain,
    router_weight,
    w_query,
    w_key,
    value_weight,
    w_out,
    keep_flags,
    keep_counts,
    keep_positions,
):
    shards = lax.axis_size("ctx")
    tok = hidden_in.shape[0]
    nq = w_query.shape[1]
    flags = keep_flags.reshape(-1, 128)
    weights = (norm_gain.reshape(1, -1), router_weight.reshape(1, -1), w_query, w_key, value_weight)

    full, first, second, rowpos = pick(keep_positions, hidden_in)
    held = {}

    def own(mine, mate):
        ride, held["sums"], *held["staged"], held["bias"], held["hot"] = own_part(
            *mine, *mate, weights, keep_counts, keep_positions, flags, tok
        )
        return ride

    def far(mine, twin, last):
        held["sums"], held["cos"], held["sin"], *pieces = more_part(
            mine, twin, held["staged"], held["sums"], angles(rowpos), lambda z: 3 - z, FAR_COST, (last,)
        )
        return tuple(pieces)

    def beside(mine, twin):
        (held["sums"],) = more_part(mine, twin, held["staged"], held["sums"], (), lambda z: z ^ 1, BESIDE_COST)

    pair, last_b, twin = spread_halves(size, full, first, second, own, far, beside)
    sums, staged, bias = held["sums"], held["staged"], held["bias"]
    cos, sin = held["cos"], held["sin"]
    half = first.shape[0]
    ring = [(s, (s + 1) % shards) for s in range(shards)]
    kvs, stats, pairs, qs, carry = [], [], [], [], []
    for i in range(2):
        if i == 1:
            kvs[0], last_b = gate(kvs[0], last_b)
            pair = (last_b,), (twin(last_b),)
        kv, stat = kv_last(i * half, pair, staged, sums, cos, sin, nq, KV_COST)
        kvs.append(kv)
        stats.append(stat)
        pairs.append(pair)
    moved = [lax.ppermute(kv, "ctx", ring) for kv in kvs]
    for i in range(2):
        q, *terms = q_part(
            i, pairs[i], staged, sums, stats[i], cos, sin, kvs[: i + 1], bias, nq, Q_COST if i else QA_COST
        )
        qs.append(q)
        carry += terms
    for step in range(1, shards):
        for i in range(2):
            last = step == shards - 1 and i == 1
            carry = attend_more(step, i * half, last, qs, moved[i], bias, carry, ATTEND_COST)
        if step < shards - 1:
            moved = [lax.ppermute(kv, "ctx", ring) for kv in moved]

    def own_out(mine, twin, rides):
        *rides, held["total"], held["w"], held["hidden"] = out_own(mine, twin, rides, w_out, hidden_in)
        return rides

    def far_out(mine, twin, rides):
        held["total"], *rides = out_more(mine, twin, held["w"], held["total"], rides, lambda z: 3 - z, PART_COST)
        return rides

    def beside_out(mine, twin, last, last_twin):
        held["total"] = out_beside(mine, twin, last, last_twin, held["w"], held["total"], PART_COST)

    twin = spread(size, *carry, own_out, far_out, beside_out)
    return out_last(twin, held["w"], held["total"], stats, held["hot"], held["hidden"])


def solution(mesh):
    in_specs = (
        P(("groups", "ctx"), "heads"),
        P(),
        P(),
        P(None, "heads"),
        P(None, "heads"),
        P(None, "heads"),
        P(None, "heads"),
        P(("groups", "ctx")),
        P("groups"),
        P("groups", None),
    )
    out_specs = P(("groups", "ctx"), "heads")
    return jax.shard_map(
        functools.partial(body, mesh.shape["heads"]),
        mesh=mesh,
        in_specs=in_specs,
        out_specs=out_specs,
        check_vma=False,
    )
```
